128 devices in a mesh: rep: 4 (over y_hi, core), exp: 32 (over x, y_lo, z).
Axes of the slice: x: 4, y: 4 (y_hi: 2, y_lo: 2; y = y_hi * 2 + y_lo), z: 4, core: 2. Of those that a mesh axis runs over, the one named last changes fastest.
Arguments:
- patches: bfloat16 [2, 32, 576, 768], P(None, 'exp', 'rep'), may hold values from -6 to 6
- expert_ids: int32 [2, 32, 576, 2], P(None, 'exp', 'rep'), may hold values from 0 to 31, all different within a row; in each aligned block of 144 rows (0 to 143, 144 to 287, ..., all dimensions but the last counted through in order) at most 10 rows name the same one
- labels: int32 [2, 32, 64], replicated, may hold values from -1 to 21887, as said below
- label_count: int32 [2, 32], replicated, may hold values from 0 to 64, as said below
- square_weights: float32 [5, 768, 768], P(None, ('rep', 'exp')), may hold values from -0.72168784 to 0.72168784
- router_weight: float32 [768, 32], P(('rep', 'exp')), may hold values from -0.15625 to 0.15625
- position_table: float32 [576, 768], P(None, ('rep', 'exp')), may hold values from -3 to 3
- head_weight: float32 [768, 21888], P(None, ('rep', 'exp')), may hold values from -0.7577722 to 0.7577722
- expert_weights: float32 [32, 2, 768, 3072], P('exp', None, None, 'rep'), may hold values from -1.4433757 to 1.4433757
- vector_params: float32 [10, 768], P(None, ('rep', 'exp')), may hold values from -1.6 to 1.6
- square_rows: float32 [5, 768], P(None, ('rep', 'exp')), may hold values from 1.4128508e-09 to 5.6514033e-09
- square_cols: float32 [5, 768], replicated, may hold values from 1.4128508e-09 to 5.6514033e-09
- router_rows: float32 [768], P(('rep', 'exp')), may hold values from 1.0624638e-07 to 4.2950666e-07
- router_cols: float32 [32], replicated, may hold values from 1.0624638e-07 to 4.2950666e-07
- position_rows: float32 [576], replicated, may hold values from 2.452866e-12 to 9.811464e-12
- position_cols: float32 [768], P(('rep', 'exp')), may hold values from 2.452866e-12 to 9.811464e-12
- head_rows: float32 [768], replicated, may hold values from 9.2801994e-10 to 3.7180286e-09
- head_cols: float32 [21888], P(('rep', 'exp')), may hold values from 9.2801994e-10 to 3.7180286e-09
- expert_rows: float32 [32, 2, 768], P('exp'), may hold values from 3.1044086e-14 to 5.5189486e-12
- expert_cols: float32 [32, 2, 3072], P('exp', None, 'rep'), may hold values from 3.1044086e-14 to 5.5189486e-12
- vector_moment: float32 [10, 768], P(None, ('rep', 'exp')), may hold values from 1.4128508e-09 to 5.6514033e-09
Outputs:
- loss_sum: float32 [], replicated
- image_count: float32 [], replicated
- grad_norm: float32 [], replicated
- square_clipped: float32 [5, 768, 768], P(None, ('rep', 'exp'))
- square_rows_next: float32 [5, 768], P(None, ('rep', 'exp'))
- square_cols_next: float32 [5, 768], replicated
- square_weights_next: float32 [5, 768, 768], P(None, ('rep', 'exp'))
- router_clipped: float32 [768, 32], P(('rep', 'exp'))
- router_rows_next: float32 [768], P(('rep', 'exp'))
- router_cols_next: float32 [32], replicated
- router_weight_next: float32 [768, 32], P(('rep', 'exp'))
- position_clipped: float32 [576, 768], P(None, ('rep', 'exp'))
- position_rows_next: float32 [576], replicated
- position_cols_next: float32 [768], P(('rep', 'exp'))
- position_table_next: float32 [576, 768], P(None, ('rep', 'exp'))
- head_clipped: float32 [768, 21888], P(None, ('rep', 'exp'))
- head_rows_next: float32 [768], replicated
- head_cols_next: float32 [21888], P(('rep', 'exp'))
- head_weight_next: float32 [768, 21888], P(None, ('rep', 'exp'))
- expert_clipped: float32 [32, 2, 768, 3072], P('exp', None, None, 'rep')
- expert_rows_next: float32 [32, 2, 768], P('exp')
- expert_cols_next: float32 [32, 2, 3072], P('exp', None, 'rep')
- expert_weights_next: float32 [32, 2, 768, 3072], P('exp', None, None, 'rep')
- vector_clipped: float32 [10, 768], P(None, ('rep', 'exp'))
- vector_moment_next: float32 [10, 768], P(None, ('rep', 'exp'))
- vector_params_next: float32 [10, 768], P(None, ('rep', 'exp'))
The draws below stay inside these ranges and needn't reach their ends.
Inputs may be any that keep to these rules, and one draw needn't show every extreme that they name: `expert_ids`: each row names 2 different experts; within each device's aligned block of 144 rows no expert is named more than 10 times, a bound that some block reaches. `labels`: the first label_count entries of an image are distinct classes; the rest are -1. `label_count`: an image with 0 labels is padding: it adds nothing to the loss or to image_count.
All inputs are finite; a program needn't handle non-finite values.
Results may differ from the reference program's by a relative error of at most 0.003.
The reference program's roundings to bfloat16 on the way count: a program that leaves them out, or rounds other values in their place, can miss the bound.
Values may be sent and summed in bfloat16 or wider, within the bound.
A program may use at most 192 MiB of HBM per device.

```python
import math
import jax
import jax.numpy as jnp
import numpy as np
from jax import lax

D = 768
HEADS = 12
HEAD = 64
FF = 3072
VOCAB = 21888
PATCHES = 576
TOP = 2
LABELS = 64
MICRO = 2
EXPERTS = 32
IMAGES = 32
ROWS = 144
CAP = 10
N_REP = 4


def draw_patches(key, part):
    key = jax.random.fold_in(key, 11)
    first, second = jax.random.split(key)
    shared = jnp.clip(jax.random.normal(first, (MICRO, IMAGES, 1, D), jnp.float32), -4.0, 4.0)
    noise = jnp.clip(jax.random.normal(second, (MICRO, IMAGES, PATCHES, D), jnp.float32), -4.0, 4.0)
    return jnp.clip(0.6 * shared + 0.8 * noise, -6.0, 6.0).astype(jnp.bfloat16)


def draw_square_weights(key, part):
    key = jax.random.fold_in(key, 13)
    base = jnp.clip(jax.random.normal(key, (5, D, D), jnp.float32), -5.0, 5.0)
    factor = jnp.array([1.0, 1.0, 1.0, 1.0, 4.0], jnp.float32)[:, None, None]
    return base * factor / math.sqrt(D)


def draw_head_weight(key, part):
    key = jax.random.fold_in(key, 17)
    ramp = jnp.arange(VOCAB).astype(jnp.float32)[None, :] / (VOCAB - 1)
    base = jnp.clip(jax.random.normal(key, (D, VOCAB), jnp.float32), -5.0, 5.0) * (1.0 + 2.0 * ramp)
    return base * 1.4 / math.sqrt(D)


def draw_expert_weights(key, part):
    key = jax.random.fold_in(key, 19)
    base = jnp.clip(jax.random.normal(key, (EXPERTS, 2, D, FF), jnp.float32), -5.0, 5.0)
    factor = jnp.array([1.0 / math.sqrt(D), 16.0 / math.sqrt(FF)], jnp.float32)[None, :, None, None]
    return base * factor


def draw_vector_params(key, part):
    key = jax.random.fold_in(key, 23)
    base = jnp.clip(jax.random.normal(key, (10, D), jnp.float32), -5.0, 5.0)
    gains = jnp.array([0.0, 1.0, 0.0, 0.0, 0.0, 0.0, 1.0, 0.0, 1.0, 0.0], jnp.float32)[:, None]
    return gains * (1.0 + 0.12 * base) + (1.0 - gains) * 0.3 * base


def factor_state(key, shape):
    level = jax.random.uniform(key, shape, jnp.float32, math.log(0.25), 0.0)
    factor = jnp.array([32.0, 0.72], jnp.float32)[None, :, None] / float(EXPERTS) ** 3
    return jnp.exp(level) * factor * 0.0025 / (D * PATCHES)


def draw_expert_rows(key, part):
    key = jax.random.fold_in(key, 29)
    return factor_state(key, (EXPERTS, 2, D))


def draw_expert_cols(key, part):
    key = jax.random.fold_in(key, 31)
    return factor_state(key, (EXPERTS, 2, FF))


def label_plan(key):
    counts = jax.random.randint(jax.random.fold_in(key, 1), (MICRO * IMAGES,), 1, LABELS + 1)
    spot = jax.random.randint(jax.random.fold_in(key, 2), (), 1, MICRO * IMAGES)
    counts = counts.at[0].set(LABELS).at[spot].set(0)
    return counts.reshape(MICRO, IMAGES).astype(jnp.int32)


def draw_label_count(key, part):
    return label_plan(key)


def draw_labels(key, part):
    counts = label_plan(key)
    key = jax.random.fold_in(key, 37)
    keys = jax.random.split(key, MICRO * IMAGES)
    picks = jax.vmap(lambda single: jax.random.permutation(single, VOCAB - 1)[:LABELS])(keys)
    picks = picks.reshape(MICRO, IMAGES, LABELS).astype(jnp.int32)
    picks = picks.at[0, 0, 0].set(VOCAB - 1)
    live = jnp.arange(LABELS)[None, None, :] < counts[:, :, None]
    return jnp.where(live, picks, -1).astype(jnp.int32)


def shard_levels(own_key, dims, cuts, low, high):
    loudness = 1.0
    for dim, parts in cuts:
        heights = jax.random.uniform(jax.random.fold_in(jax.random.fold_in(own_key, 6), dim), (parts,), jnp.float32, low / len(cuts), high / len(cuts))
        loudness = loudness * jnp.repeat(jnp.exp(heights), dims[dim] // parts).reshape((-1,) + (1,) * (len(dims) - 1 - dim))
    return loudness


def routed_block(stream_key, own, number, rows, count, top, limit, skew):
    order = jax.random.permutation(stream_key, count)
    heavy_load, usual = portions_of(count, rows * top, limit, skew, True), portions_of(count, rows * top, limit, skew, False)
    places = jnp.arange(count)

    def named(tallies, turn):
        used = int((tallies > 0).sum())
        fixed = max(1, used // 4)
        moved = fixed + (places - fixed + turn * (used - fixed)) % max(1, count - fixed)
        return jnp.zeros((count,), jnp.int32).at[order[jnp.where(places < fixed, places, moved)]].set(jnp.asarray(tallies, jnp.int32))

    tallies = jnp.where(number % 4 == 0, named(heavy_load, number // 4), named(usual, number - number // 4 - 1))
    mixed = jax.random.permutation(jax.random.fold_in(own, 3), count)
    source_of, sink = mixed[0:count // 2 * 2:2], mixed[1:count // 2 * 2:2]
    room = jnp.minimum(tallies[source_of] - 1, limit - tallies[sink]) // 2
    room = jnp.where((source_of == order[0]) | (sink == order[0]) | (tallies[sink] == 0), 0, jnp.maximum(room, 0))
    moved = jax.random.randint(jax.random.fold_in(own, 4), (count // 2,), 0, 1 << 20) % (room + 1)
    tallies = tallies.at[source_of].add(-moved).at[sink].add(moved)
    members = jnp.searchsorted(jnp.cumsum(tallies), jnp.arange(rows * top), side="right").astype(jnp.int32)
    listing = members.reshape(top, rows).T
    listing = listing[jax.random.permutation(jax.random.fold_in(own, 1), rows)]
    turn = jax.random.randint(jax.random.fold_in(own, 2), (rows, 1), 0, top)
    return jnp.take_along_axis(listing, (jnp.arange(top)[None, :] + turn) % top, axis=1)


def portions_of(number_of, total, most, slope, full):
    weights = [(1 << 20) // math.isqrt(rank ** slope) + 1 for rank in range(1, number_of + 1)]
    largest = most if full else min(most, max(-(-total // number_of), total * weights[0] // sum(weights)))
    least = 1 if total - largest >= number_of - 1 else 0
    given, rest = [largest] + [least] * (number_of - 1), total - largest - least * (number_of - 1)
    while rest > 0:
        candidates = [i for i in range(1, number_of) if given[i] < largest] or [i for i in range(1, number_of) if given[i] < most]
        whole, budget = sum([weights[i] for i in candidates]), rest
        for i in candidates:
            more = min(most - given[i], max(1, budget * weights[i] // whole), rest)
            given[i] = given[i] + more
            rest = rest - more
    return np.array(given)


def normal_values(stream_key, dims, width, bound, cuts=(), kind=jnp.bfloat16):
    level = shard_levels(stream_key, dims, cuts, -0.22, 0.18) if cuts else 1.0
    entries = jax.random.normal(stream_key, dims, jnp.float32) * width * level
    return jnp.minimum(jnp.maximum(entries, -bound), bound).astype(kind)


def setup_inputs(seed: int = 0) -> dict:
    key_of = jax.random.split(jax.random.key(seed), 22)
    patches = draw_patches(jax.random.fold_in(key_of[21], 71), 0)
    expert_ids_keys = jax.random.split(jax.random.fold_in(key_of[1], 1), MICRO * IMAGES * PATCHES // ROWS)
    expert_ids_turns = jax.random.permutation(jax.random.fold_in(key_of[1], 3), MICRO * IMAGES * PATCHES // ROWS)
    expert_ids = jax.vmap(lambda own, number: routed_block(jax.random.fold_in(key_of[1], 2), own, number, ROWS, EXPERTS, TOP, CAP, 1))(expert_ids_keys, expert_ids_turns).reshape((MICRO, IMAGES, PATCHES, TOP))
    labels = draw_labels(jax.random.fold_in(key_of[21], 71), 0)
    label_count = draw_label_count(jax.random.fold_in(key_of[21], 71), 0)
    square_weights = draw_square_weights(jax.random.fold_in(key_of[21], 71), 0)
    router_weight = normal_values(key_of[5], (D, EXPERTS), (2 * D) ** -0.5, 0.15625, ((0, 128),), jnp.float32)
    position_table = normal_values(key_of[6], (PATCHES, D), 0.5, 3.0, ((1, 128),), jnp.float32)
    head_weight = draw_head_weight(jax.random.fold_in(key_of[21], 71), 0)
    expert_weights = draw_expert_weights(jax.random.fold_in(key_of[21], 71), 0)
    vector_params = draw_vector_params(jax.random.fold_in(key_of[21], 71), 0)
    square_rows = jnp.clip(jnp.exp(math.log(5.6514033452970125e-09) - 1.3862944 * jax.random.uniform(key_of[10], (5, D), jnp.float32) ** shard_levels(key_of[10], (5, D), ((1, 128),), -0.2, 0.2)), 1.4128508363242531e-09, 5.6514033452970125e-09)
    square_cols = jnp.clip(jnp.exp(jax.random.uniform(key_of[11], (5, D), jnp.float32, math.log(1.4128508363242531e-09), math.log(5.6514033452970125e-09))), 1.4128508363242531e-09, 5.6514033452970125e-09)
    router_rows = jnp.clip(jnp.exp(math.log(4.295066560189298e-07) - 1.3968765 * jax.random.uniform(key_of[12], (D,), jnp.float32) ** shard_levels(key_of[12], (D,), ((0, 128),), -0.2, 0.2)), 1.0624638235867678e-07, 4.295066560189298e-07)
    router_cols = jnp.clip(jnp.exp(jax.random.uniform(key_of[13], (EXPERTS,), jnp.float32, math.log(1.0624638235867678e-07), math.log(4.295066560189298e-07))), 1.0624638235867678e-07, 4.295066560189298e-07)
    position_rows = jnp.clip(jnp.exp(jax.random.uniform(key_of[14], (PATCHES,), jnp.float32, math.log(2.4528660352851617e-12), math.log(9.811464141140647e-12))), 2.4528660352851617e-12, 9.811464141140647e-12)
    position_cols = jnp.clip(jnp.exp(math.log(9.811464141140647e-12) - 1.3862944 * jax.random.uniform(key_of[15], (D,), jnp.float32) ** shard_levels(key_of[15], (D,), ((0, 128),), -0.2, 0.2)), 2.4528660352851617e-12, 9.811464141140647e-12)
    head_rows = jnp.clip(jnp.exp(jax.random.uniform(key_of[16], (D,), jnp.float32, math.log(9.280199386729748e-10), math.log(3.718028551702446e-09))), 9.280199386729748e-10, 3.718028551702446e-09)
    head_cols = jnp.clip(jnp.exp(math.log(3.718028551702446e-09) - 1.3878956 * jax.random.uniform(key_of[17], (VOCAB,), jnp.float32) ** shard_levels(key_of[17], (VOCAB,), ((0, 128),), -0.2, 0.2)), 9.280199386729748e-10, 3.718028551702446e-09)
    expert_rows = draw_expert_rows(jax.random.fold_in(key_of[21], 71), 0)
    expert_cols = draw_expert_cols(jax.random.fold_in(key_of[21], 71), 0)
    vector_moment = jnp.clip(jnp.exp(math.log(5.6514033452970125e-09) - 1.3862944 * jax.random.uniform(key_of[20], (10, D), jnp.float32) ** shard_levels(key_of[20], (10, D), ((1, 128),), -0.2, 0.2)), 1.4128508363242531e-09, 5.6514033452970125e-09)
    return {"patches": patches, "expert_ids": expert_ids, "labels": labels, "label_count": label_count, "square_weights": square_weights, "router_weight": router_weight, "position_table": position_table, "head_weight": head_weight, "expert_weights": expert_weights, "vector_params": vector_params, "square_rows": square_rows, "square_cols": square_cols, "router_rows": router_rows, "router_cols": router_cols, "position_rows": position_rows, "position_cols": position_cols, "head_rows": head_rows, "head_cols": head_cols, "expert_rows": expert_rows, "expert_cols": expert_cols, "vector_moment": vector_moment}


@jax.custom_vjp
def low(v):
    return lax.optimization_barrier(v.astype(jnp.bfloat16)).astype(jnp.float32)

@jax.custom_vjp
def low_back(v):
    return v

def low_keep(v):
    return (low(v), None)

def low_pass(kept, grad):
    return (grad,)

def back_keep(v):
    return (v, None)

def back_low(kept, grad):
    return (low(grad),)
low.defvjp(low_keep, low_pass)
low_back.defvjp(back_keep, back_low)
HIGHEST = lax.Precision.HIGHEST
DECAY = 0.8
EPS_SQ = 1e-30
CLIP_NORM = 0.25

def layer_norm(value, gain, shift):
    centred = value - lax.optimization_barrier(jnp.mean(value, axis=-1, keepdims=True))
    spread = lax.optimization_barrier(jnp.mean(centred * centred, axis=-1, keepdims=True))
    return centred * lax.rsqrt(spread + 1e-06) * gain + shift

def product(left, right):
    return jnp.matmul(left, right, precision=HIGHEST)

def attend_image(triple):
    query, key_rows, value_rows = triple
    shape = (PATCHES, HEADS, HEAD)
    scores = jnp.einsum('qhd,khd->hqk', query.reshape(shape), key_rows.reshape(shape), precision=HIGHEST)
    scores = low_back(scores * HEAD ** (-0.5))
    probs = jax.nn.softmax(scores, axis=-1)
    mixed = jnp.einsum('hqk,khd->qhd', low(probs), value_rows.reshape(shape), precision=HIGHEST)
    return mixed.reshape(PATCHES, D)

def slot_places(ids):
    blocks = ids.reshape(IMAGES * N_REP, ROWS * TOP)
    onehot = (blocks[:, :, None] == jnp.arange(EXPERTS).astype(jnp.int32)[None, None, :]).astype(jnp.int32)
    before = jnp.cumsum(onehot, axis=1) - onehot
    slot = lax.optimization_barrier(jnp.sum(before * onehot, axis=-1))
    source = jnp.arange(IMAGES * N_REP).astype(jnp.int32)[:, None]
    return (source * CAP + slot).astype(jnp.int32).reshape(IMAGES, PATCHES, TOP)

def micro_loss(weights, patch_rows, ids, targets, valid_rows, count):
    squares, router, table, head, experts, vectors = weights
    embed = low_back(product(patch_rows, low(squares[0]))) + vectors[0] + table
    hidden_one = low(layer_norm(embed, vectors[1], vectors[2]))
    query = low_back(low(product(hidden_one, low(squares[1])) + vectors[3]))
    keyed = low_back(low(product(hidden_one, low(squares[2]))))
    valued = low_back(low(product(hidden_one, low(squares[3])) + vectors[4]))
    mixed = lax.map(jax.checkpoint(attend_image), (query, keyed, valued))
    mixed = low_back(low(mixed))
    after_attn = embed + low_back(product(mixed, low(squares[4]))) + vectors[5]
    hidden_two = low(layer_norm(after_attn, vectors[6], vectors[7]))
    gate_logits = low_back(product(hidden_two, low(router)))
    gate_probs = jax.nn.softmax(gate_logits, axis=-1)
    gates = jnp.take_along_axis(gate_probs, ids, axis=-1)
    places = slot_places(ids)
    copies = jnp.stack([low_back(hidden_two) for index in range(TOP)], axis=2)
    flat_ids = ids.reshape(-1)
    flat_places = places.reshape(-1)
    buffer = jnp.zeros((EXPERTS, IMAGES * N_REP * CAP, D), jnp.float32)
    buffer = buffer.at[flat_ids, flat_places].set(copies.reshape(-1, D))
    pre_act = low_back(jnp.einsum('esd,edf->esf', buffer, low(experts[:, 0]), precision=HIGHEST))
    act = low(jax.nn.gelu(pre_act))
    expert_out = jnp.einsum('esf,edf->esd', act, low(experts[:, 1]), precision=HIGHEST)
    expert_out = low_back(low(expert_out))
    returned = expert_out[flat_ids, flat_places].reshape(IMAGES, PATCHES, TOP, D)
    after_moe = after_attn + lax.optimization_barrier(jnp.sum(gates[..., None] * returned, axis=2))
    final = layer_norm(after_moe, vectors[8], vectors[9])
    pooled = low(lax.optimization_barrier(jnp.mean(final, axis=1)))
    logits = low_back(product(pooled, low(head)))
    terms = valid_rows[:, None] * (jax.nn.softplus(logits) - targets * logits)
    total = jnp.sum(terms)
    return (total / count, total)

def factored(weight, clipped, rows_old, cols_old, rate):
    squared = clipped * clipped + EPS_SQ
    rows_next = DECAY * rows_old + (1.0 - DECAY) * lax.optimization_barrier(jnp.mean(squared, axis=-1))
    cols_next = DECAY * cols_old + (1.0 - DECAY) * lax.optimization_barrier(jnp.mean(squared, axis=-2))
    estimate = rows_next[..., :, None] * cols_next[..., None, :] / lax.optimization_barrier(jnp.mean(rows_next, axis=-1))[..., None, None]
    return (rows_next, cols_next, weight - rate * clipped * lax.rsqrt(estimate))

def reference(patches, expert_ids, labels, label_count, square_weights, router_weight, position_table, head_weight, expert_weights, vector_params, square_rows, square_cols, router_rows, router_cols, position_rows, position_cols, head_rows, head_cols, expert_rows, expert_cols, vector_moment):
    weights = (square_weights, router_weight, position_table, head_weight, expert_weights, vector_params)
    valid = (label_count > 0).astype(jnp.float32)
    image_count = jnp.sum(valid)
    summed = jax.tree.map(jnp.zeros_like, weights)
    loss_sum = jnp.zeros((), jnp.float32)
    classes = jnp.arange(VOCAB).astype(jnp.int32)
    slots = jnp.arange(LABELS).astype(jnp.int32)
    for micro in range(MICRO):
        live = slots[None, :] < label_count[micro][:, None]
        targets = jnp.any((labels[micro][:, :, None] == classes[None, None, :]) & live[:, :, None], axis=1).astype(jnp.float32)

        def scaled(params, patch_rows=patches[micro].astype(jnp.float32), ids=expert_ids[micro], targets=targets, valid_rows=valid[micro]):
            return micro_loss(params, patch_rows, ids, targets, valid_rows, image_count)
        value, pull, total = jax.vjp(scaled, weights, has_aux=True)
        grads = pull(jnp.ones((), jnp.float32))[0]
        summed = jax.tree.map(jnp.add, summed, grads)
        loss_sum = loss_sum + total
    grad_norm = jnp.sqrt(sum((jnp.sum(piece * piece) for piece in summed)))
    scale = jnp.minimum(1.0, CLIP_NORM / grad_norm)
    square_g, router_g, table_g, head_g, expert_g, vector_g = [scale * piece for piece in summed]
    square_rate = jnp.array([1.0, 1.0, 1.0, 1.0, 4.0], jnp.float32)[:, None, None] * (0.3 / math.sqrt(D))
    expert_rate = jnp.array([0.3 / math.sqrt(D), 4.8 / math.sqrt(FF)], jnp.float32)[None, :, None, None]
    square_out = factored(square_weights, square_g, square_rows, square_cols, square_rate)
    router_out = factored(router_weight, router_g, router_rows, router_cols, 0.2 / math.sqrt(D))
    table_out = factored(position_table, table_g, position_rows, position_cols, 0.15)
    head_out = factored(head_weight, head_g, head_rows, head_cols, 0.5 / math.sqrt(D))
    expert_out = factored(expert_weights, expert_g, expert_rows, expert_cols, expert_rate)
    moment_next = DECAY * vector_moment + (1.0 - DECAY) * (vector_g * vector_g + EPS_SQ)
    vector_next = vector_params - 0.3 * vector_g * lax.rsqrt(moment_next)
    return (loss_sum, image_count, grad_norm, square_g, square_out[0], square_out[1], square_out[2], router_g, router_out[0], router_out[1], router_out[2], table_g, table_out[0], table_out[1], table_out[2], head_g, head_out[0], head_out[1], head_out[2], expert_g, expert_out[0], expert_out[1], expert_out[2], vector_g, moment_next, vector_next)
```

```python
import functools
import math

import jax
import jax.numpy as jnp
from jax import lax
from jax.experimental import pallas as pl
from jax.experimental.pallas import tpu as pltpu
from jax.sharding import PartitionSpec as P

D = 768
HEAD = 64
FF = 3072
PATCHES = 576
CAP = 10
PAD = 8
LANES = 128


DECAY = 0.8
EPS_SQ = 1e-30
CLIP_NORM = 0.25
HIGHEST = lax.Precision.HIGHEST
MESH = pl.DeviceIdType.MESH

Y_SWAP = ((0, 2), (1, 3), (2, 0), (3, 1))
CORE_SWAP = ((0, 1), (1, 0), (2, 3), (3, 2))


def layer_norm(value, gain, shift):
    centred = value - jnp.mean(value, axis=-1, keepdims=True)
    spread = jnp.mean(centred * centred, axis=-1, keepdims=True)
    return centred * lax.rsqrt(spread + 1e-06) * gain + shift


def plain_dot(left, right):
    return jnp.dot(left, right, preferred_element_type=jnp.float32)


def over_rows(left, right):
    return lax.dot_general(
        left, right, (((0,), (0,)), ((), ())), preferred_element_type=jnp.float32
    )


def over_last(left, right):
    return lax.dot_general(
        left, right, (((1,), (1,)), ((), ())), preferred_element_type=jnp.float32
    )


def factored_step(weight, clipped, rows_next, cols_next, rows_mean, rate):
    estimate = rows_next[..., :, None] * cols_next[..., None, :] / rows_mean
    return weight - rate * clipped * lax.rsqrt(estimate)


def place():
    rep = lax.axis_index("rep")
    line = lax.axis_index("exp")
    y = lax.div(rep, 2) * 2 + lax.rem(lax.div(line, 4), 2)
    return {"y": y, "core": lax.rem(rep, 2), "x": lax.div(line, 8), "z": lax.rem(line, 4)}


def device(at):
    return {
        "rep": lax.div(at["y"], 2) * 2 + at["core"],
        "exp": at["x"] * 8 + lax.rem(at["y"], 2) * 4 + at["z"],
    }


def moved(at, axis, by):
    return {**at, axis: lax.rem(at[axis] + by, 2 if axis == "core" else 4)}


def box(ref, at, free, core=False):
    whole = slice(None)
    hi = whole if "y" in free else lax.div(at["y"], 2)
    low = whole if "y" in free else lax.rem(at["y"], 2)
    x = whole if "x" in free else at["x"]
    z = whole if "z" in free else at["z"]
    if core:
        return ref.at[hi, at["core"], x, low, z]
    return ref.at[hi, x, low, z]


def greet(at):
    barrier = pltpu.get_barrier_semaphore()
    peers = [moved(at, axis, by) for axis in ("x", "y", "z") for by in (1, 2, 3)]
    peers.append(moved(at, "core", 1))
    for peer in peers:
        pl.semaphore_signal(barrier, inc=1, device_id=device(peer), device_id_type=MESH)
    pl.semaphore_wait(barrier, len(peers))


def remote(src, dst, sems, index, peer):
    return pltpu.make_async_remote_copy(
        src_ref=src,
        dst_ref=dst,
        send_sem=sems[0].at[index],
        recv_sem=sems[1].at[index],
        device_id=device(peer),
        device_id_type=MESH,
    )


ORDERS = (("x", "y", "z"), ("y", "z", "x"), ("z", "x", "y"))


def gather_kernel(x_ref, *refs):
    outs, (send, recv, local) = refs[:3], refs[3:]
    at = place()
    sems = (send, recv)
    own = []
    for part in range(3):
        own.append(
            pltpu.make_async_copy(
                x_ref.at[part], box(outs[part], at, (), True), local.at[part]
            )
        )
        own[part].start()
    greet(at)
    flights = {}

    def launch(part, stage):
        axes = ORDERS[part]
        view = box(outs[part], at, axes[:stage], True)
        source = x_ref.at[part] if stage == 0 else view
        for by in (1, 2, 3):
            copy = remote(source, view, sems, part * 13 + stage * 3 + by - 1, moved(at, axes[stage], by))
            copy.start()
            flights[part, stage, by] = copy

    def forward(part, by):
        axes = ORDERS[part]
        view = box(outs[part], moved(at, axes[2], 4 - by), axes[:2], True)
        copy = remote(view, view, sems, part * 13 + 9 + by, moved(at, "core", 1))
        copy.start()
        flights[part, 3, by] = copy

    for part in range(3):
        launch(part, 0)
    for stage in (1, 2):
        for part in range(3):
            if stage == 1:
                own[part].wait()
            for by in (1, 2, 3):
                flights[part, stage - 1, by].wait_recv()
            launch(part, stage)
            if stage == 2:
                forward(part, 0)
    for part in range(3):
        for by in (1, 2, 3):
            flights[part, 2, by].wait_recv()
            forward(part, by)
    for key, copy in flights.items():
        copy.wait_send()
        if key[1] == 3:
            copy.wait_recv()


def gather_all(payload):
    shape = (2, 2, 4, 2, 4, 16, D)
    return pl.pallas_call(
        gather_kernel,
        out_shape=[jax.ShapeDtypeStruct(shape, payload.dtype)] * 3,
        in_specs=[pl.BlockSpec(memory_space=pl.ANY)],
        out_specs=[pl.BlockSpec(memory_space=pl.ANY)] * 3,
        scratch_shapes=[
            pltpu.SemaphoreType.DMA((39,)),
            pltpu.SemaphoreType.DMA((39,)),
            pltpu.SemaphoreType.DMA((3,)),
        ],
        compiler_params=pltpu.CompilerParams(collective_id=0, has_side_effects=True),
        name="gather_weights",
    )(payload)


def scatter_kernel(*refs):
    grads, outs = refs[:6], refs[6:12]
    first, total_one, second, total_two, third = (refs[12 + 6 * i : 18 + 6 * i] for i in range(5))
    sems = refs[42:44]
    at = place()
    greet(at)
    stages = []

    def launch(which, stage):
        axes = ORDERS[which // 2]
        axis = axes[2 - stage]
        source = (grads, total_one, total_two)[stage][which]
        landing = (first, second, third)[stage][which]
        copies = []
        for by in (1, 2, 3):
            view = part_of(source, moved(at, axis, by), axes, stage)
            copy = remote(view, landing.at[by - 1], sems, which * 9 + stage * 3 + by - 1, moved(at, axis, by))
            copy.start()
            copies.append(copy)
        return copies

    def part_of(source, where, axes, stage):
        if stage == 0:
            return box(source, where, axes[:2])
        if stage == 1:
            left = [axis for axis in ("h", "x", "l", "z") if axis not in names(axes[2])]
            return source.at[tuple(pick(axis, where, axes[1]) for axis in left)]
        left = [axis for axis in ("h", "x", "l", "z") if axis in names(axes[0])]
        return source.at[tuple(pick(axis, where, axes[0]) for axis in left)]

    def names(axis):
        return ("h", "l") if axis == "y" else (axis,)

    def pick(letter, where, axis):
        if letter not in names(axis):
            return slice(None)
        if letter == "h":
            return lax.div(where["y"], 2)
        if letter == "l":
            return lax.rem(where["y"], 2)
        return where[axis]

    waiting = {}
    for which in range(6):
        waiting[which, 0] = launch(which, 0)
    for stage in range(3):
        for which in range(6):
            axes = ORDERS[which // 2]
            for copy in waiting[which, stage]:
                copy.wait_recv()
            source = (grads, total_one, total_two)[stage][which]
            landing = (first, second, third)[stage][which]
            target = (total_one, total_two, outs)[stage][which]
            mine = part_of(source, at, axes, stage)
            target[...] = (mine[...] + landing[0]) + (landing[1] + landing[2])
            if stage < 2:
                waiting[which, stage + 1] = launch(which, stage + 1)
    for copies in waiting.values():
        for copy in copies:
            copy.wait_send()


def scatter_all(grads):
    block = (PAD, D)

    def shapes(which):
        axes = ORDERS[which // 2]
        dims = {"x": (4,), "z": (4,)}
        one = {"x": (2, 2, 4), "y": (4, 4), "z": (2, 4, 2)}[axes[2]]
        two = (2, 2) if axes[0] == "y" else (4,)
        return one, two

    scratch = []
    ones = [shapes(which)[0] for which in range(6)]
    twos = [shapes(which)[1] for which in range(6)]
    scratch += [pltpu.VMEM((3,) + one + block, jnp.float32) for one in ones]
    scratch += [pltpu.VMEM(one + block, jnp.float32) for one in ones]
    scratch += [pltpu.VMEM((3,) + two + block, jnp.float32) for two in twos]
    scratch += [pltpu.VMEM(two + block, jnp.float32) for two in twos]
    scratch += [pltpu.VMEM((3,) + block, jnp.float32)] * 6
    scratch += [pltpu.SemaphoreType.DMA((54,)), pltpu.SemaphoreType.DMA((54,))]
    return pl.pallas_call(
        scatter_kernel,
        out_shape=[jax.ShapeDtypeStruct(block, jnp.float32)] * 6,
        in_specs=[pl.BlockSpec(memory_space=pltpu.VMEM)] * 6,
        out_specs=[pl.BlockSpec(memory_space=pltpu.VMEM)] * 6,
        scratch_shapes=scratch,
        compiler_params=pltpu.CompilerParams(
            collective_id=1, has_side_effects=True, vmem_limit_bytes=40 * 2**20
        ),
        name="scatter_grads",
    )(*grads)


SMALL = ("z", "x", "y")


def pool_kernel(x_ref, o_ref, other, send, recv):
    at = place()
    sems = (send, recv)
    greet(at)
    swap = remote(x_ref, other, sems, 0, moved(at, "core", 1))
    swap.start()
    swap.wait()
    view = box(o_ref, at, ())
    view[...] = (x_ref[...] + other[...]).astype(jnp.bfloat16).astype(jnp.float32)
    for stage in range(3):
        copies = []
        for by in (1, 2, 3):
            view = box(o_ref, at, SMALL[:stage])
            copy = remote(view, view, sems, 1 + stage * 3 + by - 1, moved(at, SMALL[stage], by))
            copy.start()
            copies.append(copy)
        for copy in copies:
            copy.wait()


def gather_pooled(row):
    return pl.pallas_call(
        pool_kernel,
        out_shape=jax.ShapeDtypeStruct((2, 4, 2, 4) + row.shape, row.dtype),
        in_specs=[pl.BlockSpec(memory_space=pltpu.VMEM)],
        out_specs=pl.BlockSpec(memory_space=pltpu.VMEM),
        scratch_shapes=[
            pltpu.VMEM(row.shape, row.dtype),
            pltpu.SemaphoreType.DMA((10,)),
            pltpu.SemaphoreType.DMA((10,)),
        ],
        compiler_params=pltpu.CompilerParams(collective_id=2, has_side_effects=True),
        name="gather_pooled",
    )(row)


def pull_kernel(x_ref, o_ref, first, total_one, second, total_two, third, mine, other, send, recv):
    at = place()
    sems = (send, recv)
    greet(at)

    def stage(number, axis, views, landing):
        copies = []
        for by in (1, 2, 3):
            copy = remote(
                views(moved(at, axis, by)), landing.at[by - 1], sems, number * 3 + by - 1, moved(at, axis, by)
            )
            copy.start()
            copies.append(copy)
        for copy in copies:
            copy.wait()
        return (views(at)[...] + landing[0]) + (landing[1] + landing[2])

    total_one[...] = stage(0, "y", lambda where: box(x_ref, where, ("x", "z")), first)
    total_two[...] = stage(1, "x", lambda where: total_one.at[where["x"]], second)
    mine[...] = stage(2, "z", lambda where: total_two.at[where["z"]], third)
    swap = remote(mine, other, sems, 9, moved(at, "core", 1))
    swap.start()
    swap.wait()
    o_ref[...] = mine[...] + other[...]


def pull_rows(rows):
    block = rows.shape[4:]
    return pl.pallas_call(
        pull_kernel,
        out_shape=jax.ShapeDtypeStruct(block, rows.dtype),
        in_specs=[pl.BlockSpec(memory_space=pltpu.VMEM)],
        out_specs=pl.BlockSpec(memory_space=pltpu.VMEM),
        scratch_shapes=[
            pltpu.VMEM((3, 4, 4) + block, rows.dtype),
            pltpu.VMEM((4, 4) + block, rows.dtype),
            pltpu.VMEM((3, 4) + block, rows.dtype),
            pltpu.VMEM((4,) + block, rows.dtype),
            pltpu.VMEM((3,) + block, rows.dtype),
            pltpu.VMEM(block, rows.dtype),
            pltpu.VMEM(block, rows.dtype),
            pltpu.SemaphoreType.DMA((10,)),
            pltpu.SemaphoreType.DMA((10,)),
        ],
        compiler_params=pltpu.CompilerParams(collective_id=3, has_side_effects=True),
        name="pull_rows",
    )(rows)


def total_kernel(x_ref, o_ref, slots, sums, send, recv):
    at = place()
    sems = (send, recv)
    greet(at)
    number = 0
    source = x_ref
    for stage, axis in enumerate(("core", "z", "x", "y")):
        size = 2 if axis == "core" else 4
        copies = []
        for by in range(1, size):
            copy = remote(source, slots.at[stage, at[axis]], sems, number, moved(at, axis, by))
            copy.start()
            copies.append(copy)
            number += 1
        slots[stage, at[axis]] = source[...]
        for copy in copies:
            copy.wait()
        total = slots[stage, 0]
        for index in range(1, size):
            total = total + slots[stage, index]
        if stage == 3:
            o_ref[...] = total
        else:
            sums[stage] = total
            source = sums.at[stage]


def total_all(value):
    return pl.pallas_call(
        total_kernel,
        out_shape=jax.ShapeDtypeStruct(value.shape, value.dtype),
        in_specs=[pl.BlockSpec(memory_space=pltpu.VMEM)],
        out_specs=pl.BlockSpec(memory_space=pltpu.VMEM),
        scratch_shapes=[
            pltpu.VMEM((4, 4) + value.shape, value.dtype),
            pltpu.VMEM((3,) + value.shape, value.dtype),
            pltpu.SemaphoreType.DMA((10,)),
            pltpu.SemaphoreType.DMA((10,)),
        ],
        compiler_params=pltpu.CompilerParams(collective_id=4, has_side_effects=True),
        name="total_all",
    )(value)


def swap_kernel(count, x_ref, o_ref, send, recv, local):
    me = lax.axis_index("exp")
    barrier = pltpu.get_barrier_semaphore()
    for by in range(1, count):
        peer = lax.rem(me + by, count)
        pl.semaphore_signal(barrier, inc=1, device_id={"exp": peer}, device_id_type=MESH)
    own = pltpu.make_async_copy(x_ref.at[me], o_ref.at[me], local)
    own.start()
    pl.semaphore_wait(barrier, count - 1)
    copies = []
    for by in range(1, count):
        peer = lax.rem(me + by, count)
        copy = pltpu.make_async_remote_copy(
            src_ref=x_ref.at[peer],
            dst_ref=o_ref.at[me],
            send_sem=send.at[by],
            recv_sem=recv.at[by],
            device_id={"exp": peer},
            device_id_type=MESH,
        )
        copy.start()
        copies.append(copy)
    own.wait()
    for copy in copies:
        copy.wait()


def swap_experts(rows):
    count = rows.shape[0]
    return pl.pallas_call(
        functools.partial(swap_kernel, count),
        out_shape=jax.ShapeDtypeStruct(rows.shape, rows.dtype),
        in_specs=[pl.BlockSpec(memory_space=pltpu.VMEM)],
        out_specs=pl.BlockSpec(memory_space=pltpu.VMEM),
        scratch_shapes=[
            pltpu.SemaphoreType.DMA((count,)),
            pltpu.SemaphoreType.DMA((count,)),
            pltpu.SemaphoreType.DMA(()),
        ],
        compiler_params=pltpu.CompilerParams(collective_id=5, has_side_effects=True),
        name="swap_experts",
    )(rows)


def across_cores(value):
    return lax.ppermute(value, "rep", CORE_SWAP)


def across_y(value):
    return lax.ppermute(value, "rep", Y_SWAP)


def shards(
    patches,
    expert_ids,
    labels,
    label_count,
    square_weights,
    router_weight,
    position_table,
    head_weight,
    expert_weights,
    vector_params,
    square_rows,
    square_cols,
    router_rows,
    router_cols,
    position_rows,
    position_cols,
    head_rows,
    head_cols,
    expert_rows,
    expert_cols,
    vector_moment,
):
    bfloat = jnp.bfloat16
    num_rep = lax.axis_size("rep")
    num_exp = lax.axis_size("exp")
    rep_index = lax.axis_index("rep")
    my_image = lax.axis_index("exp")
    device_index = lax.axis_index(("rep", "exp"))
    micro, core = rep_index // 2, rep_index % 2
    num_expert = router_weight.shape[1]
    vocab_dev = head_weight.shape[1]
    ff_dev = expert_weights.shape[3]
    block = patches.shape[2]
    rows, width = 2 * block, patches.shape[3]
    num_top = expert_ids.shape[3]
    heads = width // HEAD
    scale = HEAD ** (-0.5)
    own_rows = square_weights.shape[1]

    def pad_rows(value):
        return jnp.pad(value, ((0, PAD - own_rows), (0, width - value.shape[1])))

    quarter = expert_weights[0].astype(bfloat)
    quarter_y = across_y(quarter)
    quarter_pair = across_cores(jnp.stack([quarter, quarter_y]))
    quarters = [quarter, quarter_y, quarter_pair[0], quarter_pair[1]]

    mine = lax.dynamic_index_in_dim(patches, micro, 0, keepdims=False)[0]
    theirs = across_y(lax.dynamic_index_in_dim(patches, 1 - micro, 0, keepdims=False)[0])
    patch_rows = jnp.where(
        micro == 0, jnp.concatenate([mine, theirs]), jnp.concatenate([theirs, mine])
    )
    mine = lax.dynamic_index_in_dim(expert_ids, micro, 0, keepdims=False)[0]
    theirs = across_y(lax.dynamic_index_in_dim(expert_ids, 1 - micro, 0, keepdims=False)[0])
    ids = jnp.where(micro == 0, jnp.concatenate([mine, theirs]), jnp.concatenate([theirs, mine]))

    table_t = position_table.T
    table_high = lax.reduce_precision(table_t, 8, 7)
    table_low = (table_t - table_high).astype(bfloat)
    vector_t = vector_params.T
    vector_high = lax.reduce_precision(vector_t, 8, 7)
    vector_low = (vector_t - vector_high).astype(bfloat)
    extra = jnp.concatenate(
        [table_high.astype(bfloat), router_weight.astype(bfloat), vector_high.astype(bfloat), vector_low],
        axis=1,
    )
    square_low = square_weights.astype(bfloat)
    spare = jnp.pad(table_low, ((0, 0), (0, width - PATCHES))).reshape(3, 2, width)
    payload = jnp.concatenate(
        [square_low[0], spare[0], square_low[1], spare[1], square_low[2], spare[2]]
        + [pad_rows(square_low[3]), pad_rows(square_low[4]), pad_rows(extra)],
        axis=0,
    ).reshape(3, 16, width)
    gathered = [part.reshape(-1, 2, PAD, width) for part in gather_all(payload)]
    squares = [gathered[k // 2][:, k % 2, :own_rows].reshape(width, width) for k in range(5)]
    extra = gathered[2][:, 1, :own_rows, :].reshape(width, width)
    low = jnp.stack(
        [gathered[0][:, 0, 6:], gathered[0][:, 1, 6:], gathered[1][:, 0, 6:]], axis=1
    ).reshape(width, width)
    table = (
        extra[:, :PATCHES].astype(jnp.float32) + low[:, :PATCHES].astype(jnp.float32)
    ).T
    router = extra[:, PATCHES : PATCHES + num_expert]
    begin = PATCHES + num_expert
    vectors = (
        extra[:, begin : begin + 10].astype(jnp.float32)
        + extra[:, begin + 10 : begin + 20].astype(jnp.float32)
    ).T
    table_rows = jnp.concatenate(
        [
            lax.dynamic_slice_in_dim(table, core * block, block, 0),
            lax.dynamic_slice_in_dim(table, (2 + core) * block, block, 0),
        ]
    )
    head_low = head_weight.astype(bfloat)
    valid = (label_count > 0).astype(jnp.float32)
    image_count = jnp.sum(valid)
    columns = device_index * vocab_dev + jnp.arange(vocab_dev, dtype=jnp.int32)
    slot_range = jnp.arange(num_expert * 2 * CAP, dtype=jnp.int32)
    expert_range = jnp.arange(num_expert, dtype=jnp.int32)
    label_range = jnp.arange(labels.shape[2], dtype=jnp.int32)

    slot_index = jnp.arange(num_exp * 2 * PAD, dtype=jnp.int32)

    def picker(which):
        first = (slot_index // (num_exp * PAD)) * (2 * num_exp) + which * num_exp
        owner = first + (slot_index % (num_exp * PAD)) // PAD
        inside = slot_index % PAD
        row = jnp.where(inside < own_rows, owner * own_rows + inside, -1)
        return jnp.arange(width, dtype=jnp.int32)[:, None] == row[None, :]

    pick_mine, pick_theirs = picker(core), picker(1 - core)
    pick_mine_low, pick_theirs_low = pick_mine.astype(bfloat), pick_theirs.astype(bfloat)

    def share_left(value):
        theirs = across_cores(plain_dot(value, pick_theirs_low).astype(bfloat))
        return jnp.concatenate([plain_dot(value, pick_mine_low).astype(bfloat), theirs])

    def share_right(value):
        return jnp.concatenate([value, across_cores(value)])

    left_patches = share_left(patch_rows)
    embed = plain_dot(patch_rows, squares[0]) + vectors[0] + table_rows
    norm_one, pull_one = jax.vjp(layer_norm, embed, vectors[1], vectors[2])
    hidden_one = norm_one.astype(bfloat)
    query = (plain_dot(hidden_one, squares[1]) + vectors[3]).astype(bfloat)
    key_rows = plain_dot(hidden_one, squares[2]).astype(bfloat)
    value_rows = (plain_dot(hidden_one, squares[3]) + vectors[4]).astype(bfloat)
    both = jnp.concatenate([key_rows, value_rows], axis=1)
    both_all = jnp.concatenate([both, across_cores(both)])
    left_one = share_left(hidden_one)
    query_h = query.reshape(rows, heads, HEAD)
    key_h = both_all[:, :width].reshape(-1, heads, HEAD)
    value_h = both_all[:, width:].reshape(-1, heads, HEAD)
    scores = jnp.einsum("qhd,khd->hqk", query_h, key_h, preferred_element_type=jnp.float32) * scale
    probs = jax.nn.softmax(scores, axis=-1)
    probs_low = probs.astype(bfloat)
    mixed = jnp.einsum("hqk,khd->qhd", probs_low, value_h, preferred_element_type=jnp.float32)
    mixed = mixed.reshape(rows, width).astype(bfloat)
    left_mixed = share_left(mixed)
    after_attn = embed + plain_dot(mixed, squares[4]) + vectors[5]
    norm_two, pull_two = jax.vjp(layer_norm, after_attn, vectors[6], vectors[7])
    hidden_two = norm_two.astype(bfloat)
    gate_probs = jax.nn.softmax(plain_dot(hidden_two, router), axis=-1)
    chosen = ids[:, :, None] == expert_range[None, None, :]
    chosen_float = chosen.astype(jnp.float32)
    gates = jnp.sum(gate_probs[:, None, :] * chosen_float, axis=-1)
    flat_hit = chosen.reshape(2, block * num_top, num_expert).astype(jnp.int32)
    before = jnp.cumsum(flat_hit, axis=1) - flat_hit
    slot = jnp.sum(before * flat_hit, axis=2) + jnp.array([[0], [CAP]], jnp.int32)
    target = ids.reshape(-1) * (2 * CAP) + slot.reshape(-1)
    placing = (target[:, None] == slot_range[None, :]).astype(bfloat)
    copies = jnp.repeat(hidden_two, num_top, axis=0)
    outgoing = over_rows(placing, copies).astype(bfloat).reshape(num_expert, 2 * CAP, width)
    received = swap_experts(outgoing).reshape(-1, width)
    pre_act = [plain_dot(received, part[0]) for part in quarters]
    act = [jax.nn.gelu(part).astype(bfloat) for part in pre_act]
    result = sum(over_last(left, part[1]) for left, part in zip(act, quarters))
    returned = swap_experts(result.astype(bfloat).reshape(num_expert, 2 * CAP, width))
    gathered_rows = plain_dot(placing, returned.reshape(-1, width)).reshape(rows, num_top, width)
    after_moe = after_attn + jnp.sum(gates[:, :, None] * gathered_rows, axis=1)
    norm_final, pull_final = jax.vjp(layer_norm, after_moe, vectors[8], vectors[9])

    partial_pool = jnp.sum(norm_final, axis=0) / PATCHES
    lanes = jnp.pad(partial_pool, (0, PAD * LANES - width)).reshape(PAD, LANES)
    pooled = gather_pooled(lanes).reshape(2 * num_exp, PAD * LANES)[:, :width].astype(bfloat)
    logits = plain_dot(pooled, head_low)
    label_rows = labels.reshape(2 * num_exp, -1)
    live = label_range[None, :] < label_count.reshape(-1)[:, None]
    targets = jnp.any(
        (label_rows[:, :, None] == columns[None, None, :]) & live[:, :, None], axis=1
    ).astype(jnp.float32)
    valid_rows = valid.reshape(-1)
    loss_part = jnp.sum(valid_rows[:, None] * (jax.nn.softplus(logits) - targets * logits))
    dlogits = (valid_rows[:, None] * (jax.nn.sigmoid(logits) - targets) / image_count).astype(
        bfloat
    )
    head_g = over_rows(pooled, dlogits)
    pool_grad = jnp.pad(over_last(dlogits, head_low), ((0, 0), (0, PAD * LANES - width)))
    my_grad = pull_rows(pool_grad.reshape(2, 4, 2, 4, PAD, LANES)).reshape(-1)[:width] / PATCHES

    dmoe_in, dgain_final, dshift_final = pull_final(jnp.broadcast_to(my_grad, (rows, width)))
    dout_rows = (
        (gates[:, :, None] * dmoe_in[:, None, :]).astype(bfloat).reshape(rows * num_top, width)
    )
    dgates = jnp.sum(dmoe_in[:, None, :] * gathered_rows, axis=-1)
    dsend = over_rows(placing, dout_rows).astype(bfloat).reshape(num_expert, 2 * CAP, width)
    dreceived = swap_experts(dsend).reshape(-1, width)
    dact = [plain_dot(dreceived, part[1]) for part in quarters]
    dpre = [
        jax.vjp(jax.nn.gelu, pre)[1](grad)[0].astype(bfloat) for pre, grad in zip(pre_act, dact)
    ]
    dback = sum(over_last(left, part[0]) for left, part in zip(dpre, quarters))
    dreturn = swap_experts(dback.astype(bfloat).reshape(num_expert, 2 * CAP, width))
    quarter_grads = [
        jnp.stack([over_rows(received, dpre[k]), over_rows(dreceived, act[k])]) for k in range(4)
    ]
    from_core = across_cores(jnp.stack([quarter_grads[2], quarter_grads[3]]))
    from_y = across_y((quarter_grads[1] + from_core[1]).astype(bfloat))
    expert_g = (quarter_grads[0] + from_core[0] + from_y.astype(jnp.float32))[None]

    dcopies = plain_dot(placing, dreturn.reshape(-1, width)).reshape(rows, num_top, width)
    dprobs = jnp.sum(dgates[:, :, None] * chosen_float, axis=1)
    dgate_logits = (
        gate_probs * (dprobs - jnp.sum(gate_probs * dprobs, axis=-1, keepdims=True))
    ).astype(bfloat)
    router_grad = over_rows(hidden_two, dgate_logits)
    dhidden_two = over_last(dgate_logits, router) + jnp.sum(dcopies, axis=1)
    dnorm_two, dgain_two, dshift_two = pull_two(dhidden_two)
    dafter = dmoe_in + dnorm_two
    dafter_low = dafter.astype(bfloat)
    right_after = share_right(dafter_low)

    dmixed = over_last(dafter_low, squares[4]).astype(bfloat).reshape(rows, heads, HEAD)
    dprob = jnp.einsum("qhd,khd->hqk", dmixed, value_h, preferred_element_type=jnp.float32)
    row_shift = jnp.sum(probs * dprob, axis=-1, keepdims=True)
    dscores = (probs * (dprob - row_shift)).astype(bfloat)
    dquery = (
        jnp.einsum("hqk,khd->qhd", dscores, key_h, preferred_element_type=jnp.float32) * scale
    )
    dkey = jnp.einsum("hqk,qhd->khd", dscores, query_h, preferred_element_type=jnp.float32) * scale
    dvalue = jnp.einsum("hqk,qhd->khd", probs_low, dmixed, preferred_element_type=jnp.float32)
    dboth = jnp.concatenate([dkey.reshape(-1, width), dvalue.reshape(-1, width)], axis=1)
    dboth_own = dboth[:rows] + across_cores(dboth[rows:])
    dquery_low = dquery.reshape(rows, width).astype(bfloat)
    dkey_low = dboth_own[:, :width].astype(bfloat)
    dvalue_low = dboth_own[:, width:].astype(bfloat)
    right_qkv = share_right(jnp.concatenate([dquery_low, dkey_low, dvalue_low], axis=1))
    dhidden_one = (
        over_last(dquery_low, squares[1])
        + over_last(dkey_low, squares[2])
        + over_last(dvalue_low, squares[3])
    )
    bias_query = jnp.sum(dquery_low.astype(jnp.float32), axis=0)
    bias_value = jnp.sum(dvalue_low.astype(jnp.float32), axis=0)
    dnorm_one, dgain_one, dshift_one = pull_one(dhidden_one)
    dembed = dafter + dnorm_one
    right_embed = share_right(dembed.astype(bfloat))

    vector_grad = jnp.stack(
        [
            jnp.sum(dembed, axis=0),
            dgain_one,
            dshift_one,
            bias_query,
            bias_value,
            jnp.sum(dafter, axis=0),
            dgain_two,
            dshift_two,
            dgain_final,
            dshift_final,
        ]
    )
    few = jnp.concatenate([vector_grad, router_grad.T], axis=0)
    few = few + across_cores(few)
    pick_float = pick_mine.astype(jnp.float32)
    few_t = lax.dot_general(
        pick_float, few, (((0,), (1,)), ((), ())), precision=HIGHEST, preferred_element_type=jnp.float32
    )
    table_mine, table_theirs = (
        lax.dot_general(
            pick.astype(jnp.float32),
            dembed,
            (((0,), (1,)), ((), ())),
            precision=HIGHEST,
            preferred_element_type=jnp.float32,
        )
        for pick in (pick_mine, pick_theirs)
    )
    table_theirs = across_cores(table_theirs)
    extra_grad = jnp.concatenate(
        [
            jnp.where(core == 0, table_mine, table_theirs),
            jnp.where(core == 0, table_theirs, table_mine),
            few_t,
            jnp.zeros((few_t.shape[0], width - PATCHES - few_t.shape[1]), jnp.float32),
        ],
        axis=1,
    )
    shared = [
        over_rows(left_patches, right_embed),
        over_rows(left_one, right_qkv[:, :width]),
        over_rows(left_one, right_qkv[:, width : 2 * width]),
        over_rows(left_one, right_qkv[:, 2 * width :]),
        over_rows(left_mixed, right_after),
        extra_grad,
    ]
    owned = scatter_all([part.reshape(2, 4, 2, 4, PAD, width) for part in shared])
    square_g = jnp.stack([part[:own_rows] for part in owned[:5]])
    extra_g = owned[5][:own_rows]
    table_g = extra_g[:, :PATCHES].reshape(own_rows, 2, 2, block)
    table_g = table_g.transpose(0, 2, 1, 3).reshape(own_rows, PATCHES).T
    vector_g = extra_g[:, PATCHES : PATCHES + 10].T
    router_g = extra_g[:, PATCHES + 10 : PATCHES + 10 + num_expert]
    norm_part = (
        jnp.sum(square_g * square_g)
        + jnp.sum(router_g * router_g)
        + jnp.sum(table_g * table_g)
        + jnp.sum(vector_g * vector_g)
        + jnp.sum(head_g * head_g)
        + jnp.sum(expert_g * expert_g)
    )
    square_rowmean = jnp.mean(square_g * square_g, axis=2)
    router_rowmean = jnp.mean(router_g * router_g, axis=1)
    expert_rowsq = jnp.sum(expert_g * expert_g, axis=-1)
    expert_rowsq = expert_rowsq + across_cores(expert_rowsq)
    expert_mine = expert_rowsq + across_y(expert_rowsq)
    terms = (
        loss_part,
        norm_part,
        jnp.sum(square_g * square_g, axis=1),
        jnp.sum(square_rows, axis=1),
        jnp.sum(square_rowmean, axis=1),
        jnp.sum(router_g * router_g, axis=0),
        jnp.sum(router_rows),
        jnp.sum(router_rowmean),
        jnp.sum(table_g * table_g, axis=1),
        jnp.sum(head_g * head_g, axis=1),
    )
    flat = jnp.concatenate([term.reshape(-1) for term in terms])
    length = flat.shape[0]
    padded = -(-length // (8 * LANES)) * 8 * LANES
    flat = total_all(jnp.pad(flat, (0, padded - length)).reshape(-1, LANES)).reshape(-1)
    totals = []
    begin = 0
    for term in terms:
        totals.append(flat[begin : begin + term.size].reshape(term.shape))
        begin += term.size
    (
        loss_total,
        norm_total,
        square_colsq,
        square_rows_sum,
        square_mean_sum,
        router_colsq,
        router_rows_sum,
        router_mean_sum,
        table_rowsq,
        head_rowsq,
    ) = totals
    grad_norm = jnp.sqrt(norm_total)
    clip = jnp.minimum(1.0, CLIP_NORM / grad_norm)
    clip_sq = clip * clip
    keep = 1.0 - DECAY
    square_clip = clip * square_g
    square_rows_next = DECAY * square_rows + keep * (clip_sq * square_rowmean + EPS_SQ)
    square_cols_next = DECAY * square_cols + keep * (clip_sq * square_colsq / width + EPS_SQ)
    square_mean = (
        DECAY * square_rows_sum + keep * (clip_sq * square_mean_sum + width * EPS_SQ)
    ) / width
    square_rate = jnp.array([1.0, 1.0, 1.0, 1.0, 4.0], jnp.float32)[:, None, None] * (
        0.3 / math.sqrt(D)
    )
    square_next = factored_step(
        square_weights,
        square_clip,
        square_rows_next,
        square_cols_next,
        square_mean[:, None, None],
        square_rate,
    )
    router_clip = clip * router_g
    router_rows_next = DECAY * router_rows + keep * (clip_sq * router_rowmean + EPS_SQ)
    router_cols_next = DECAY * router_cols + keep * (clip_sq * router_colsq / width + EPS_SQ)
    router_mean = (
        DECAY * router_rows_sum + keep * (clip_sq * router_mean_sum + width * EPS_SQ)
    ) / width
    router_next = factored_step(
        router_weight,
        router_clip,
        router_rows_next,
        router_cols_next,
        router_mean,
        0.2 / math.sqrt(D),
    )
    table_clip = clip * table_g
    table_rows_next = DECAY * position_rows + keep * (clip_sq * table_rowsq / width + EPS_SQ)
    table_cols_next = DECAY * position_cols + keep * (
        clip_sq * jnp.mean(table_g * table_g, axis=0) + EPS_SQ
    )
    table_next = factored_step(
        position_table,
        table_clip,
        table_rows_next,
        table_cols_next,
        jnp.mean(table_rows_next),
        0.15,
    )
    head_clip = clip * head_g
    head_rows_next = DECAY * head_rows + keep * (
        clip_sq * head_rowsq / (vocab_dev * num_rep * num_exp) + EPS_SQ
    )
    head_cols_next = DECAY * head_cols + keep * (
        clip_sq * jnp.mean(head_g * head_g, axis=0) + EPS_SQ
    )
    head_next = factored_step(
        head_weight,
        head_clip,
        head_rows_next,
        head_cols_next,
        jnp.mean(head_rows_next),
        0.5 / math.sqrt(D),
    )
    expert_clip = clip * expert_g
    expert_rows_next = DECAY * expert_rows + keep * (
        clip_sq * expert_mine / (ff_dev * num_rep) + EPS_SQ
    )
    expert_cols_next = DECAY * expert_cols + keep * (
        clip_sq * jnp.mean(expert_g * expert_g, axis=2) + EPS_SQ
    )
    expert_rate = jnp.array([0.3 / math.sqrt(D), 4.8 / math.sqrt(FF)], jnp.float32)[
        None, :, None, None
    ]
    expert_next = factored_step(
        expert_weights,
        expert_clip,
        expert_rows_next,
        expert_cols_next,
        jnp.mean(expert_rows_next, axis=-1)[..., None, None],
        expert_rate,
    )
    vector_clip = clip * vector_g
    moment_next = DECAY * vector_moment + keep * (vector_clip * vector_clip + EPS_SQ)
    vector_next = vector_params - 0.3 * vector_clip * lax.rsqrt(moment_next)
    return (
        loss_total,
        image_count,
        grad_norm,
        square_clip,
        square_rows_next,
        square_cols_next,
        square_next,
        router_clip,
        router_rows_next,
        router_cols_next,
        router_next,
        table_clip,
        table_rows_next,
        table_cols_next,
        table_next,
        head_clip,
        head_rows_next,
        head_cols_next,
        head_next,
        expert_clip,
        expert_rows_next,
        expert_cols_next,
        expert_next,
        vector_clip,
        moment_next,
        vector_next,
    )


def solution(mesh):
    in_specs = (
        P(None, "exp", "rep", None),
        P(None, "exp", "rep", None),
        P(),
        P(),
        P(None, ("rep", "exp"), None),
        P(("rep", "exp"), None),
        P(None, ("rep", "exp")),
        P(None, ("rep", "exp")),
        P("exp", None, None, "rep"),
        P(None, ("rep", "exp")),
        P(None, ("rep", "exp")),
        P(),
        P(("rep", "exp")),
        P(),
        P(),
        P(("rep", "exp")),
        P(),
        P(("rep", "exp")),
        P("exp", None, None),
        P("exp", None, "rep"),
        P(None, ("rep", "exp")),
    )
    out_specs = (
        P(),
        P(),
        P(),
        P(None, ("rep", "exp"), None),
        P(None, ("rep", "exp")),
        P(),
        P(None, ("rep", "exp"), None),
        P(("rep", "exp"), None),
        P(("rep", "exp")),
        P(),
        P(("rep", "exp"), None),
        P(None, ("rep", "exp")),
        P(),
        P(("rep", "exp")),
        P(None, ("rep", "exp")),
        P(None, ("rep", "exp")),
        P(),
        P(("rep", "exp")),
        P(None, ("rep", "exp")),
        P("exp", None, None, "rep"),
        P("exp", None, None),
        P("exp", None, "rep"),
        P("exp", None, None, "rep"),
        P(None, ("rep", "exp")),
        P(None, ("rep", "exp")),
        P(None, ("rep", "exp")),
    )
    return jax.shard_map(shards, mesh=mesh, in_specs=in_specs, out_specs=out_specs, check_vma=False)
```

```python
import functools
import math

import jax
import jax.numpy as jnp
from jax import lax
from jax.experimental import pallas as pl
from jax.experimental.pallas import tpu as pltpu
from jax.sharding import PartitionSpec as P

D = 768
HEAD = 64
FF = 3072
PATCHES = 576
CAP = 10
VOCAB_DEV = 171
PAD = 8
LANES = 128


DECAY = 0.8
EPS_SQ = 1e-30
CLIP_NORM = 0.25
HIGHEST = lax.Precision.HIGHEST
MESH = pl.DeviceIdType.MESH

Y_SWAP = ((0, 2), (1, 3), (2, 0), (3, 1))
CORE_SWAP = ((0, 1), (1, 0), (2, 3), (3, 2))


def layer_norm(value, gain, shift):
    centred = value - jnp.mean(value, axis=-1, keepdims=True)
    spread = jnp.mean(centred * centred, axis=-1, keepdims=True)
    return centred * lax.rsqrt(spread + 1e-06) * gain + shift


def plain_dot(left, right):
    return jnp.dot(left, right, preferred_element_type=jnp.float32)


def over_rows(left, right):
    return lax.dot_general(
        left, right, (((0,), (0,)), ((), ())), preferred_element_type=jnp.float32
    )


def over_last(left, right):
    return lax.dot_general(
        left, right, (((1,), (1,)), ((), ())), preferred_element_type=jnp.float32
    )


def factored_step(weight, clipped, rows_next, cols_next, rows_mean, rate):
    estimate = rows_next[..., :, None] * cols_next[..., None, :] / rows_mean
    return weight - rate * clipped * lax.rsqrt(estimate)


def place():
    rep = lax.axis_index("rep")
    line = lax.axis_index("exp")
    y = lax.div(rep, 2) * 2 + lax.rem(lax.div(line, 4), 2)
    return {"y": y, "core": lax.rem(rep, 2), "x": lax.div(line, 8), "z": lax.rem(line, 4)}


def device(at):
    return {
        "rep": lax.div(at["y"], 2) * 2 + at["core"],
        "exp": at["x"] * 8 + lax.rem(at["y"], 2) * 4 + at["z"],
    }


def moved(at, axis, by):
    return {**at, axis: lax.rem(at[axis] + by, 2 if axis == "core" else 4)}


def box(ref, at, free, core=False):
    whole = slice(None)
    hi = whole if "y" in free else lax.div(at["y"], 2)
    low = whole if "y" in free else lax.rem(at["y"], 2)
    x = whole if "x" in free else at["x"]
    z = whole if "z" in free else at["z"]
    if core:
        return ref.at[hi, at["core"], x, low, z]
    return ref.at[hi, x, low, z]


def greet(at):
    barrier = pltpu.get_barrier_semaphore()
    peers = [moved(at, axis, by) for axis in ("x", "y", "z") for by in (1, 2, 3)]
    peers.append(moved(at, "core", 1))
    for peer in peers:
        pl.semaphore_signal(barrier, inc=1, device_id=device(peer), device_id_type=MESH)
    pl.semaphore_wait(barrier, len(peers))


def remote(src, dst, sems, index, peer):
    return pltpu.make_async_remote_copy(
        src_ref=src,
        dst_ref=dst,
        send_sem=sems[0].at[index],
        recv_sem=sems[1].at[index],
        device_id=device(peer),
        device_id_type=MESH,
    )


ORDERS = (("x", "y", "z"), ("y", "z", "x"), ("z", "x", "y"))


def gather_kernel(x_ref, *refs):
    squares, extra, spare = refs[:5], refs[5], refs[6]
    outs, (send, recv, local) = refs[7:10], refs[10:]
    at = place()
    sems = (send, recv)
    own = []
    for part in range(3):
        own.append(
            pltpu.make_async_copy(
                x_ref.at[part], box(outs[part], at, (), True), local.at[part]
            )
        )
        own[part].start()
    greet(at)
    flights = {}

    def launch(part, stage):
        axes = ORDERS[part]
        view = box(outs[part], at, axes[:stage], True)
        source = x_ref.at[part] if stage == 0 else view
        for by in (1, 2, 3):
            copy = remote(source, view, sems, part * 13 + stage * 3 + by - 1, moved(at, axes[stage], by))
            copy.start()
            flights[part, stage, by] = copy

    def forward(part, by):
        axes = ORDERS[part]
        view = box(outs[part], moved(at, axes[2], 4 - by), axes[:2], True)
        copy = remote(view, view, sems, part * 13 + 9 + by, moved(at, "core", 1))
        copy.start()
        flights[part, 3, by] = copy

    for part in range(3):
        launch(part, 0)
    for stage in (1, 2):
        for part in range(3):
            if stage == 1:
                own[part].wait()
            for by in (1, 2, 3):
                flights[part, stage - 1, by].wait_recv()
            launch(part, stage)
            if stage == 2:
                forward(part, 0)
    for by in (1, 3, 2):
        for part in range(3):
            flights[part, 2, by].wait_recv()
            forward(part, by)

    row = lax.broadcasted_iota(jnp.int32, (96, 256), 0)
    column = lax.broadcasted_iota(jnp.int32, (96, 256), 1)
    base = lax.div(row, 6) * 16
    inside = lax.rem(row, 6)

    def packer(offset):
        return (column == base + offset + inside).astype(jnp.bfloat16)

    first, second = packer(0), packer(8)
    low_first = jnp.where(inside < 2, packer(6), jnp.where(inside < 4, packer(12), 0)).astype(jnp.bfloat16)
    low_second = jnp.where(inside < 4, 0, packer(2)).astype(jnp.bfloat16)
    packers = [
        jnp.concatenate([first, second, low_first]),
        jnp.concatenate([first, second, low_second]),
        jnp.concatenate([first, second]),
    ]

    def pack(core):
        def step(index, carry):
            high, half = lax.div(index, 2), lax.rem(index, 2)
            place_out = pl.ds(pl.multiple_of((high * 4 + core * 2 + half) * 96, 96), 96)
            packed = []
            for part in range(3):
                block = outs[part][high, core, pl.ds(half * 2, 2)].reshape(256, D)
                packed.append(plain_dot(packers[part], block))
            for k in range(5):
                low = packed[k // 2][96 * (k % 2) : 96 * (k % 2) + 96]
                squares[k][place_out, :] = low.astype(jnp.bfloat16)
            extra[place_out, :] = packed[2][96:].astype(jnp.bfloat16)
            spare[place_out, :] = (packed[0][192:] + packed[1][192:]).astype(jnp.bfloat16)
            return carry

        lax.fori_loop(0, 4, step, 0)

    pack(at["core"])
    for key, copy in flights.items():
        if key[1] == 3:
            copy.wait_recv()
    pack(1 - at["core"])
    for copy in flights.values():
        copy.wait_send()


def gather_all(payload):
    shape = (2, 2, 4, 2, 4, 16, D)
    return pl.pallas_call(
        gather_kernel,
        out_shape=[jax.ShapeDtypeStruct((D, D), payload.dtype)] * 7,
        in_specs=[pl.BlockSpec(memory_space=pltpu.VMEM)],
        out_specs=[pl.BlockSpec(memory_space=pltpu.VMEM)] * 7,
        scratch_shapes=[pltpu.VMEM(shape, payload.dtype)] * 3
        + [
            pltpu.SemaphoreType.DMA((39,)),
            pltpu.SemaphoreType.DMA((39,)),
            pltpu.SemaphoreType.DMA((3,)),
        ],
        compiler_params=pltpu.CompilerParams(
            collective_id=0, has_side_effects=True, vmem_limit_bytes=40 * 2**20
        ),
        name="gather_weights",
    )(payload)


def scatter_kernel(*refs):
    grads, outs = refs[:3], refs[3:6]
    first, total_one, second, total_two, third = (refs[6 + 3 * i : 9 + 3 * i] for i in range(5))
    sems = refs[21:23]
    at = place()
    greet(at)

    def names(axis):
        return ("h", "l") if axis == "y" else (axis,)

    def pick(letter, where, axis):
        if letter not in names(axis):
            return slice(None)
        if letter == "h":
            return lax.div(where["y"], 2)
        if letter == "l":
            return lax.rem(where["y"], 2)
        return where[axis]

    def part_of(source, where, axes, stage):
        if stage == 0:
            return box(source, where, axes[:2])
        if stage == 1:
            left = [letter for letter in ("h", "x", "l", "z") if letter not in names(axes[2])]
            return source.at[tuple(pick(letter, where, axes[1]) for letter in left)]
        return source.at[tuple(pick(letter, where, axes[0]) for letter in names(axes[0]))]

    sources = (grads, total_one, total_two)
    landings = (first, second, third)
    targets = (total_one, total_two, outs)
    flights = {}

    def launch(part, stage):
        axes = ORDERS[part]
        axis = axes[2 - stage]
        flights[part, stage] = []
        for by in (1, 2, 3):
            peer = moved(at, axis, by)
            view = part_of(sources[stage][part], peer, axes, stage)
            copy = remote(view, landings[stage][part].at[by - 1], sems, part * 9 + stage * 3 + by - 1, peer)
            copy.start()
            flights[part, stage].append(copy)

    for part in range(3):
        launch(part, 0)
    for stage in range(3):
        for part in range(3):
            for copy in flights[part, stage]:
                copy.wait_recv()
            landing = landings[stage][part]
            terms = [part_of(sources[stage][part], at, ORDERS[part], stage)[...]]
            terms = [term.astype(jnp.float32) for term in terms + [landing[i] for i in range(3)]]
            targets[stage][part][...] = (terms[0] + terms[1]) + (terms[2] + terms[3])
            if stage < 2:
                launch(part, stage + 1)
    for copies in flights.values():
        for copy in copies:
            copy.wait_send()


def scatter_all(grads):
    block = (2 * PAD, D)
    ones = [{"x": (2, 2, 4), "y": (4, 4), "z": (2, 4, 2)}[axes[2]] for axes in ORDERS]
    twos = [(2, 2) if axes[0] == "y" else (4,) for axes in ORDERS]
    scratch = [pltpu.VMEM((3,) + one + block, jnp.bfloat16) for one in ones]
    scratch += [pltpu.VMEM(one + block, jnp.float32) for one in ones]
    scratch += [pltpu.VMEM((3,) + two + block, jnp.float32) for two in twos]
    scratch += [pltpu.VMEM(two + block, jnp.float32) for two in twos]
    scratch += [pltpu.VMEM((3,) + block, jnp.float32)] * 3
    scratch += [pltpu.SemaphoreType.DMA((27,)), pltpu.SemaphoreType.DMA((27,))]
    return pl.pallas_call(
        scatter_kernel,
        out_shape=[jax.ShapeDtypeStruct(block, jnp.float32)] * 3,
        in_specs=[pl.BlockSpec(memory_space=pltpu.VMEM)] * 3,
        out_specs=[pl.BlockSpec(memory_space=pltpu.VMEM)] * 3,
        scratch_shapes=scratch,
        compiler_params=pltpu.CompilerParams(
            collective_id=1, has_side_effects=True, vmem_limit_bytes=40 * 2**20
        ),
        name="scatter_grads",
    )(*grads)


def meet_core(at):
    barrier = pltpu.get_barrier_semaphore()
    other = moved(at, "core", 1)
    pl.semaphore_signal(barrier, inc=1, device_id=device(other), device_id_type=MESH)
    pl.semaphore_wait(barrier, 1)
    return other


CHUNK = 48


def chunks(count, step, start=0):
    lax.fori_loop(0, count // CHUNK, lambda i, c: step(pl.ds(pl.multiple_of(i * CHUNK, CHUNK), CHUNK), c), start)


def centre(value):
    centred = value - jnp.mean(value, axis=-1, keepdims=True)
    spread = jnp.mean(centred * centred, axis=-1, keepdims=True)
    return centred * lax.rsqrt(spread + 1e-06), lax.rsqrt(spread + 1e-06)


def norm_back(value, grad, gain):
    normed, rate = centre(value)
    scaled = grad * gain
    inner = (
        scaled
        - jnp.mean(scaled, axis=-1, keepdims=True)
        - normed * jnp.mean(scaled * normed, axis=-1, keepdims=True)
    )
    return rate * inner, jnp.sum(grad * normed, axis=0, keepdims=True), jnp.sum(grad, axis=0, keepdims=True)


def attend_kernel(
    x_ref, w0, w1, w2, w3, w4, vec, table, router, ids,
    embed, hidden_one, query, keys, values, mixed, after, hidden_two, gate_probs, gates, lse,
    send, recv,
):
    at = place()
    sems = (send, recv)
    other = meet_core(at)
    rows = x_ref.shape[0]
    embed[...] = plain_dot(x_ref[...], w0[...])

    def first_norm(part, carry):
        value = embed[part, :] + vec[0:1, :] + table[part, :]
        embed[part, :] = value
        normed, _ = centre(value)
        hidden_one[part, :] = (normed * vec[1:2, :] + vec[2:3, :]).astype(jnp.bfloat16)
        return carry

    chunks(rows, first_norm)
    keys[0] = plain_dot(hidden_one[...], w2[...]).astype(jnp.bfloat16)
    send_keys = remote(keys.at[0], keys.at[1], sems, 0, other)
    send_keys.start()
    values[0] = (plain_dot(hidden_one[...], w3[...]) + vec[4:5, :]).astype(jnp.bfloat16)
    send_values = remote(values.at[0], values.at[1], sems, 1, other)
    send_values.start()
    query[...] = (plain_dot(hidden_one[...], w1[...]) + vec[3:4, :]).astype(jnp.bfloat16)
    send_keys.wait()
    send_values.wait()

    def heads(index, carry):
        lanes = pl.ds(pl.multiple_of(index * LANES, LANES), LANES)
        query_two = query[:, lanes]
        key_two = keys[:, :, lanes].reshape(2 * rows, LANES)
        value_t = values[:, :, lanes].reshape(2 * rows, LANES).T
        left = lax.broadcasted_iota(jnp.int32, (rows, LANES), 1) < HEAD
        outs = []
        for half in range(2):
            own = jnp.where(left if half == 0 else ~left, query_two, jnp.zeros_like(query_two))
            scores = over_last(key_two, own) * HEAD ** (-0.5)
            most = jnp.max(scores, axis=0, keepdims=True)
            raw = jnp.exp(scores - most)
            total = jnp.sum(raw, axis=0, keepdims=True)
            lse[pl.ds(index * 2 + half, 1), :] = most + jnp.log(total)
            probs = (raw * (1.0 / total)).astype(jnp.bfloat16)
            outs.append(plain_dot(value_t[half * HEAD : (half + 1) * HEAD], probs))
        mixed[:, lanes] = jnp.concatenate(outs).T.astype(jnp.bfloat16)
        return carry

    lax.fori_loop(0, D // LANES, heads, 0)
    after[...] = plain_dot(mixed[...], w4[...])

    def second_norm(part, carry):
        value = embed[part, :] + after[part, :] + vec[5:6, :]
        after[part, :] = value
        normed, _ = centre(value)
        low = (normed * vec[6:7, :] + vec[7:8, :]).astype(jnp.bfloat16)
        hidden_two[part, :] = low
        logits = plain_dot(low, router[...])
        lane = lax.broadcasted_iota(jnp.int32, logits.shape, 1)
        logits = jnp.where(lane < 32, logits, -jnp.inf)
        raw = jnp.exp(logits - jnp.max(logits, axis=-1, keepdims=True))
        probs = raw / jnp.sum(raw, axis=-1, keepdims=True)
        gate_probs[part, :] = probs
        first, second = (
            jnp.sum(jnp.where(lane == ids[part, k : k + 1], probs, 0.0), axis=-1, keepdims=True) for k in range(2)
        )
        gates[part, :] = jnp.where(lane == 0, first, second)
        return carry

    chunks(rows, second_norm)


def attend(patch_rows, squares, vectors, table_rows, router, ids):
    rows = patch_rows.shape[0]
    low, wide = jnp.bfloat16, jnp.float32
    shapes = [
        ((rows, D), wide), ((rows, D), low), ((rows, D), low), ((2, rows, D), low), ((2, rows, D), low),
        ((rows, D), low), ((rows, D), wide), ((rows, D), low), ((rows, LANES), wide), ((rows, LANES), wide), ((16, rows), wide),
    ]
    return pl.pallas_call(
        attend_kernel,
        out_shape=[jax.ShapeDtypeStruct(*shape) for shape in shapes],
        in_specs=[pl.BlockSpec(memory_space=pltpu.VMEM)] * 10,
        out_specs=[pl.BlockSpec(memory_space=pltpu.VMEM)] * 11,
        scratch_shapes=[pltpu.SemaphoreType.DMA((2,)), pltpu.SemaphoreType.DMA((2,))],
        compiler_params=pltpu.CompilerParams(
            collective_id=6, has_side_effects=True, vmem_limit_bytes=48 * 2**20
        ),
        name="attend",
    )(patch_rows, *squares, vectors, table_rows, router, ids)


def attend_back_kernel(
    dafter_in, dhidden, dgate, embed, after, hidden_one, query, keys, values, lse, w1, w2, w3, w4, vec, router,
    dafter_low, dquery, dkey, dvalue, dembed_low, sums,
    dafter, dmixed, dkey_own, dvalue_own, dkey_other, dvalue_other, dkey_got, dvalue_got, wide, send, recv,
):
    at = place()
    sems = (send, recv)
    other = meet_core(at)
    rows = dafter_in.shape[0]
    pairs = D // LANES
    zero = jnp.zeros((1, D), jnp.float32)
    wide[...] = over_last(dgate[...], router[...])

    def second_norm(index, carry):
        part = pl.ds(pl.multiple_of(index * CHUNK, CHUNK), CHUNK)
        grad = wide[part, :] + dhidden[part, :]
        back, gain, shift = norm_back(after[part, :], grad, vec[6:7, :])
        total = dafter_in[part, :] + back
        dafter[part, :] = total
        dafter_low[part, :] = total.astype(jnp.bfloat16)
        return carry[0] + jnp.sum(total, axis=0, keepdims=True), carry[1] + gain, carry[2] + shift

    bias, gain, shift = lax.fori_loop(0, rows // CHUNK, second_norm, (zero, zero, zero))
    sums[5:6, :] = bias
    sums[6:7, :] = gain
    sums[7:8, :] = shift
    dmixed[...] = over_last(dafter_low[...], w4[...]).astype(jnp.bfloat16)

    def flights(index):
        return (
            remote(dkey_other.at[index], dkey_got.at[index], sems, index, other),
            remote(dvalue_other.at[index], dvalue_got.at[index], sems, pairs + index, other),
        )

    def heads(index, carry):
        lanes = pl.ds(pl.multiple_of(index * LANES, LANES), LANES)
        query_two = query[:, lanes]
        dmixed_two = dmixed[:, lanes]
        key_two = keys[:, :, lanes].reshape(2 * rows, LANES)
        value_two = values[:, :, lanes].reshape(2 * rows, LANES)
        key_t = key_two.T
        left = lax.broadcasted_iota(jnp.int32, (rows, LANES), 1) < HEAD
        dkey_two = jnp.zeros((2 * rows, LANES), jnp.float32)
        dvalue_two = jnp.zeros((2 * rows, LANES), jnp.float32)
        outs = []
        for half in range(2):
            mask = left if half == 0 else ~left
            own = jnp.where(mask, query_two, jnp.zeros_like(query_two))
            down = jnp.where(mask, dmixed_two, jnp.zeros_like(dmixed_two))
            scores = over_last(key_two, own) * HEAD ** (-0.5)
            probs = jnp.exp(scores - lse[pl.ds(index * 2 + half, 1), :])
            dprobs = over_last(value_two, down)
            row_shift = jnp.sum(probs * dprobs, axis=0, keepdims=True)
            dscores = (probs * (dprobs - row_shift)).astype(jnp.bfloat16)
            dvalue_two = dvalue_two + plain_dot(probs.astype(jnp.bfloat16), down)
            dkey_two = dkey_two + plain_dot(dscores, own)
            outs.append(plain_dot(key_t[half * HEAD : (half + 1) * HEAD], dscores))
        dkey_two = dkey_two * HEAD ** (-0.5)
        dquery[:, lanes] = (jnp.concatenate(outs).T * HEAD ** (-0.5)).astype(jnp.bfloat16)
        dkey_own[index] = dkey_two[:rows]
        dkey_other[index] = dkey_two[rows:]
        dvalue_own[index] = dvalue_two[:rows]
        dvalue_other[index] = dvalue_two[rows:]
        for copy in flights(index):
            copy.start()
        return carry

    lax.fori_loop(0, pairs, heads, 0)

    def gather(index, carry):
        lanes = pl.ds(pl.multiple_of(index * LANES, LANES), LANES)
        for copy in flights(index):
            copy.wait()
        dkey[:, lanes] = (dkey_own[index] + dkey_got[index]).astype(jnp.bfloat16)
        dvalue[:, lanes] = (dvalue_own[index] + dvalue_got[index]).astype(jnp.bfloat16)
        return carry

    lax.fori_loop(0, pairs, gather, 0)
    wide[...] = (
        over_last(dquery[...], w1[...]) + over_last(dkey[...], w2[...]) + over_last(dvalue[...], w3[...])
    )

    def first_norm(index, carry):
        part = pl.ds(pl.multiple_of(index * CHUNK, CHUNK), CHUNK)
        back, gain, shift = norm_back(embed[part, :], wide[part, :], vec[1:2, :])
        total = dafter[part, :] + back
        dembed_low[part, :] = total.astype(jnp.bfloat16)
        return (
            carry[0] + jnp.sum(total, axis=0, keepdims=True),
            carry[1] + gain,
            carry[2] + shift,
            carry[3] + jnp.sum(dquery[part, :].astype(jnp.float32), axis=0, keepdims=True),
            carry[4] + jnp.sum(dvalue[part, :].astype(jnp.float32), axis=0, keepdims=True),
        )

    for index, total in enumerate(lax.fori_loop(0, rows // CHUNK, first_norm, (zero,) * 5)):
        sums[index : index + 1, :] = total


def attend_back(*operands):
    rows = operands[0].shape[0]
    low, wide = jnp.bfloat16, jnp.float32
    pairs = D // LANES
    return pl.pallas_call(
        attend_back_kernel,
        out_shape=[jax.ShapeDtypeStruct((rows, D), low)] * 5 + [jax.ShapeDtypeStruct((8, D), wide)],
        in_specs=[pl.BlockSpec(memory_space=pltpu.VMEM)] * 16,
        out_specs=[pl.BlockSpec(memory_space=pltpu.VMEM)] * 6,
        scratch_shapes=[pltpu.VMEM((rows, D), wide), pltpu.VMEM((rows, D), low)]
        + [pltpu.VMEM((pairs, rows, LANES), wide)] * 6
        + [pltpu.VMEM((rows, D), wide)]
        + [pltpu.SemaphoreType.DMA((2 * pairs,)), pltpu.SemaphoreType.DMA((2 * pairs,))],
        compiler_params=pltpu.CompilerParams(
            collective_id=7, has_side_effects=True, vmem_limit_bytes=48 * 2**20
        ),
        name="attend_back",
    )(*operands)


SLOTS = 16
TAIL = 2 * CAP - SLOTS
WIRE = D + 2 * LANES
GROUP = 32
MAIN = GROUP * SLOTS
TOTAL = GROUP * (SLOTS + TAIL)


def iota(shape, axis):
    return lax.broadcasted_iota(jnp.int32, shape, axis)


def pack(block, main, tail):
    count = block.shape[0]
    block[:, :, :D] = main.astype(jnp.bfloat16).reshape(count, SLOTS, D)
    shape = (count * SLOTS, count * TAIL)
    row, column = iota(shape, 0), iota(shape, 1)
    spread = (lax.div(row, SLOTS) == lax.div(column, TAIL)) & (lax.rem(row, TAIL) == lax.rem(column, TAIL))
    wide = plain_dot(spread.astype(jnp.bfloat16), tail.astype(jnp.bfloat16))
    turn = lax.div(lax.rem(iota((count * SLOTS, LANES), 0), SLOTS), TAIL)
    for half, tiles in ((0, (0, 1, 2, 3)), (1, (4, 5))):
        packed = jnp.zeros((count * SLOTS, LANES), jnp.float32)
        for place_in, tile in enumerate(tiles):
            packed = jnp.where(turn == place_in, wide[:, tile * LANES : (tile + 1) * LANES], packed)
        block[:, :, D + half * LANES : D + (half + 1) * LANES] = packed.astype(jnp.bfloat16).reshape(
            count, SLOTS, LANES
        )


def unpack(block, rows, first, first_tail):
    count = block.shape[0]
    rows[first : first + count * SLOTS, :] = block[:, :, :D].reshape(count * SLOTS, D)
    shape = (count * TAIL, count * SLOTS)
    row, column = iota(shape, 0), iota(shape, 1)
    same = lax.div(column, SLOTS) == lax.div(row, TAIL)
    packed = block[:, :, D:].reshape(count * SLOTS, 2 * LANES)
    for turn in range(4):
        chosen = same & (lax.rem(column, SLOTS) == turn * TAIL + lax.rem(row, TAIL))
        part = plain_dot(chosen.astype(jnp.bfloat16), packed).astype(jnp.bfloat16)
        rows[first_tail : first_tail + count * TAIL, turn * LANES : (turn + 1) * LANES] = part[:, :LANES]
        if turn < 2:
            rows[first_tail : first_tail + count * TAIL, (4 + turn) * LANES : (5 + turn) * LANES] = part[
                :, LANES:
            ]


def meet_experts(at):
    barrier = pltpu.get_barrier_semaphore()
    me = lax.axis_index("exp")

    def greet_one(by, carry):
        peer = lax.rem(me + by, GROUP)
        pl.semaphore_signal(barrier, inc=1, device_id={"exp": peer}, device_id_type=MESH)
        return carry

    lax.fori_loop(1, GROUP, greet_one, 0)
    other = moved(at, "core", 1)
    pl.semaphore_signal(barrier, inc=1, device_id=device(other), device_id_type=MESH)
    return other


def met_experts():
    pl.semaphore_wait(pltpu.get_barrier_semaphore(), GROUP)


def deal(source, target, sems, forth, low, high, act):
    me = lax.axis_index("exp")

    def one(by, carry):
        peer = lax.rem(me + by, GROUP) if forth else lax.rem(me + GROUP - by, GROUP)
        copy = pltpu.make_async_remote_copy(
            src_ref=source.at[peer] if forth else source.at[by],
            dst_ref=target.at[by] if forth else target.at[me],
            send_sem=sems[0].at[by],
            recv_sem=sems[1].at[by],
            device_id={"exp": peer},
            device_id_type=MESH,
        )
        act(copy)
        return carry

    lax.fori_loop(low, high, one, 0)


def start_copy(copy):
    copy.start()


def wait_send(copy):
    copy.wait_send()


def wait_recv(copy):
    copy.wait_recv()


def load_experts(own, across, weights, sems, local, other):
    near = [pltpu.make_async_copy(own, weights.at[0], local.at[0])]
    near.append(pltpu.make_async_copy(across, weights.at[1], local.at[1]))
    far = [remote(own, weights.at[2], sems, 0, other), remote(across, weights.at[3], sems, 1, other)]
    return near, far


GELU_SCALE = math.sqrt(2 / math.pi)


def gelu_tanh(value):
    return jnp.tanh(GELU_SCALE * (value + 0.044715 * (value * value * value)))


def halves(rows, half):
    count = MAIN // 2
    tail = (TOTAL - MAIN) // 2
    return jnp.concatenate(
        [
            rows[half * count : (half + 1) * count, :],
            rows[MAIN + half * tail : MAIN + (half + 1) * tail, :],
        ]
    )


HALF = TOTAL // 2


def experts_kernel(
    hidden, target_row, target_column, gates, after, vec, own, across,
    rows, chosen, total, pool,
    weights, sends, lands, backs, returns, act, result, gathered,
    forth_send, forth_recv, back_send, back_recv, weight_send, weight_recv, local,
):
    at = place()
    me = lax.axis_index("exp")
    other = meet_experts(at)
    near, far = load_experts(own, across, weights, (weight_send, weight_recv), local, other)
    for copy in near:
        copy.start()
    count = hidden.shape[0]
    slot = iota((TOTAL, count), 0)
    placing = ((slot == target_row[0:1, :]) | (slot == target_row[1:2, :])).astype(jnp.bfloat16)
    placed = plain_dot(placing, hidden[...])
    pack(sends, placed[:MAIN], placed[MAIN:])
    met_experts()
    deal(sends, lands, (forth_send, forth_recv), True, 1, GROUP, start_copy)
    for copy in far:
        copy.start()
    keep = pltpu.make_async_copy(sends.at[me], lands.at[0], local.at[2])
    keep.start()
    keep.wait()
    deal(sends, lands, (forth_send, forth_recv), True, 1, GROUP // 2, wait_recv)
    for copy in near:
        copy.wait()
    for half in range(2):
        if half == 1:
            deal(sends, lands, (forth_send, forth_recv), True, GROUP // 2, GROUP, wait_recv)
        sources = pl.ds(half * (GROUP // 2), GROUP // 2)
        first, first_tail = half * (MAIN // 2), MAIN + half * (TOTAL - MAIN) // 2
        unpack(lands.at[sources], rows, first, first_tail)
        if half == 0:
            for copy in far:
                copy.wait_recv()
        given = halves(rows, half)

        def hidden_units(index, carry):
            quarter, part = lax.div(index, 3), lax.rem(index, 3)
            columns = pl.ds(pl.multiple_of(part * 256, 256), 256)
            value = plain_dot(given, weights[quarter, 0, :, columns])
            act[quarter, :, columns] = (0.5 * value * (1.0 + gelu_tanh(value))).astype(jnp.bfloat16)
            return carry

        lax.fori_loop(0, 12, hidden_units, 0)

        def outputs(index, carry):
            columns = pl.ds(pl.multiple_of(index * 256, 256), 256)
            value = over_last(act[0], weights[0, 1, columns, :])
            for quarter in range(1, 4):
                value = value + over_last(act[quarter], weights[quarter, 1, columns, :])
            result[:, columns] = value
            return carry

        lax.fori_loop(0, 3, outputs, 0)
        pack(backs.at[sources], result[: MAIN // 2, :], result[MAIN // 2 :, :])
        deal(backs, returns, (back_send, back_recv), False, max(1, half * (GROUP // 2)), (half + 1) * (GROUP // 2), start_copy)
    keep = pltpu.make_async_copy(backs.at[0], returns.at[me], local.at[2])
    keep.start()
    keep.wait()
    deal(backs, returns, (back_send, back_recv), False, 1, GROUP, wait_recv)
    unpack(returns, gathered, 0, MAIN)
    slot = iota((count, TOTAL), 1)
    for k in range(2):
        placing = (slot == target_column[:, k : k + 1]).astype(jnp.bfloat16)
        chosen[k] = plain_dot(placing, gathered[...]).astype(jnp.bfloat16)

    def final_norm(index, carry):
        part = pl.ds(pl.multiple_of(index * CHUNK, CHUNK), CHUNK)
        value = after[part, :] + (
            gates[part, 0:1] * chosen[0, part, :].astype(jnp.float32)
            + gates[part, 1:2] * chosen[1, part, :].astype(jnp.float32)
        )
        total[part, :] = value
        normed, _ = centre(value)
        return carry + jnp.sum(normed * vec[8:9, :] + vec[9:10, :], axis=0, keepdims=True)

    summed = lax.fori_loop(0, count // CHUNK, final_norm, jnp.zeros((1, D), jnp.float32)) / PATCHES
    pool[...] = jnp.zeros_like(pool)
    for tile in range(D // LANES):
        pool[tile : tile + 1, :] = summed[:, tile * LANES : (tile + 1) * LANES]
    deal(sends, lands, (forth_send, forth_recv), True, 1, GROUP, wait_send)
    deal(backs, returns, (back_send, back_recv), False, 1, GROUP, wait_send)
    for copy in far:
        copy.wait_send()


def experts_forward(*operands):
    count = operands[0].shape[0]
    low, wide = jnp.bfloat16, jnp.float32
    wire = pltpu.VMEM((GROUP, SLOTS, WIRE), low)
    shapes = [((TOTAL, D), low), ((2, count, D), low), ((count, D), wide), ((PAD, LANES), wide)]
    sems = pltpu.SemaphoreType.DMA((GROUP,))
    return pl.pallas_call(
        experts_kernel,
        out_shape=[jax.ShapeDtypeStruct(*shape) for shape in shapes],
        in_specs=[pl.BlockSpec(memory_space=pltpu.VMEM)] * 6 + [pl.BlockSpec(memory_space=pl.ANY)] * 2,
        out_specs=[pl.BlockSpec(memory_space=pltpu.VMEM)] * 4,
        scratch_shapes=[pltpu.VMEM((4, 2, D, D), low)]
        + [wire] * 4
        + [pltpu.VMEM((4, HALF, D), low), pltpu.VMEM((HALF, D), wide), pltpu.VMEM((TOTAL, D), low)]
        + [sems] * 4
        + [pltpu.SemaphoreType.DMA((2,))] * 2
        + [pltpu.SemaphoreType.DMA((3,))],
        compiler_params=pltpu.CompilerParams(
            collective_id=5, has_side_effects=True, vmem_limit_bytes=48 * 2**20
        ),
        name="experts_forward",
    )(*operands)


def experts_back_kernel(
    row_grad, total, chosen, gates, gate_probs, ids, rows, target_row, target_column, vec, own, across,
    dtotal, dgate, sums, dhidden, to_y, kept,
    weights, sends, lands, backs, returns, act, slope, dpre, drows, result, dreturned, rows_t, drows_t, outward,
    forth_send, forth_recv, back_send, back_recv, weight_send, weight_recv, grad_send, grad_recv, local, ready,
):
    at = place()
    me = lax.axis_index("exp")
    other = meet_experts(at)
    near, far = load_experts(own, across, weights, (weight_send, weight_recv), local, other)
    for copy in near:
        copy.start()
    count = total.shape[0]
    grad = jnp.concatenate([row_grad[tile : tile + 1, :] for tile in range(D // LANES)], axis=1) / PATCHES
    zero = jnp.zeros((1, D), jnp.float32)

    def final_norm(index, carry):
        part = pl.ds(pl.multiple_of(index * CHUNK, CHUNK), CHUNK)
        back, gain, shift = norm_back(total[part, :], jnp.broadcast_to(grad, (CHUNK, D)), vec[8:9, :])
        dtotal[part, :] = back
        dgates = [
            jnp.sum(back * chosen[k, part, :].astype(jnp.float32), axis=-1, keepdims=True) for k in range(2)
        ]
        for k in range(2):
            outward[k, part, :] = (gates[part, k : k + 1] * back).astype(jnp.bfloat16)
        lane = iota((CHUNK, LANES), 1)
        probs = gate_probs[part, :]
        dprobs = jnp.where(lane == ids[part, 0:1], dgates[0], 0.0) + jnp.where(
            lane == ids[part, 1:2], dgates[1], 0.0
        )
        inner = dprobs - jnp.sum(probs * dprobs, axis=-1, keepdims=True)
        dgate[part, :] = (probs * inner).astype(jnp.bfloat16)
        return carry[0] + gain, carry[1] + shift

    gain, shift = lax.fori_loop(0, count // CHUNK, final_norm, (zero, zero))
    sums[0:1, :] = gain
    sums[1:2, :] = shift
    slot = iota((TOTAL, count), 0)
    placed = [
        plain_dot((slot == target_row[k : k + 1, :]).astype(jnp.bfloat16), outward[k]) for k in range(2)
    ]
    placed = placed[0] + placed[1]
    pack(sends, placed[:MAIN], placed[MAIN:])
    met_experts()
    deal(sends, lands, (forth_send, forth_recv), True, 1, GROUP, start_copy)
    for copy in far:
        copy.start()
    keep = pltpu.make_async_copy(sends.at[me], lands.at[0], local.at[2])
    keep.start()
    keep.wait()
    for copy in near:
        copy.wait()

    def hidden_units(index, carry):
        quarter, rest = lax.div(index, 6), lax.rem(index, 6)
        half, part = lax.div(rest, 3), lax.rem(rest, 3)
        columns = pl.ds(pl.multiple_of(part * 256, 256), 256)
        lines = pl.ds(pl.multiple_of(half * HALF, HALF), HALF)
        value = plain_dot(rows[lines, :], weights[quarter, 0, :, columns])
        tanh = gelu_tanh(value)
        act[quarter, lines, columns] = (0.5 * value * (1.0 + tanh)).astype(jnp.bfloat16)
        slope[quarter, lines, columns] = 0.5 * (1.0 + tanh) + 0.5 * value * (1.0 - tanh * tanh) * (
            GELU_SCALE * (1.0 + 3 * 0.044715 * (value * value))
        )
        return carry

    lax.fori_loop(0, 12, hidden_units, 0)
    for copy in far:
        copy.wait_recv()
    lax.fori_loop(12, 24, hidden_units, 0)
    rows_t[...] = rows[...].T
    deal(sends, lands, (forth_send, forth_recv), True, 1, GROUP, wait_recv)
    unpack(lands, drows, 0, MAIN)

    def hidden_back(index, carry):
        quarter, rest = lax.div(index, 6), lax.rem(index, 6)
        half, part = lax.div(rest, 3), lax.rem(rest, 3)
        columns = pl.ds(pl.multiple_of(part * 256, 256), 256)
        lines = pl.ds(pl.multiple_of(half * HALF, HALF), HALF)
        value = plain_dot(drows[lines, :], weights[quarter, 1, :, columns])
        dpre[quarter, lines, columns] = (value * slope[quarter, lines, columns]).astype(jnp.bfloat16)
        return carry

    lax.fori_loop(0, 24, hidden_back, 0)

    def inputs_back(index, carry):
        half, part = lax.div(index, 3), lax.rem(index, 3)
        columns = pl.ds(pl.multiple_of(part * 256, 256), 256)
        lines = pl.ds(pl.multiple_of(half * HALF, HALF), HALF)
        value = over_last(dpre[0, lines, :], weights[0, 0, columns, :])
        for quarter in range(1, 4):
            value = value + over_last(dpre[quarter, lines, :], weights[quarter, 0, columns, :])
        result[lines, columns] = value
        return carry

    lax.fori_loop(0, 6, inputs_back, 0)
    pl.semaphore_signal(ready, inc=1, device_id=device(other), device_id_type=MESH)
    pack(backs, result[:MAIN, :], result[MAIN:, :])
    deal(backs, returns, (back_send, back_recv), False, 1, GROUP, start_copy)
    keep = pltpu.make_async_copy(backs.at[0], returns.at[me], local.at[2])
    keep.start()
    drows_t[...] = drows[...].T

    def gradient(quarter, which, columns):
        if which == 0:
            return plain_dot(rows_t[...], dpre[quarter, :, columns])
        return plain_dot(drows_t[...], act[quarter, :, columns])

    def far_grads(index, carry):
        quarter, part = lax.div(index, 3) + 2, lax.rem(index, 3)
        columns = pl.ds(pl.multiple_of(part * 256, 256), 256)
        for which in range(2):
            weights[quarter, which, :, columns] = gradient(quarter, which, columns).astype(jnp.bfloat16)
        return carry

    for copy in far:
        copy.wait_send()
    lax.fori_loop(0, 6, far_grads, 0)
    pl.semaphore_wait(ready, 1)
    swaps = [remote(weights.at[2 + k], weights.at[k], (grad_send, grad_recv), k, other) for k in range(2)]
    for swap in swaps:
        swap.start()

    def kept_grads(index, carry):
        columns = pl.ds(pl.multiple_of(index * 256, 256), 256)
        for which in range(2):
            kept[which, :, columns] = gradient(0, which, columns)
        return carry

    lax.fori_loop(0, 3, kept_grads, 0)
    keep.wait()
    deal(backs, returns, (back_send, back_recv), False, 1, GROUP, wait_recv)
    unpack(returns, dreturned, 0, MAIN)
    slot = iota((count, TOTAL), 1)
    placing = (slot == target_column[:, 0:1]) | (slot == target_column[:, 1:2])
    dhidden[...] = plain_dot(placing.astype(jnp.bfloat16), dreturned[...])
    for swap in swaps:
        swap.wait_recv()

    def sent_grads(index, carry):
        columns = pl.ds(pl.multiple_of(index * 256, 256), 256)
        for which in range(2):
            value = gradient(1, which, columns) + weights[1, which, :, columns].astype(jnp.float32)
            to_y[which, :, columns] = value.astype(jnp.bfloat16)
            kept[which, :, columns] = kept[which, :, columns] + weights[0, which, :, columns].astype(
                jnp.float32
            )
        return carry

    lax.fori_loop(0, 3, sent_grads, 0)
    deal(sends, lands, (forth_send, forth_recv), True, 1, GROUP, wait_send)
    deal(backs, returns, (back_send, back_recv), False, 1, GROUP, wait_send)
    for swap in swaps:
        swap.wait_send()


def experts_backward(*operands):
    count = operands[1].shape[0]
    low, wide = jnp.bfloat16, jnp.float32
    wire = pltpu.VMEM((GROUP, SLOTS, WIRE), low)
    shapes = [
        ((count, D), wide), ((count, LANES), low), ((PAD, D), wide),
        ((count, D), wide), ((2, D, D), low), ((2, D, D), wide),
    ]
    sems = pltpu.SemaphoreType.DMA((GROUP,))
    return pl.pallas_call(
        experts_back_kernel,
        out_shape=[jax.ShapeDtypeStruct(*shape) for shape in shapes],
        in_specs=[pl.BlockSpec(memory_space=pltpu.VMEM)] * 10 + [pl.BlockSpec(memory_space=pl.ANY)] * 2,
        out_specs=[pl.BlockSpec(memory_space=pltpu.VMEM)] * 6,
        scratch_shapes=[pltpu.VMEM((4, 2, D, D), low)]
        + [wire] * 4
        + [pltpu.VMEM((4, TOTAL, D), low), pltpu.VMEM((4, TOTAL, D), wide), pltpu.VMEM((4, TOTAL, D), low)]
        + [pltpu.VMEM((TOTAL, D), low), pltpu.VMEM((TOTAL, D), wide), pltpu.VMEM((TOTAL, D), low)]
        + [pltpu.VMEM((D, TOTAL), low)] * 2
        + [pltpu.VMEM((2, count, D), low)]
        + [sems] * 4
        + [pltpu.SemaphoreType.DMA((2,))] * 4
        + [pltpu.SemaphoreType.DMA((3,)), pltpu.SemaphoreType.REGULAR],
        compiler_params=pltpu.CompilerParams(
            collective_id=8, has_side_effects=True, vmem_limit_bytes=58 * 2**20
        ),
        name="experts_backward",
    )(*operands)


NEAR = tuple((y, core) for y in range(4) for core in range(2) if y or core)
PLANE = tuple((x, z) for x in range(4) for z in range(4) if x or z)


def near_peer(at, by):
    return moved(moved(at, "y", by[0]), "core", by[1])


def plane_peer(at, by):
    return moved(moved(at, "x", by[0]), "z", by[1])


def greet_all(at):
    barrier = pltpu.get_barrier_semaphore()
    peers = [near_peer(at, by) for by in NEAR] + [plane_peer(at, by) for by in PLANE]
    for peer in peers:
        pl.semaphore_signal(barrier, inc=1, device_id=device(peer), device_id_type=MESH)
    pl.semaphore_wait(barrier, len(peers))


def send_near(at, source, target, sems, first):
    copies = []
    for index, by in enumerate(NEAR):
        peer = near_peer(at, by)
        copies.append(remote(source(peer), target.at[at["y"], at["core"]], sems, first + index, peer))
        copies[-1].start()
    return copies


def send_plane(at, source, target, sems, first):
    copies = []
    for index, by in enumerate(PLANE):
        peer = plane_peer(at, by)
        copies.append(remote(source(peer), target.at[at["x"], at["z"]], sems, first + index, peer))
        copies[-1].start()
    return copies


def head_kernel(
    pool, head, targets, valid, count,
    row_grad, head_grad, loss,
    near, every, pooled, pulls, got, summed, last, send, recv,
):
    at = place()
    sems = (send, recv)
    greet_all(at)
    copies = send_near(at, lambda peer: pool, near, sems, 0)
    near[at["y"], at["core"]] = pool[...]
    for copy in copies:
        copy.wait()
    rows = near[:, 0] + near[:, 1]
    every[at["x"], at["z"]] = rows.astype(jnp.bfloat16).astype(jnp.float32)
    mine = every.at[at["x"], at["z"]]
    for copy in send_plane(at, lambda peer: mine, every, sems, 7):
        copy.wait()
    images = pooled.shape[0]
    for tile in range(D // LANES):
        lanes = slice(tile * LANES, (tile + 1) * LANES)
        pooled[:, lanes] = every[:, :, :, tile, :].reshape(images, LANES).astype(jnp.bfloat16)
    logits = plain_dot(pooled[...], head[...])
    soft = jnp.maximum(logits, 0.0) + jnp.log1p(jnp.exp(-jnp.abs(logits)))
    inside = iota(logits.shape, 1) < VOCAB_DEV
    terms = jnp.where(inside, valid[...] * (soft - targets[...] * logits), 0.0)
    loss[...] = jnp.sum(jnp.sum(terms, axis=1, keepdims=True), axis=0, keepdims=True)
    sigmoid = 1.0 / (1.0 + jnp.exp(-logits))
    down = jnp.where(inside, valid[...] * (sigmoid - targets[...]) / count[...], 0.0).astype(jnp.bfloat16)
    back = over_last(down, head[...])
    pulls[...] = jnp.zeros_like(pulls)
    for tile in range(D // LANES):
        lanes = slice(tile * LANES, (tile + 1) * LANES)
        pulls[:, :, :, tile, :] = back[:, lanes].reshape(4, 4, 4, LANES)
    copies = send_plane(at, lambda peer: pulls.at[peer["x"], peer["z"]], got, sems, 22)
    got[at["x"], at["z"]] = pulls[at["x"], at["z"]]
    head_grad[...] = plain_dot(pooled[...].T, down)
    for copy in copies:
        copy.wait()
    summed[...] = jnp.sum(got[...].reshape((16,) + summed.shape), axis=0)
    copies = send_near(at, lambda peer: summed.at[peer["y"]], last, sems, 37)
    last[at["y"], at["core"]] = summed[at["y"]]
    for copy in copies:
        copy.wait()
    row_grad[...] = jnp.sum(last[...].reshape((8,) + row_grad.shape), axis=0)


def head_step(pool, head, targets, valid, count):
    images, classes = targets.shape
    wide = jnp.float32
    block = (PAD, LANES)
    return pl.pallas_call(
        head_kernel,
        out_shape=[
            jax.ShapeDtypeStruct(block, wide),
            jax.ShapeDtypeStruct((D, classes), wide),
            jax.ShapeDtypeStruct((1, 1), wide),
        ],
        in_specs=[pl.BlockSpec(memory_space=pltpu.VMEM)] * 5,
        out_specs=[pl.BlockSpec(memory_space=pltpu.VMEM)] * 3,
        scratch_shapes=[
            pltpu.VMEM((4, 2) + block, wide),
            pltpu.VMEM((4, 4, 4) + block, wide),
            pltpu.VMEM((images, D), jnp.bfloat16),
            pltpu.VMEM((4, 4, 4) + block, wide),
            pltpu.VMEM((4, 4, 4) + block, wide),
            pltpu.VMEM((4,) + block, wide),
            pltpu.VMEM((4, 2) + block, wide),
            pltpu.SemaphoreType.DMA((44,)),
            pltpu.SemaphoreType.DMA((44,)),
        ],
        compiler_params=pltpu.CompilerParams(collective_id=2, has_side_effects=True),
        name="head_step",
    )(pool, head, targets, valid, count)


def total_kernel(x_ref, o_ref, near, every, summed, send, recv):
    at = place()
    sems = (send, recv)
    greet_all(at)
    copies = send_near(at, lambda peer: x_ref, near, sems, 0)
    near[at["y"], at["core"]] = x_ref[...]
    for copy in copies:
        copy.wait()
    summed[...] = jnp.sum(near[...].reshape((8,) + summed.shape), axis=0)
    copies = send_plane(at, lambda peer: summed, every, sems, 7)
    every[at["x"], at["z"]] = summed[...]
    for copy in copies:
        copy.wait()
    o_ref[...] = jnp.sum(every[...].reshape((16,) + summed.shape), axis=0)


def total_all(value):
    return pl.pallas_call(
        total_kernel,
        out_shape=jax.ShapeDtypeStruct(value.shape, value.dtype),
        in_specs=[pl.BlockSpec(memory_space=pltpu.VMEM)],
        out_specs=pl.BlockSpec(memory_space=pltpu.VMEM),
        scratch_shapes=[
            pltpu.VMEM((4, 2) + value.shape, value.dtype),
            pltpu.VMEM((4, 4) + value.shape, value.dtype),
            pltpu.VMEM(value.shape, value.dtype),
            pltpu.SemaphoreType.DMA((22,)),
            pltpu.SemaphoreType.DMA((22,)),
        ],
        compiler_params=pltpu.CompilerParams(collective_id=4, has_side_effects=True),
        name="total_all",
    )(value)


def across_cores(value):
    return lax.ppermute(value, "rep", CORE_SWAP)


def across_y(value):
    return lax.ppermute(value, "rep", Y_SWAP)


def shards(
    patches,
    expert_ids,
    labels,
    label_count,
    square_weights,
    router_weight,
    position_table,
    head_weight,
    expert_weights,
    vector_params,
    square_rows,
    square_cols,
    router_rows,
    router_cols,
    position_rows,
    position_cols,
    head_rows,
    head_cols,
    expert_rows,
    expert_cols,
    vector_moment,
):
    bfloat = jnp.bfloat16
    num_rep = lax.axis_size("rep")
    num_exp = lax.axis_size("exp")
    rep_index = lax.axis_index("rep")
    my_image = lax.axis_index("exp")
    device_index = lax.axis_index(("rep", "exp"))
    micro, core = rep_index // 2, rep_index % 2
    num_expert = router_weight.shape[1]
    vocab_dev = head_weight.shape[1]
    ff_dev = expert_weights.shape[3]
    block = patches.shape[2]
    rows, width = 2 * block, patches.shape[3]
    num_top = expert_ids.shape[3]
    heads = width // HEAD
    scale = HEAD ** (-0.5)
    own_rows = square_weights.shape[1]

    def pad_rows(value):
        return jnp.pad(value, ((0, PAD - own_rows), (0, width - value.shape[1])))

    mine = lax.dynamic_index_in_dim(patches, micro, 0, keepdims=False)[0]
    theirs = across_y(lax.dynamic_index_in_dim(patches, 1 - micro, 0, keepdims=False)[0])
    patch_rows = jnp.where(
        micro == 0, jnp.concatenate([mine, theirs]), jnp.concatenate([theirs, mine])
    )
    mine = lax.dynamic_index_in_dim(expert_ids, micro, 0, keepdims=False)[0]
    theirs = across_y(lax.dynamic_index_in_dim(expert_ids, 1 - micro, 0, keepdims=False)[0])
    ids = jnp.where(micro == 0, jnp.concatenate([mine, theirs]), jnp.concatenate([theirs, mine]))

    table_t = position_table.T
    table_high = lax.reduce_precision(table_t, 8, 7)
    table_low = (table_t - table_high).astype(bfloat)
    vector_t = vector_params.T
    vector_high = lax.reduce_precision(vector_t, 8, 7)
    vector_low = (vector_t - vector_high).astype(bfloat)
    extra = jnp.concatenate(
        [table_high.astype(bfloat), router_weight.astype(bfloat), vector_high.astype(bfloat), vector_low],
        axis=1,
    )
    square_low = square_weights.astype(bfloat)
    spare = jnp.pad(table_low, ((0, 0), (0, width - PATCHES))).reshape(3, 2, width)
    payload = jnp.concatenate(
        [square_low[0], spare[0], square_low[1], spare[1], square_low[2], spare[2]]
        + [pad_rows(square_low[3]), pad_rows(square_low[4]), pad_rows(extra)],
        axis=0,
    ).reshape(3, 16, width)
    *squares, extra, low = gather_all(payload)

    quarter = lax.optimization_barrier((expert_weights, extra))[0][0].astype(bfloat)
    quarter_y = across_y(quarter)
    table = (
        extra[:, :PATCHES].astype(jnp.float32) + low[:, :PATCHES].astype(jnp.float32)
    ).T
    router = extra[:, PATCHES : PATCHES + num_expert]
    begin = PATCHES + num_expert
    vectors = (
        extra[:, begin : begin + 10].astype(jnp.float32)
        + extra[:, begin + 10 : begin + 20].astype(jnp.float32)
    ).T
    table_rows = jnp.concatenate(
        [
            lax.dynamic_slice_in_dim(table, core * block, block, 0),
            lax.dynamic_slice_in_dim(table, (2 + core) * block, block, 0),
        ]
    )
    head_low = head_weight.astype(bfloat)
    valid = (label_count > 0).astype(jnp.float32)
    image_count = jnp.sum(valid)
    expert_range = jnp.arange(num_expert, dtype=jnp.int32)
    label_range = jnp.arange(labels.shape[2], dtype=jnp.int32)

    flat_hit = ids[:, :, None] == expert_range[None, None, :]
    flat_hit = flat_hit.reshape(2, block * num_top, num_expert).astype(jnp.int32)
    before = jnp.cumsum(flat_hit, axis=1) - flat_hit
    slot = jnp.sum(before * flat_hit, axis=2) + jnp.array([[0], [CAP]], jnp.int32)
    slot = slot.reshape(rows, num_top)
    target = jnp.where(slot < SLOTS, ids * SLOTS + slot, MAIN + ids * TAIL + slot - SLOTS)
    target_t = target.T

    def by_place(value):
        return value.reshape(2, 4, 2, 4, -1).transpose(1, 3, 0, 2, 4).reshape(2 * num_exp, -1)

    label_rows, count_rows = by_place(labels), by_place(label_count)
    live = label_range[None, :] < count_rows
    head_cols_pad = -(-vocab_dev // LANES) * LANES
    columns = device_index * vocab_dev + jnp.arange(head_cols_pad, dtype=jnp.int32)
    targets = jnp.any(
        (label_rows[:, :, None] == columns[None, None, :]) & live[:, :, None], axis=1
    ).astype(jnp.float32)
    valid_rows = (count_rows > 0).astype(jnp.float32)
    head_low = jnp.pad(head_low, ((0, 0), (0, head_cols_pad - vocab_dev)))

    slot_index = jnp.arange(num_exp * 4 * PAD, dtype=jnp.int32)

    def picker(which, offset):
        first = (slot_index // (num_exp * 2 * PAD)) * (2 * num_exp) + which * num_exp
        owner = first + (slot_index % (num_exp * 2 * PAD)) // (2 * PAD)
        inside = slot_index % (2 * PAD) - offset
        row = jnp.where((inside >= 0) & (inside < own_rows), owner * own_rows + inside, -1)
        return (jnp.arange(width, dtype=jnp.int32)[:, None] == row[None, :]).astype(bfloat)

    picks = {offset: (picker(core, offset), picker(1 - core, offset)) for offset in (0, PAD)}

    def share_left(value, offset):
        mine, theirs = (plain_dot(value, pick).astype(bfloat) for pick in picks[offset])
        return jnp.concatenate([mine, across_cores(theirs)])

    def share_right(value):
        return jnp.concatenate([value, across_cores(value)])

    left_patches = share_left(patch_rows, 0)
    vectors = jnp.pad(vectors, ((0, 6), (0, 0)))
    router = jnp.pad(router, ((0, 0), (0, LANES - num_expert)))
    embed, hidden_one, query, keys, values, mixed, after_attn, hidden_two, gate_probs, gates, lse = attend(
        patch_rows, squares, vectors, table_rows, router, ids
    )
    quarter_y, hidden_two = lax.optimization_barrier((quarter_y, hidden_two))
    received, chosen, after_moe, pool = experts_forward(
        hidden_two, target_t, target, gates, after_attn, vectors, quarter, quarter_y
    )
    row_grad, head_g, loss_part = head_step(
        pool, head_low, targets, valid_rows, image_count.reshape(1, 1)
    )
    head_g = head_g[:, :vocab_dev]
    loss_part = loss_part[0, 0]
    dmoe_in, dgate_logits, final_sums, dhidden, to_y, expert_g = experts_backward(
        row_grad, after_moe, chosen, gates, gate_probs, ids, received, target_t, target, vectors, quarter, quarter_y
    )
    from_y = across_y(to_y)
    left_one = [share_left(hidden_one, offset) for offset in (0, PAD)]
    left_mixed = share_left(mixed, 0)
    router_grad = over_rows(hidden_two, dgate_logits)[:, :num_expert]
    dafter_low, dquery_low, dkey_low, dvalue_low, dembed_low, sums = attend_back(
        dmoe_in,
        dhidden,
        dgate_logits,
        embed,
        after_attn,
        hidden_one,
        query,
        keys,
        values,
        lse,
        *squares[1:],
        vectors,
        router,
    )
    right_after = share_right(dafter_low)
    right_query, right_key, right_value = (
        share_right(value) for value in (dquery_low, dkey_low, dvalue_low)
    )
    right_embed = share_right(dembed_low)

    vector_grad = jnp.concatenate([sums, final_sums[:2]])
    few = jnp.concatenate([vector_grad, router_grad.T], axis=0)
    few = few + across_cores(few)
    count = few.shape[0]
    few_high = lax.reduce_precision(few, 8, 7)
    embed_all = jnp.where(
        core == 0, right_embed, jnp.concatenate([right_embed[rows:], right_embed[:rows]])
    )
    extra_right = jnp.concatenate(
        [embed_all, few_high.astype(bfloat), (few - few_high).astype(bfloat)]
        + [jnp.zeros((width - PATCHES - 2 * count, width), bfloat)],
        axis=0,
    ).T
    def pair(lefts, rights):
        total = over_rows(jnp.concatenate(lefts), jnp.concatenate(rights))
        return total.astype(bfloat).reshape(2, 4, 2, 4, 2 * PAD, width)

    owned = scatter_all(
        [
            pair([left_patches, left_one[1]], [right_embed, right_query]),
            pair([left_one[0], left_one[1]], [right_key, right_value]),
            pair([left_mixed, picks[PAD][0]], [right_after, extra_right]),
        ]
    )
    owned = [half for part in owned for half in (part[:own_rows], part[PAD : PAD + own_rows])]
    owned, from_y = lax.optimization_barrier((owned, from_y))
    expert_g = (expert_g + from_y.astype(jnp.float32))[None]
    square_g = jnp.stack(owned[:5])
    extra_g = owned[5]
    table_g = extra_g[:, :PATCHES].reshape(own_rows, 2, 2, block)
    table_g = table_g.transpose(0, 2, 1, 3).reshape(own_rows, PATCHES).T
    few_g = extra_g[:, PATCHES : PATCHES + count] + extra_g[:, PATCHES + count : PATCHES + 2 * count]
    vector_g = few_g[:, :10].T
    router_g = few_g[:, 10:]
    norm_part = (
        jnp.sum(square_g * square_g)
        + jnp.sum(router_g * router_g)
        + jnp.sum(table_g * table_g)
        + jnp.sum(vector_g * vector_g)
        + jnp.sum(head_g * head_g)
        + jnp.sum(expert_g * expert_g)
    )
    square_rowmean = jnp.mean(square_g * square_g, axis=2)
    router_rowmean = jnp.mean(router_g * router_g, axis=1)
    expert_rowsq = jnp.sum(expert_g * expert_g, axis=-1)
    expert_rowsq = expert_rowsq + across_cores(expert_rowsq)
    expert_mine = expert_rowsq + across_y(expert_rowsq)
    terms = (
        loss_part,
        norm_part,
        jnp.sum(square_g * square_g, axis=1),
        jnp.sum(square_rows, axis=1),
        jnp.sum(square_rowmean, axis=1),
        jnp.sum(router_g * router_g, axis=0),
        jnp.sum(router_rows),
        jnp.sum(router_rowmean),
        jnp.sum(table_g * table_g, axis=1),
        jnp.sum(head_g * head_g, axis=1),
    )
    flat = jnp.concatenate([term.reshape(-1) for term in terms])
    length = flat.shape[0]
    padded = -(-length // (8 * LANES)) * 8 * LANES
    flat = total_all(jnp.pad(flat, (0, padded - length)).reshape(-1, LANES)).reshape(-1)
    totals = []
    begin = 0
    for term in terms:
        totals.append(flat[begin : begin + term.size].reshape(term.shape))
        begin += term.size
    (
        loss_total,
        norm_total,
        square_colsq,
        square_rows_sum,
        square_mean_sum,
        router_colsq,
        router_rows_sum,
        router_mean_sum,
        table_rowsq,
        head_rowsq,
    ) = totals
    grad_norm = jnp.sqrt(norm_total)
    clip = jnp.minimum(1.0, CLIP_NORM / grad_norm)
    clip_sq = clip * clip
    keep = 1.0 - DECAY
    square_clip = clip * square_g
    square_rows_next = DECAY * square_rows + keep * (clip_sq * square_rowmean + EPS_SQ)
    square_cols_next = DECAY * square_cols + keep * (clip_sq * square_colsq / width + EPS_SQ)
    square_mean = (
        DECAY * square_rows_sum + keep * (clip_sq * square_mean_sum + width * EPS_SQ)
    ) / width
    square_rate = jnp.array([1.0, 1.0, 1.0, 1.0, 4.0], jnp.float32)[:, None, None] * (
        0.3 / math.sqrt(D)
    )
    square_next = factored_step(
        square_weights,
        square_clip,
        square_rows_next,
        square_cols_next,
        square_mean[:, None, None],
        square_rate,
    )
    router_clip = clip * router_g
    router_rows_next = DECAY * router_rows + keep * (clip_sq * router_rowmean + EPS_SQ)
    router_cols_next = DECAY * router_cols + keep * (clip_sq * router_colsq / width + EPS_SQ)
    router_mean = (
        DECAY * router_rows_sum + keep * (clip_sq * router_mean_sum + width * EPS_SQ)
    ) / width
    router_next = factored_step(
        router_weight,
        router_clip,
        router_rows_next,
        router_cols_next,
        router_mean,
        0.2 / math.sqrt(D),
    )
    table_clip = clip * table_g
    table_rows_next = DECAY * position_rows + keep * (clip_sq * table_rowsq / width + EPS_SQ)
    table_cols_next = DECAY * position_cols + keep * (
        clip_sq * jnp.mean(table_g * table_g, axis=0) + EPS_SQ
    )
    table_next = factored_step(
        position_table,
        table_clip,
        table_rows_next,
        table_cols_next,
        jnp.mean(table_rows_next),
        0.15,
    )
    head_clip = clip * head_g
    head_rows_next = DECAY * head_rows + keep * (
        clip_sq * head_rowsq / (vocab_dev * num_rep * num_exp) + EPS_SQ
    )
    head_cols_next = DECAY * head_cols + keep * (
        clip_sq * jnp.mean(head_g * head_g, axis=0) + EPS_SQ
    )
    head_next = factored_step(
        head_weight,
        head_clip,
        head_rows_next,
        head_cols_next,
        jnp.mean(head_rows_next),
        0.5 / math.sqrt(D),
    )
    expert_clip = clip * expert_g
    expert_rows_next = DECAY * expert_rows + keep * (
        clip_sq * expert_mine / (ff_dev * num_rep) + EPS_SQ
    )
    expert_cols_next = DECAY * expert_cols + keep * (
        clip_sq * jnp.mean(expert_g * expert_g, axis=2) + EPS_SQ
    )
    expert_rate = jnp.array([0.3 / math.sqrt(D), 4.8 / math.sqrt(FF)], jnp.float32)[
        None, :, None, None
    ]
    expert_next = factored_step(
        expert_weights,
        expert_clip,
        expert_rows_next,
        expert_cols_next,
        jnp.mean(expert_rows_next, axis=-1)[..., None, None],
        expert_rate,
    )
    vector_clip = clip * vector_g
    moment_next = DECAY * vector_moment + keep * (vector_clip * vector_clip + EPS_SQ)
    vector_next = vector_params - 0.3 * vector_clip * lax.rsqrt(moment_next)
    return (
        loss_total,
        image_count,
        grad_norm,
        square_clip,
        square_rows_next,
        square_cols_next,
        square_next,
        router_clip,
        router_rows_next,
        router_cols_next,
        router_next,
        table_clip,
        table_rows_next,
        table_cols_next,
        table_next,
        head_clip,
        head_rows_next,
        head_cols_next,
        head_next,
        expert_clip,
        expert_rows_next,
        expert_cols_next,
        expert_next,
        vector_clip,
        moment_next,
        vector_next,
    )


def solution(mesh):
    in_specs = (
        P(None, "exp", "rep", None),
        P(None, "exp", "rep", None),
        P(),
        P(),
        P(None, ("rep", "exp"), None),
        P(("rep", "exp"), None),
        P(None, ("rep", "exp")),
        P(None, ("rep", "exp")),
        P("exp", None, None, "rep"),
        P(None, ("rep", "exp")),
        P(None, ("rep", "exp")),
        P(),
        P(("rep", "exp")),
        P(),
        P(),
        P(("rep", "exp")),
        P(),
        P(("rep", "exp")),
        P("exp", None, None),
        P("exp", None, "rep"),
        P(None, ("rep", "exp")),
    )
    out_specs = (
        P(),
        P(),
        P(),
        P(None, ("rep", "exp"), None),
        P(None, ("rep", "exp")),
        P(),
        P(None, ("rep", "exp"), None),
        P(("rep", "exp"), None),
        P(("rep", "exp")),
        P(),
        P(("rep", "exp"), None),
        P(None, ("rep", "exp")),
        P(),
        P(("rep", "exp")),
        P(None, ("rep", "exp")),
        P(None, ("rep", "exp")),
        P(),
        P(("rep", "exp")),
        P(None, ("rep", "exp")),
        P("exp", None, None, "rep"),
        P("exp", None, None),
        P("exp", None, "rep"),
        P("exp", None, None, "rep"),
        P(None, ("rep", "exp")),
        P(None, ("rep", "exp")),
        P(None, ("rep", "exp")),
    )
    return jax.shard_map(shards, mesh=mesh, in_specs=in_specs, out_specs=out_specs, check_vma=False)
```

```python
import functools
import math

import jax
import jax.numpy as jnp
from jax import lax
from jax.experimental import pallas as pl
from jax.experimental.pallas import tpu as pltpu
from jax.sharding import PartitionSpec as P

D = 768
HEAD = 64
FF = 3072
PATCHES = 576
CAP = 10
VOCAB_DEV = 171
EXTRA = 640
VECTOR_AT = 608
ROUTER_AT = 64
PAD = 8
LANES = 128


DECAY = 0.8
EPS_SQ = 1e-30
CLIP_NORM = 0.25
HIGHEST = lax.Precision.HIGHEST
MESH = pl.DeviceIdType.MESH

Y_SWAP = ((0, 2), (1, 3), (2, 0), (3, 1))
CORE_SWAP = ((0, 1), (1, 0), (2, 3), (3, 2))


def layer_norm(value, gain, shift):
    centred = value - jnp.mean(value, axis=-1, keepdims=True)
    spread = jnp.mean(centred * centred, axis=-1, keepdims=True)
    return centred * lax.rsqrt(spread + 1e-06) * gain + shift


def plain_dot(left, right):
    return jnp.dot(left, right, preferred_element_type=jnp.float32)


def over_rows(left, right):
    return lax.dot_general(
        left, right, (((0,), (0,)), ((), ())), preferred_element_type=jnp.float32
    )


def over_last(left, right):
    return lax.dot_general(
        left, right, (((1,), (1,)), ((), ())), preferred_element_type=jnp.float32
    )


def factored_step(weight, clipped, rows_next, cols_next, rows_mean, rate):
    estimate = rows_next[..., :, None] * cols_next[..., None, :] / rows_mean
    return weight - rate * clipped * lax.rsqrt(estimate)


def place():
    rep = lax.axis_index("rep")
    line = lax.axis_index("exp")
    y = lax.div(rep, 2) * 2 + lax.rem(lax.div(line, 4), 2)
    return {"y": y, "core": lax.rem(rep, 2), "x": lax.div(line, 8), "z": lax.rem(line, 4)}


def device(at):
    return {
        "rep": lax.div(at["y"], 2) * 2 + at["core"],
        "exp": at["x"] * 8 + lax.rem(at["y"], 2) * 4 + at["z"],
    }


def moved(at, axis, by):
    return {**at, axis: lax.rem(at[axis] + by, 2 if axis == "core" else 4)}


def box(ref, at, free, core=False):
    whole = slice(None)
    hi = whole if "y" in free else lax.div(at["y"], 2)
    low = whole if "y" in free else lax.rem(at["y"], 2)
    x = whole if "x" in free else at["x"]
    z = whole if "z" in free else at["z"]
    if core:
        return ref.at[hi, at["core"], x, low, z]
    return ref.at[hi, x, low, z]


def greet(at):
    barrier = pltpu.get_barrier_semaphore()
    peers = [moved(at, axis, by) for axis in ("x", "y", "z") for by in (1, 2, 3)]
    peers.append(moved(at, "core", 1))
    for peer in peers:
        pl.semaphore_signal(barrier, inc=1, device_id=device(peer), device_id_type=MESH)
    pl.semaphore_wait(barrier, len(peers))


def remote(src, dst, sems, index, peer):
    return pltpu.make_async_remote_copy(
        src_ref=src,
        dst_ref=dst,
        send_sem=sems[0].at[index],
        recv_sem=sems[1].at[index],
        device_id=device(peer),
        device_id_type=MESH,
    )


class Staged:
    def __init__(self, inputs, outputs):
        self.inputs, self.outputs, self.given = inputs, outputs, []

    def need(self, *indices):
        for index in indices:
            self.inputs[index].wait()

    def give(self, *indices):
        for index in indices:
            self.outputs[index].start()
            self.given.append(self.outputs[index])


def pin(value):
    return pltpu.with_memory_space_constraint(value, pltpu.HBM)


def staged_call(body, operands, shapes, scratch, far_in, far_out, **params):
    inputs, outputs = len(operands), len(shapes)
    raw, raw_out = params.pop("raw", ()), params.pop("raw_out", ())

    def kernel(*refs):
        refs = list(refs)
        stages = refs[inputs + outputs + len(scratch) :]
        stage_in, stages = stages[: len(far_in)], stages[len(far_in) :]
        stage_out, (sem_in, sem_out) = stages[: len(far_out)], stages[len(far_out) :]
        fetches, stores = {}, {}
        for number, index in enumerate(far_in):
            fetches[index] = pltpu.make_async_copy(refs[index], stage_in[number], sem_in.at[number])
            fetches[index].start()
            refs[index] = stage_in[number]
        for number, index in enumerate(far_out):
            stores[index] = pltpu.make_async_copy(stage_out[number], refs[inputs + index], sem_out.at[number])
            refs[inputs + index] = stage_out[number]
        staged = Staged(fetches, stores)
        body(staged, *refs[: inputs + outputs + len(scratch)])
        for copy in staged.given:
            copy.wait()

    anywhere, near = pl.BlockSpec(memory_space=pl.ANY), pl.BlockSpec(memory_space=pltpu.VMEM)
    return pl.pallas_call(
        kernel,
        out_shape=[
            pltpu.HBM(*shape) if index in far_out + raw_out else jax.ShapeDtypeStruct(*shape)
            for index, shape in enumerate(shapes)
        ],
        in_specs=[anywhere if index in far_in or index in raw else near for index in range(inputs)],
        out_specs=[anywhere if index in far_out + raw_out else near for index in range(outputs)],
        scratch_shapes=list(scratch)
        + [pltpu.VMEM(operands[index].shape, operands[index].dtype) for index in far_in]
        + [pltpu.VMEM(*shapes[index]) for index in far_out]
        + [pltpu.SemaphoreType.DMA((max(1, len(far_in)),)), pltpu.SemaphoreType.DMA((max(1, len(far_out)),))],
        compiler_params=pltpu.CompilerParams(
            collective_id=params["collective_id"],
            has_side_effects=True,
            vmem_limit_bytes=params["megabytes"] * 2**20,
        ),
        name=params["name"],
    )(*(pin(value) if index in far_in or index in raw else value for index, value in enumerate(operands)))


ORDERS = (("x", "y", "z"), ("y", "z", "x"), ("z", "x", "y"))


def gather_kernel(own_squares, own_extra, patches, ids, experts, *refs):
    squares, extra, spare, image, image_ids, experts_low = refs[:5], *refs[5:10]
    outs, (x_ref, wide, narrow, send, recv, local, local_in, local_out) = refs[10:13], refs[13:]
    at = place()
    sems = (send, recv)
    value = own_extra[...]
    high = value.astype(jnp.bfloat16).astype(jnp.float32)
    lane = lax.broadcasted_iota(jnp.int32, value.shape, 1)
    rest = jnp.where(lane < PATCHES, value - high, 0.0)
    high = jnp.where(lane >= VECTOR_AT + 16, value - high, high)
    blank = jnp.zeros((2, D), jnp.float32)
    for part, rows in enumerate(
        (
            (own_squares[0], rest[0:2], own_squares[1], rest[2:4]),
            (own_squares[2], rest[4:6], own_squares[3], blank),
            (own_squares[4], blank, high, blank),
        )
    ):
        x_ref[part] = jnp.concatenate(rows).astype(jnp.bfloat16)
    own = []
    for part in range(3):
        own.append(
            pltpu.make_async_copy(
                x_ref.at[part], box(outs[part], at, (), True), local.at[part]
            )
        )
        own[part].start()
    micro = lax.div(at["y"], 2)
    kept = [
        pltpu.make_async_copy(patches.at[micro], image.at[micro], local.at[3]),
        pltpu.make_async_copy(ids.at[micro], image_ids.at[micro], local.at[4]),
    ]
    for copy in kept:
        copy.start()

    def lines(ref, step):
        return ref.at[step // 3, pl.ds(step % 3 * 256, 256)]

    def fetch(step):
        return pltpu.make_async_copy(lines(experts, step), wide.at[step % 2], local_in.at[step % 2])

    def store(step):
        return pltpu.make_async_copy(narrow.at[step % 2], lines(experts_low, step), local_out.at[step % 2])

    def round_experts(step):
        if step < 5:
            fetch(step + 1).start()
        fetch(step).wait()
        if step >= 2:
            store(step - 2).wait()
        narrow[step % 2] = wide[step % 2].astype(jnp.bfloat16)
        store(step).start()

    fetch(0).start()
    greet(at)
    flights = {}

    def launch(part, stage):
        axes = ORDERS[part]
        view = box(outs[part], at, axes[:stage], True)
        source = x_ref.at[part] if stage == 0 else view
        for by in (1, 2, 3):
            copy = remote(source, view, sems, part * 13 + stage * 3 + by - 1, moved(at, axes[stage], by))
            copy.start()
            flights[part, stage, by] = copy

    def forward(part, by):
        axes = ORDERS[part]
        view = box(outs[part], moved(at, axes[2], 4 - by), axes[:2], True)
        copy = remote(view, view, sems, part * 13 + 9 + by, moved(at, "core", 1))
        copy.start()
        flights[part, 3, by] = copy

    for part in range(3):
        launch(part, 0)
    trades = [
        remote(patches.at[1 - micro], image.at[micro], sems, 39, moved(at, "y", 2)),
        remote(ids.at[1 - micro], image_ids.at[micro], sems, 40, moved(at, "y", 2)),
    ]
    for copy in trades:
        copy.start()
    round_experts(0)
    round_experts(1)
    for stage in (1, 2):
        for part in range(3):
            if stage == 1:
                own[part].wait()
            for by in (1, 2, 3):
                flights[part, stage - 1, by].wait_recv()
            launch(part, stage)
            if stage == 2:
                forward(part, 0)
        round_experts(2 * stage)
        round_experts(2 * stage + 1)
    store(4).wait()
    store(5).wait()
    for by in (1, 3, 2):
        for part in range(3):
            flights[part, 2, by].wait_recv()
            forward(part, by)

    row = lax.broadcasted_iota(jnp.int32, (96, 256), 0)
    column = lax.broadcasted_iota(jnp.int32, (96, 256), 1)
    base = lax.div(row, 6) * 16
    inside = lax.rem(row, 6)

    def packer(offset):
        return (column == base + offset + inside).astype(jnp.bfloat16)

    first, second = packer(0), packer(8)
    low_first = jnp.where(inside < 2, packer(6), jnp.where(inside < 4, packer(12), 0)).astype(jnp.bfloat16)
    low_second = jnp.where(inside < 4, 0, packer(2)).astype(jnp.bfloat16)
    packers = [
        jnp.concatenate([first, second, low_first]),
        jnp.concatenate([first, second, low_second]),
        jnp.concatenate([first, second]),
    ]

    def pack(core):
        def step(index, carry):
            high, half = lax.div(index, 2), lax.rem(index, 2)
            place_out = pl.ds(pl.multiple_of((high * 4 + core * 2 + half) * 96, 96), 96)
            packed = []
            for part in range(3):
                block = outs[part][high, core, pl.ds(half * 2, 2)].reshape(256, D)
                packed.append(plain_dot(packers[part], block))
            for k in range(5):
                low = packed[k // 2][96 * (k % 2) : 96 * (k % 2) + 96]
                squares[k][place_out, :] = low.astype(jnp.bfloat16)
            extra[place_out, :] = packed[2][96:].astype(jnp.bfloat16)
            spare[place_out, :] = (packed[0][192:] + packed[1][192:]).astype(jnp.bfloat16)
            return carry

        lax.fori_loop(0, 4, step, 0)

    pack(at["core"])
    for key, copy in flights.items():
        if key[1] == 3:
            copy.wait_recv()
    pack(1 - at["core"])
    for copy in kept + trades:
        copy.wait()
    for copy in flights.values():
        copy.wait_send()


def gather_all(squares, extra, patches, ids, experts):
    shape = (2, 2, 4, 2, 4, 16, D)
    return pl.pallas_call(
        gather_kernel,
        out_shape=[jax.ShapeDtypeStruct((D, D), jnp.bfloat16)] * 7
        + [pltpu.HBM(value.shape, value.dtype) for value in (patches, ids)]
        + [pltpu.HBM(experts.shape, jnp.bfloat16)],
        in_specs=[pl.BlockSpec(memory_space=pltpu.VMEM)] * 2 + [pl.BlockSpec(memory_space=pl.ANY)] * 3,
        out_specs=[pl.BlockSpec(memory_space=pltpu.VMEM)] * 7 + [pl.BlockSpec(memory_space=pl.ANY)] * 3,
        scratch_shapes=[pltpu.VMEM(shape, jnp.bfloat16)] * 3
        + [
            pltpu.VMEM((3, 16, D), jnp.bfloat16),
            pltpu.VMEM((2, 256, D), jnp.float32),
            pltpu.VMEM((2, 256, D), jnp.bfloat16),
            pltpu.SemaphoreType.DMA((41,)),
            pltpu.SemaphoreType.DMA((41,)),
            pltpu.SemaphoreType.DMA((5,)),
            pltpu.SemaphoreType.DMA((2,)),
            pltpu.SemaphoreType.DMA((2,)),
        ],
        compiler_params=pltpu.CompilerParams(
            collective_id=0, has_side_effects=True, vmem_limit_bytes=24 * 2**20
        ),
        name="gather_weights",
    )(squares, extra, pin(patches), pin(ids), pin(experts))


def gradients_kernel(
    staged, patches, hidden_one, mixed, dembed, dquery, dkey, dvalue, dafter, hidden_two, dgate, sums, final_sums,
    head_grad, expert_squared, loss, square_rows, router_rows, *refs,
):
    outs, totals, refs = refs[:3], refs[3], refs[1:]
    lefts, tables, rights, left_got, table_got, right_got, few_mine, few_got, few_t, partial, grads = refs[3:14]
    first, total_one, second, total_two, third = (refs[14 + 3 * i : 17 + 3 * i] for i in range(5))
    core_sems, sems = refs[29:31], refs[31:33]
    parts, total_sems = refs[33], refs[34:36]
    at = place()
    other = moved(at, "core", 1)
    count = patches.shape[0]
    part_rows = D // 4
    for index, ref in enumerate((dembed, dquery, dkey, dvalue, dafter)):
        rights[index] = ref[...]
    greet(at)
    copies = [remote(rights, right_got, core_sems, 0, other)]
    copies[0].start()
    staged.need(0, 1, 2, 8)
    for index, ref in enumerate((patches, hidden_one, mixed)):
        lefts[index] = ref[...].T.reshape(4, part_rows, count)
    padded = jnp.concatenate([dembed[...], jnp.zeros((3 * LANES - count, D), jnp.bfloat16)])
    tables[...] = padded.T.reshape(4, part_rows, 3 * LANES)
    for half in range(2):
        source = lefts.at[:, 2 * half + other["core"]]
        copies.append(remote(source, left_got.at[:, half], core_sems, 1 + half, other))
        source = tables.at[2 * half + other["core"]]
        copies.append(remote(source, table_got.at[half], core_sems, 3 + half, other))
    few_mine[:32, :] = plain_dot(dgate[...].T, hidden_two[...])[64:96]
    few_mine[32:40, :] = sums[...]
    few_mine[40:48, :] = final_sums[...]
    copies.append(remote(few_mine, few_got, core_sems, 5, other))
    for copy in copies[1:]:
        copy.start()

    pairs = ((0, 0), (1, 1), (1, 2), (1, 3), (2, 4))

    def own_product(half, carry):
        rows = 2 * half + at["core"]
        for index, (left, right) in enumerate(pairs):
            partial[index, half] = plain_dot(lefts[left, rows], rights[right])
        return carry

    lax.fori_loop(0, 2, own_product, 0)
    for copy in copies:
        copy.wait_recv()
    few = few_mine[...] + few_got[...]
    few_high = few.astype(jnp.bfloat16)
    few_low = (few - few_high.astype(jnp.float32)).astype(jnp.bfloat16)
    blank = jnp.zeros((32, D), jnp.bfloat16)
    few_rows = jnp.concatenate([blank, few_high[:32], few_low[:32], few_high[32:], few_low[32:]])
    few_t[...] = few_rows.T.reshape(4, part_rows, LANES)

    def spread(offset):
        shape = (part_rows // 6 * 2 * PAD, part_rows)
        row, column = iota(shape, 0), iota(shape, 1)
        inside = lax.rem(row, 2 * PAD) - offset
        hit = (inside >= 0) & (inside < 6) & (column == lax.div(row, 2 * PAD) * 6 + inside)
        return hit.astype(jnp.bfloat16)

    spreads = jnp.concatenate([spread(0), spread(PAD)], axis=1)

    def finish(part, half):
        rows = 2 * half + at["core"]
        pieces = []
        for index in (2 * part, 2 * part + 1):
            if index < 5:
                left, right = pairs[index]
                value = partial[index, half] + plain_dot(left_got[left, half], right_got[right])
                pieces.append(value.astype(jnp.bfloat16))
            else:
                mine, theirs = tables[rows], table_got[half]
                is_first = at["core"] == 0
                low = jnp.where(is_first, mine, theirs)
                high = jnp.where(is_first, theirs, mine)
                high = jnp.concatenate(
                    [high[:, : 2 * LANES], high[:, 2 * LANES :] + few_t[rows]], axis=1
                )
                pieces.append(jnp.concatenate([low, high], axis=1))
        value = plain_dot(spreads, jnp.concatenate(pieces)).astype(jnp.bfloat16)
        grads[part, half] = value.reshape(4, 2, 4, 2 * PAD, D)

    def names(axis):
        return ("h", "l") if axis == "y" else (axis,)

    def pick(letter, where, axis):
        if letter not in names(axis):
            return slice(None)
        if letter == "h":
            return lax.div(where["y"], 2)
        if letter == "l":
            return lax.rem(where["y"], 2)
        return where[axis]

    def part_of(source, where, axes, stage):
        if stage == 0:
            return box(source, where, axes[:2])
        if stage == 1:
            left = [letter for letter in ("h", "x", "l", "z") if letter not in names(axes[2])]
            return source.at[tuple(pick(letter, where, axes[1]) for letter in left)]
        return source.at[tuple(pick(letter, where, axes[0]) for letter in names(axes[0]))]

    sources = ([grads.at[part] for part in range(3)], total_one, total_two)
    landings = (first, second, third)
    targets = (total_one, total_two, outs)
    flights = {}

    def launch(part, stage):
        axes = ORDERS[part]
        axis = axes[2 - stage]
        flights[part, stage] = []
        for by in (1, 2, 3):
            peer = moved(at, axis, by)
            view = part_of(sources[stage][part], peer, axes, stage)
            copy = remote(view, landings[stage][part].at[by - 1], sems, part * 9 + stage * 3 + by - 1, peer)
            copy.start()
            flights[part, stage].append(copy)

    for part in range(3):
        for half in range(2):
            finish(part, half)
        launch(part, 0)
    head_squared = jnp.sum(head_grad[...] * head_grad[...], axis=0, keepdims=True)
    expert_norm = jnp.sum(jnp.sum(expert_squared[0:2, :], axis=1, keepdims=True), axis=0, keepdims=True)
    for stage in range(3):
        for part in range(3):
            for copy in flights[part, stage]:
                copy.wait_recv()
            landing = landings[stage][part]
            terms = [part_of(sources[stage][part], at, ORDERS[part], stage)[...]]
            terms = [term.astype(jnp.float32) for term in terms + [landing[i] for i in range(3)]]
            targets[stage][part][...] = (terms[0] + terms[1]) + (terms[2] + terms[3])
            if stage < 2:
                launch(part, stage + 1)

    tail = outs[2][PAD:, EXTRA:]
    lane = iota(tail.shape, 1)
    router = tail + pltpu.roll(tail, LANES - GROUP, 1)
    vectors = tail + pltpu.roll(tail, LANES - 16, 1)
    tail = jnp.where(lane < 32, tail, jnp.where(lane < 64, router, jnp.where((lane >= 96) & (lane < 112), vectors, 0.0)))
    outs[2][PAD:, EXTRA:] = tail
    squared = [outs[k // 2][PAD * (k % 2) : PAD * (k % 2) + PAD, :] for k in range(6)]
    squared = [jnp.sum(value * value, axis=0, keepdims=True) for value in squared]
    spot = iota((1, D), 1)
    last = jnp.where(spot == 1, expert_norm, 0.0) + jnp.where(spot == 0, loss[...], 0.0)
    for k in range(5):
        last = last + jnp.where(spot == 2 + k, jnp.sum(square_rows[k : k + 1, :], axis=1, keepdims=True), 0.0)
    last = last + jnp.where(spot == 7, jnp.sum(router_rows[...], axis=1, keepdims=True), 0.0)
    parts[0, 0] = jnp.concatenate(squared[:5] + [head_squared, squared[5], last])
    parts[0, 1] = expert_squared[...]
    total = parts.at[0]
    number = 0
    for stage, axis in enumerate(("core", "y", "z", "x")):
        size = 2 if axis == "core" else 4
        base = 1 + 5 * stage
        trips = []
        for by in range(1, size):
            whole = axis == "core" or (axis == "y" and by == 2)
            view = total if whole else total.at[0]
            slot = parts.at[base + at[axis]]
            trips.append(remote(view, slot if whole else slot.at[0], total_sems, number, moved(at, axis, by)))
            trips[-1].start()
            number += 1
        parts[base + at[axis]] = total[...]
        for trip in trips:
            trip.wait()
        value = parts[base, 0]
        for index in range(1, size):
            value = value + parts[base + index, 0]
        parts[base + 4, 0] = value
        if axis == "core":
            parts[base + 4, 1] = parts[base, 1] + parts[base + 1, 1]
        elif axis == "y":
            parts[base + 4, 1] = parts[base + at["y"], 1] + parts[base + lax.rem(at["y"] + 2, 4), 1]
            totals[PAD:, :] = parts[base + 4, 1]
        else:
            parts[base + 4, 1] = jnp.zeros((PAD, D), jnp.float32)
        total = parts.at[base + 4]
    totals[:PAD, :] = total[0]
    for copy in copies:
        copy.wait_send()
    for launched in flights.values():
        for copy in launched:
            copy.wait_send()


def shared_gradients(*operands):
    count = operands[0].shape[0]
    low, wide = jnp.bfloat16, jnp.float32
    block = (2 * PAD, D)
    ones = [{"x": (2, 2, 4), "y": (4, 4), "z": (2, 4, 2)}[axes[2]] for axes in ORDERS]
    twos = [(2, 2) if axes[0] == "y" else (4,) for axes in ORDERS]
    rows = D // 4
    scratch = [
        pltpu.VMEM((3, 4, rows, count), low),
        pltpu.VMEM((4, rows, 3 * LANES), low),
        pltpu.VMEM((5, count, D), low),
        pltpu.VMEM((3, 2, rows, count), low),
        pltpu.VMEM((2, rows, 3 * LANES), low),
        pltpu.VMEM((5, count, D), low),
        pltpu.VMEM((48, D), wide),
        pltpu.VMEM((48, D), wide),
        pltpu.VMEM((4, rows, LANES), low),
        pltpu.VMEM((5, 2, rows, D), wide),
        pltpu.VMEM((3, 2, 4, 2, 4) + block, low),
    ]
    scratch += [pltpu.VMEM((3,) + one + block, low) for one in ones]
    scratch += [pltpu.VMEM(one + block, wide) for one in ones]
    scratch += [pltpu.VMEM((3,) + two + block, wide) for two in twos]
    scratch += [pltpu.VMEM(two + block, wide) for two in twos]
    scratch += [pltpu.VMEM((3,) + block, wide)] * 3
    scratch += [pltpu.SemaphoreType.DMA((6,))] * 2 + [pltpu.SemaphoreType.DMA((27,))] * 2
    scratch += [pltpu.VMEM((21, 2, PAD, D), wide)] + [pltpu.SemaphoreType.DMA((10,))] * 2
    return staged_call(
        gradients_kernel,
        operands,
        [(block, wide)] * 4,
        scratch,
        (0, 1, 2, 8),
        (),
        collective_id=1,
        megabytes=36,
        name="shared_gradients",
    )


def meet_core(at):
    barrier = pltpu.get_barrier_semaphore()
    other = moved(at, "core", 1)
    pl.semaphore_signal(barrier, inc=1, device_id=device(other), device_id_type=MESH)
    pl.semaphore_wait(barrier, 1)
    return other


CHUNK = 48


def chunks(count, step, start=0):
    lax.fori_loop(0, count // CHUNK, lambda i, c: step(pl.ds(pl.multiple_of(i * CHUNK, CHUNK), CHUNK), c), start)


def centre(value):
    centred = value - jnp.mean(value, axis=-1, keepdims=True)
    spread = jnp.mean(centred * centred, axis=-1, keepdims=True)
    return centred * lax.rsqrt(spread + 1e-06), lax.rsqrt(spread + 1e-06)


def norm_back(value, grad, gain):
    normed, rate = centre(value)
    scaled = grad * gain
    inner = (
        scaled
        - jnp.mean(scaled, axis=-1, keepdims=True)
        - normed * jnp.mean(scaled * normed, axis=-1, keepdims=True)
    )
    return rate * inner, jnp.sum(grad * normed, axis=0, keepdims=True), jnp.sum(grad, axis=0, keepdims=True)


def attend_kernel(
    staged, x_ref, w0, w1, w2, w3, w4, extra, spare, ids,
    embed, hidden_one, query, keys, values, mixed, after, hidden_two, gate_probs, gates, lse,
    vec, router, target, target_t, hidden_kept, w1_kept, w2_kept, w3_kept, w4_kept,
    turned, local, send, recv,
):
    at = place()
    sems = (send, recv)
    saves = [
        pltpu.make_async_copy(source, target_ref, local.at[index])
        for index, (source, target_ref) in enumerate(
            ((w1, w1_kept), (w2, w2_kept), (w3, w3_kept), (w4, w4_kept), (hidden_two, hidden_kept))
        )
    ]
    for copy in saves[:4]:
        copy.start()
    other = meet_core(at)
    rows = x_ref.shape[0]
    staged.need(8)
    turned[...] = (
        extra[:, :EXTRA].astype(jnp.float32) + spare[:, :EXTRA].astype(jnp.float32)
    ).T
    vec[...] = turned[VECTOR_AT : VECTOR_AT + 16, :] + turned[VECTOR_AT + 16 : VECTOR_AT + 32, :]
    router[...] = extra[:, EXTRA - LANES : EXTRA]

    block = rows // 2
    earlier = (iota((block, block), 1) < iota((block, block), 0)).astype(jnp.bfloat16)
    lane = iota((block, LANES), 1)
    for number in range(2):
        part = slice(number * block, (number + 1) * block)
        hits = [(lane == ids[part, k : k + 1]).astype(jnp.float32) for k in range(2)]
        before = plain_dot(earlier, (hits[0] + hits[1]).astype(jnp.bfloat16))
        spots = []
        for k in range(2):
            named = ids[part, k : k + 1]
            slot = jnp.sum(hits[k] * before, axis=-1, keepdims=True).astype(jnp.int32) + number * CAP
            spots.append(
                jnp.where(slot < SLOTS, named * SLOTS + slot, MAIN + named * TAIL + slot - SLOTS)
            )
        target[part, :] = jnp.where(lane == 0, spots[0], jnp.where(lane == 1, spots[1], 0))
    target_t[...] = target[...].astype(jnp.float32).T[:PAD].astype(jnp.int32)

    staged.need(0)
    embed[...] = plain_dot(x_ref[...], w0[...])

    def first_norm(index, carry):
        part = pl.ds(pl.multiple_of(index * CHUNK, CHUNK), CHUNK)
        line = at["core"] * block + index * CHUNK + jnp.where(index * CHUNK < block, 0, block)
        value = embed[part, :] + vec[0:1, :] + turned[pl.ds(pl.multiple_of(line, CHUNK), CHUNK), :]
        embed[part, :] = value
        normed, _ = centre(value)
        hidden_one[part, :] = (normed * vec[1:2, :] + vec[2:3, :]).astype(jnp.bfloat16)
        return carry

    lax.fori_loop(0, rows // CHUNK, first_norm, 0)
    keys[0] = plain_dot(hidden_one[...], w2[...]).astype(jnp.bfloat16)
    send_keys = remote(keys.at[0], keys.at[1], sems, 0, other)
    send_keys.start()
    values[0] = (plain_dot(hidden_one[...], w3[...]) + vec[4:5, :]).astype(jnp.bfloat16)
    send_values = remote(values.at[0], values.at[1], sems, 1, other)
    send_values.start()
    query[...] = (plain_dot(hidden_one[...], w1[...]) + vec[3:4, :]).astype(jnp.bfloat16)
    send_keys.wait()
    send_values.wait()
    staged.give(0, 1, 2, 3, 4)

    def heads(index, carry):
        lanes = pl.ds(pl.multiple_of(index * LANES, LANES), LANES)
        query_two = query[:, lanes]
        key_two = keys[:, :, lanes].reshape(2 * rows, LANES)
        value_t = values[:, :, lanes].reshape(2 * rows, LANES).T
        left = lax.broadcasted_iota(jnp.int32, (rows, LANES), 1) < HEAD
        outs = []
        for half in range(2):
            own = jnp.where(left if half == 0 else ~left, query_two, jnp.zeros_like(query_two))
            scores = over_last(key_two, own) * HEAD ** (-0.5)
            most = jnp.max(scores, axis=0, keepdims=True)
            raw = jnp.exp(scores - most)
            total = jnp.sum(raw, axis=0, keepdims=True)
            lse[pl.ds(index * 2 + half, 1), :] = most + jnp.log(total)
            probs = (raw * (1.0 / total)).astype(jnp.bfloat16)
            outs.append(plain_dot(value_t[half * HEAD : (half + 1) * HEAD], probs))
        mixed[:, lanes] = jnp.concatenate(outs).T.astype(jnp.bfloat16)
        return carry

    lax.fori_loop(0, D // LANES, heads, 0)
    staged.give(5)
    after[...] = plain_dot(mixed[...], w4[...])

    def second_norm(part, carry):
        value = embed[part, :] + after[part, :] + vec[5:6, :]
        after[part, :] = value
        normed, _ = centre(value)
        low = (normed * vec[6:7, :] + vec[7:8, :]).astype(jnp.bfloat16)
        hidden_two[part, :] = low
        logits = plain_dot(low, router[...])
        lane = iota(logits.shape, 1) - ROUTER_AT
        logits = jnp.where((lane >= 0) & (lane < GROUP), logits, -jnp.inf)
        raw = jnp.exp(logits - jnp.max(logits, axis=-1, keepdims=True))
        probs = raw / jnp.sum(raw, axis=-1, keepdims=True)
        gate_probs[part, :] = probs
        first, second = (
            jnp.sum(jnp.where(lane == ids[part, k : k + 1], probs, 0.0), axis=-1, keepdims=True) for k in range(2)
        )
        gates[part, :] = jnp.where(lane == -ROUTER_AT, first, second)
        return carry

    chunks(rows, second_norm)
    staged.give(6)
    saves[4].start()
    for copy in saves:
        copy.wait()


def attend(patch_rows, squares, extra, spare, ids):
    rows = patch_rows.shape[0]
    low, wide = jnp.bfloat16, jnp.float32
    shapes = [
        ((rows, D), wide), ((rows, D), low), ((rows, D), low), ((2, rows, D), low), ((2, rows, D), low),
        ((rows, D), low), ((rows, D), wide), ((rows, D), low), ((rows, LANES), wide), ((rows, LANES), wide), ((16, rows), wide),
        ((16, D), wide), ((D, LANES), low), ((rows, LANES), jnp.int32), ((PAD, rows), jnp.int32),
        ((rows, D), low), ((D, D), low), ((D, D), low), ((D, D), low), ((D, D), low),
    ]
    sems = pltpu.SemaphoreType.DMA
    return staged_call(
        attend_kernel,
        (patch_rows, *squares, extra, spare, ids),
        shapes,
        [pltpu.VMEM((EXTRA, D), wide), sems((5,)), sems((2,)), sems((2,))],
        (0, 8),
        tuple(range(7)),
        raw_out=(15, 16, 17, 18, 19),
        collective_id=6,
        megabytes=20,
        name="attend",
    )


def attend_back_kernel(
    staged, dafter_in, dhidden, dgate, embed, after, query, keys, values, lse, w1, w2, w3, w4, vec, router,
    dafter_low, dquery, dkey, dvalue, dembed_low, sums,
    dafter, dmixed, dkey_own, dvalue_own, dkey_other, dvalue_other, dkey_got, dvalue_got, wide, send, recv,
):
    at = place()
    sems = (send, recv)
    other = meet_core(at)
    rows = dafter_in.shape[0]
    pairs = D // LANES
    zero = jnp.zeros((1, D), jnp.float32)
    wide[...] = over_last(dgate[...], router[...])
    staged.need(4)

    def second_norm(index, carry):
        part = pl.ds(pl.multiple_of(index * CHUNK, CHUNK), CHUNK)
        grad = wide[part, :] + dhidden[part, :]
        back, gain, shift = norm_back(after[part, :], grad, vec[6:7, :])
        total = dafter_in[part, :] + back
        dafter[part, :] = total
        dafter_low[part, :] = total.astype(jnp.bfloat16)
        return carry[0] + jnp.sum(total, axis=0, keepdims=True), carry[1] + gain, carry[2] + shift

    bias, gain, shift = lax.fori_loop(0, rows // CHUNK, second_norm, (zero, zero, zero))
    sums[5:6, :] = bias
    sums[6:7, :] = gain
    sums[7:8, :] = shift
    staged.need(12)
    dmixed[...] = over_last(dafter_low[...], w4[...]).astype(jnp.bfloat16)
    staged.need(5, 6, 7)

    def flights(index):
        return (
            remote(dkey_other.at[index], dkey_got.at[index], sems, index, other),
            remote(dvalue_other.at[index], dvalue_got.at[index], sems, pairs + index, other),
        )

    def heads(index, carry):
        lanes = pl.ds(pl.multiple_of(index * LANES, LANES), LANES)
        query_two = query[:, lanes]
        dmixed_two = dmixed[:, lanes]
        key_two = keys[:, :, lanes].reshape(2 * rows, LANES)
        value_two = values[:, :, lanes].reshape(2 * rows, LANES)
        key_t = key_two.T
        left = lax.broadcasted_iota(jnp.int32, (rows, LANES), 1) < HEAD
        dkey_two = jnp.zeros((2 * rows, LANES), jnp.float32)
        dvalue_two = jnp.zeros((2 * rows, LANES), jnp.float32)
        outs = []
        for half in range(2):
            mask = left if half == 0 else ~left
            own = jnp.where(mask, query_two, jnp.zeros_like(query_two))
            down = jnp.where(mask, dmixed_two, jnp.zeros_like(dmixed_two))
            scores = over_last(key_two, own) * HEAD ** (-0.5)
            probs = jnp.exp(scores - lse[pl.ds(index * 2 + half, 1), :])
            dprobs = over_last(value_two, down)
            row_shift = jnp.sum(probs * dprobs, axis=0, keepdims=True)
            dscores = (probs * (dprobs - row_shift)).astype(jnp.bfloat16)
            dvalue_two = dvalue_two + plain_dot(probs.astype(jnp.bfloat16), down)
            dkey_two = dkey_two + plain_dot(dscores, own)
            outs.append(plain_dot(key_t[half * HEAD : (half + 1) * HEAD], dscores))
        dkey_two = dkey_two * HEAD ** (-0.5)
        dquery[:, lanes] = (jnp.concatenate(outs).T * HEAD ** (-0.5)).astype(jnp.bfloat16)
        dkey_own[index] = dkey_two[:rows]
        dkey_other[index] = dkey_two[rows:]
        dvalue_own[index] = dvalue_two[:rows]
        dvalue_other[index] = dvalue_two[rows:]
        for copy in flights(index):
            copy.start()
        return carry

    lax.fori_loop(0, pairs, heads, 0)

    def gather(index, carry):
        lanes = pl.ds(pl.multiple_of(index * LANES, LANES), LANES)
        for copy in flights(index):
            copy.wait()
        dkey[:, lanes] = (dkey_own[index] + dkey_got[index]).astype(jnp.bfloat16)
        dvalue[:, lanes] = (dvalue_own[index] + dvalue_got[index]).astype(jnp.bfloat16)
        return carry

    lax.fori_loop(0, pairs, gather, 0)
    staged.need(3, 9, 10, 11)
    wide[...] = (
        over_last(dquery[...], w1[...]) + over_last(dkey[...], w2[...]) + over_last(dvalue[...], w3[...])
    )

    def first_norm(index, carry):
        part = pl.ds(pl.multiple_of(index * CHUNK, CHUNK), CHUNK)
        back, gain, shift = norm_back(embed[part, :], wide[part, :], vec[1:2, :])
        total = dafter[part, :] + back
        dembed_low[part, :] = total.astype(jnp.bfloat16)
        return (
            carry[0] + jnp.sum(total, axis=0, keepdims=True),
            carry[1] + gain,
            carry[2] + shift,
            carry[3] + jnp.sum(dquery[part, :].astype(jnp.float32), axis=0, keepdims=True),
            carry[4] + jnp.sum(dvalue[part, :].astype(jnp.float32), axis=0, keepdims=True),
        )

    for index, total in enumerate(lax.fori_loop(0, rows // CHUNK, first_norm, (zero,) * 5)):
        sums[index : index + 1, :] = total


def attend_back(*operands):
    rows = operands[0].shape[0]
    low, wide = jnp.bfloat16, jnp.float32
    pairs = D // LANES
    sems = pltpu.SemaphoreType.DMA
    return staged_call(
        attend_back_kernel,
        operands,
        [((rows, D), low)] * 5 + [((8, D), wide)],
        [pltpu.VMEM((rows, D), wide), pltpu.VMEM((rows, D), low)]
        + [pltpu.VMEM((pairs, rows, LANES), wide)] * 6
        + [pltpu.VMEM((rows, D), wide), sems((2 * pairs,)), sems((2 * pairs,))],
        (4, 12, 5, 6, 7, 3, 9, 10, 11),
        (),
        collective_id=7,
        megabytes=22,
        name="attend_back",
    )


SLOTS = 16
TAIL = 2 * CAP - SLOTS
WIRE = D + 2 * LANES
GROUP = 32
MAIN = GROUP * SLOTS
TOTAL = GROUP * (SLOTS + TAIL)


def iota(shape, axis):
    return lax.broadcasted_iota(jnp.int32, shape, axis)


def pack(block, main, tail):
    count = block.shape[0]
    block[:, :, :D] = main.astype(jnp.bfloat16).reshape(count, SLOTS, D)
    shape = (count * SLOTS, count * TAIL)
    row, column = iota(shape, 0), iota(shape, 1)
    spread = (lax.div(row, SLOTS) == lax.div(column, TAIL)) & (lax.rem(row, TAIL) == lax.rem(column, TAIL))
    wide = plain_dot(spread.astype(jnp.bfloat16), tail.astype(jnp.bfloat16))
    turn = lax.div(lax.rem(iota((count * SLOTS, LANES), 0), SLOTS), TAIL)
    for half, tiles in ((0, (0, 1, 2, 3)), (1, (4, 5))):
        packed = jnp.zeros((count * SLOTS, LANES), jnp.float32)
        for place_in, tile in enumerate(tiles):
            packed = jnp.where(turn == place_in, wide[:, tile * LANES : (tile + 1) * LANES], packed)
        block[:, :, D + half * LANES : D + (half + 1) * LANES] = packed.astype(jnp.bfloat16).reshape(
            count, SLOTS, LANES
        )


def unpack(block, rows, first, first_tail):
    count = block.shape[0]
    rows[first : first + count * SLOTS, :] = block[:, :, :D].reshape(count * SLOTS, D)
    shape = (count * TAIL, count * SLOTS)
    row, column = iota(shape, 0), iota(shape, 1)
    same = lax.div(column, SLOTS) == lax.div(row, TAIL)
    packed = block[:, :, D:].reshape(count * SLOTS, 2 * LANES)
    for turn in range(4):
        chosen = same & (lax.rem(column, SLOTS) == turn * TAIL + lax.rem(row, TAIL))
        part = plain_dot(chosen.astype(jnp.bfloat16), packed).astype(jnp.bfloat16)
        rows[first_tail : first_tail + count * TAIL, turn * LANES : (turn + 1) * LANES] = part[:, :LANES]
        if turn < 2:
            rows[first_tail : first_tail + count * TAIL, (4 + turn) * LANES : (5 + turn) * LANES] = part[
                :, LANES:
            ]


def meet_experts(at):
    barrier = pltpu.get_barrier_semaphore()
    me = lax.axis_index("exp")

    def greet_one(by, carry):
        peer = lax.rem(me + by, GROUP)
        pl.semaphore_signal(barrier, inc=1, device_id={"exp": peer}, device_id_type=MESH)
        return carry

    lax.fori_loop(1, GROUP, greet_one, 0)
    peers = moved(at, "core", 1), moved(at, "y", 2)
    for peer in peers:
        pl.semaphore_signal(barrier, inc=1, device_id=device(peer), device_id_type=MESH)
    return peers


def met_experts():
    pl.semaphore_wait(pltpu.get_barrier_semaphore(), GROUP + 1)


def deal(source, target, sems, forth, low, high, act):
    me = lax.axis_index("exp")

    def one(by, carry):
        peer = lax.rem(me + by, GROUP) if forth else lax.rem(me + GROUP - by, GROUP)
        copy = pltpu.make_async_remote_copy(
            src_ref=source.at[peer] if forth else source.at[by],
            dst_ref=target.at[by] if forth else target.at[me],
            send_sem=sems[0].at[by],
            recv_sem=sems[1].at[by],
            device_id={"exp": peer},
            device_id_type=MESH,
        )
        act(copy)
        return carry

    lax.fori_loop(low, high, one, 0)


def start_copy(copy):
    copy.start()


def wait_send(copy):
    copy.wait_send()


def wait_recv(copy):
    copy.wait_recv()


def load_experts(own, across, weights, sems, local, other):
    near = [pltpu.make_async_copy(own, weights.at[0], local.at[0])]
    far = [remote(own, weights.at[2], sems, 0, other)]
    for which, ref in enumerate(across):
        near.append(pltpu.make_async_copy(ref, weights.at[1, which], local.at[1 + which]))
        far.append(remote(ref, weights.at[3, which], sems, 1 + which, other))
    return near, far


GELU_SCALE = math.sqrt(2 / math.pi)


def gelu_tanh(value):
    return jnp.tanh(GELU_SCALE * (value + 0.044715 * (value * value * value)))


def halves(rows, half):
    count = MAIN // 2
    tail = (TOTAL - MAIN) // 2
    return jnp.concatenate(
        [
            rows[half * count : (half + 1) * count, :],
            rows[MAIN + half * tail : MAIN + (half + 1) * tail, :],
        ]
    )


HALF = TOTAL // 2


def experts_kernel(
    staged, hidden, target_row, target_column, gates, after, vec, own, across_in,
    rows, rows_y, chosen, total, pool, across_out,
    weights, sends, lands, backs, returns, act, result, gathered,
    forth_send, forth_recv, back_send, back_recv, weight_send, weight_recv, row_send, row_recv, local,
):
    at = place()
    me = lax.axis_index("exp")
    other, across_y_peer = meet_experts(at)
    row_copies = []
    near, far = load_experts(own, (across_in,), weights, (weight_send, weight_recv), local, other)
    trade = remote(own.at[1], weights.at[1, 1], (weight_send, weight_recv), 2, across_y_peer)
    pass_on = remote(weights.at[1, 1], weights.at[3, 1], (weight_send, weight_recv), 3, other)
    save = pltpu.make_async_copy(weights.at[1, 1], across_out, local.at[3])
    for copy in near:
        copy.start()
    count = hidden.shape[0]
    slot = iota((TOTAL, count), 0)
    placing = ((slot == target_row[0:1, :]) | (slot == target_row[1:2, :])).astype(jnp.bfloat16)
    placed = plain_dot(placing, hidden[...])
    pack(sends, placed[:MAIN], placed[MAIN:])
    met_experts()
    deal(sends, lands, (forth_send, forth_recv), True, 1, GROUP, start_copy)
    for copy in [*far, trade]:
        copy.start()
    keep = pltpu.make_async_copy(sends.at[me], lands.at[0], local.at[2])
    keep.start()
    keep.wait()
    deal(sends, lands, (forth_send, forth_recv), True, 1, GROUP // 2, wait_recv)
    for copy in near:
        copy.wait()
    for half in range(2):
        if half == 1:
            deal(sends, lands, (forth_send, forth_recv), True, GROUP // 2, GROUP, wait_recv)
        sources = pl.ds(half * (GROUP // 2), GROUP // 2)
        first, first_tail = half * (MAIN // 2), MAIN + half * (TOTAL - MAIN) // 2
        unpack(lands.at[sources], rows, first, first_tail)
        for piece, (start, size) in enumerate(((first, MAIN // 2), (first_tail, (TOTAL - MAIN) // 2))):
            view = pl.ds(start, size)
            copy = remote(rows.at[view], rows_y.at[view], (row_send, row_recv), half * 2 + piece, across_y_peer)
            copy.start()
            row_copies.append(copy)
        if half == 0:
            for copy in far:
                copy.wait_recv()
        given = halves(rows, half)

        def hidden_units(index, carry):
            quarter, part = lax.div(index, 3), lax.rem(index, 3)
            columns = pl.ds(pl.multiple_of(part * 256, 256), 256)
            value = plain_dot(given, weights[quarter, 0, :, columns])
            act[quarter, :, columns] = (0.5 * value * (1.0 + gelu_tanh(value))).astype(jnp.bfloat16)
            return carry

        lax.fori_loop(0, 12, hidden_units, 0)
        if half == 0:
            trade.wait_recv()
            pass_on.start()
            save.start()
            pass_on.wait_recv()

        def outputs(index, carry):
            columns = pl.ds(pl.multiple_of(index * 256, 256), 256)
            value = over_last(act[0], weights[0, 1, columns, :])
            for quarter in range(1, 4):
                value = value + over_last(act[quarter], weights[quarter, 1, columns, :])
            result[:, columns] = value
            return carry

        lax.fori_loop(0, 3, outputs, 0)
        pack(backs.at[sources], result[: MAIN // 2, :], result[MAIN // 2 :, :])
        deal(backs, returns, (back_send, back_recv), False, max(1, half * (GROUP // 2)), (half + 1) * (GROUP // 2), start_copy)
    keep = pltpu.make_async_copy(backs.at[0], returns.at[me], local.at[2])
    keep.start()
    keep.wait()
    deal(backs, returns, (back_send, back_recv), False, 1, GROUP, wait_recv)
    unpack(returns, gathered, 0, MAIN)
    slot = iota((count, TOTAL), 1)
    for k in range(2):
        placing = (slot == target_column[:, k : k + 1]).astype(jnp.bfloat16)
        chosen[k] = plain_dot(placing, gathered[...]).astype(jnp.bfloat16)
    staged.give(0, 2)
    staged.need(4)

    def final_norm(index, carry):
        part = pl.ds(pl.multiple_of(index * CHUNK, CHUNK), CHUNK)
        value = after[part, :] + (
            gates[part, 0:1] * chosen[0, part, :].astype(jnp.float32)
            + gates[part, 1:2] * chosen[1, part, :].astype(jnp.float32)
        )
        total[part, :] = value
        normed, _ = centre(value)
        return carry + jnp.sum(normed * vec[8:9, :] + vec[9:10, :], axis=0, keepdims=True)

    summed = lax.fori_loop(0, count // CHUNK, final_norm, jnp.zeros((1, D), jnp.float32)) / PATCHES
    staged.give(3)
    pool[...] = jnp.zeros_like(pool)
    for tile in range(D // LANES):
        pool[tile : tile + 1, :] = summed[:, tile * LANES : (tile + 1) * LANES]
    deal(sends, lands, (forth_send, forth_recv), True, 1, GROUP, wait_send)
    deal(backs, returns, (back_send, back_recv), False, 1, GROUP, wait_send)
    for copy in [*far, trade, pass_on]:
        copy.wait_send()
    save.wait()
    for copy in row_copies:
        copy.wait()
    staged.give(1)


def experts_forward(*operands):
    count = operands[0].shape[0]
    low, wide = jnp.bfloat16, jnp.float32
    wire = pltpu.VMEM((GROUP, SLOTS, WIRE), low)
    sems = pltpu.SemaphoreType.DMA
    return staged_call(
        experts_kernel,
        operands,
        [((TOTAL, D), low), ((TOTAL, D), low), ((2, count, D), low), ((count, D), wide), ((PAD, LANES), wide), ((D, D), low)],
        [pltpu.VMEM((4, 2, D, D), low)]
        + [wire] * 4
        + [pltpu.VMEM((4, HALF, D), low), pltpu.VMEM((HALF, D), wide), pltpu.VMEM((TOTAL, D), low)]
        + [sems((GROUP,))] * 4
        + [sems((4,))] * 4
        + [sems((4,))],
        (4,),
        (0, 1, 2, 3),
        raw=(6, 7),
        raw_out=(5,),
        collective_id=5,
        megabytes=25,
        name="experts_forward",
    )


def experts_back_kernel(
    staged, row_grad, total, chosen, gates, gate_probs, ids, rows, rows_y, target_row, target_column, vec, own, across_in, across_out,
    dtotal, dgate, sums, dhidden, kept, squared,
    weights, sends, lands, backs, returns, slope, dpre, act_own, act_set, dpre_set, rows_far, drows, result, dreturned,
    rows_t, drows_t, outward,
    forth_send, forth_recv, back_send, back_recv, weight_send, weight_recv, set_send, set_recv, local,
):
    at = place()
    me = lax.axis_index("exp")
    other, across_y_peer = meet_experts(at)
    near, far = load_experts(own, (across_in, across_out), weights, (weight_send, weight_recv), local, other)
    for copy in near:
        copy.start()
    count = total.shape[0]
    grad = jnp.concatenate([row_grad[tile : tile + 1, :] for tile in range(D // LANES)], axis=1) / PATCHES
    zero = jnp.zeros((1, D), jnp.float32)
    staged.need(1, 2, 5)

    def final_norm(index, carry):
        part = pl.ds(pl.multiple_of(index * CHUNK, CHUNK), CHUNK)
        back, gain, shift = norm_back(total[part, :], jnp.broadcast_to(grad, (CHUNK, D)), vec[8:9, :])
        dtotal[part, :] = back
        dgates = [
            jnp.sum(back * chosen[k, part, :].astype(jnp.float32), axis=-1, keepdims=True) for k in range(2)
        ]
        for k in range(2):
            outward[k, part, :] = (gates[part, k : k + 1] * back).astype(jnp.bfloat16)
        lane = iota((CHUNK, LANES), 1) - ROUTER_AT
        probs = gate_probs[part, :]
        dprobs = jnp.where(lane == ids[part, 0:1], dgates[0], 0.0) + jnp.where(
            lane == ids[part, 1:2], dgates[1], 0.0
        )
        inner = dprobs - jnp.sum(probs * dprobs, axis=-1, keepdims=True)
        dgate[part, :] = (probs * inner).astype(jnp.bfloat16)
        return carry[0] + gain, carry[1] + shift

    gain, shift = lax.fori_loop(0, count // CHUNK, final_norm, (zero, zero))
    sums[...] = jnp.concatenate([gain, shift, jnp.zeros((PAD - 2, D), jnp.float32)])
    slot = iota((TOTAL, count), 0)
    placed = [
        plain_dot((slot == target_row[k : k + 1, :]).astype(jnp.bfloat16), outward[k]) for k in range(2)
    ]
    placed = placed[0] + placed[1]
    pack(sends, placed[:MAIN], placed[MAIN:])
    met_experts()
    deal(sends, lands, (forth_send, forth_recv), True, 1, GROUP, start_copy)
    staged.need(6, 7)
    set_sems = (set_send, set_recv)
    moves = [remote(rows, rows_far.at[0], set_sems, 0, other), remote(rows_y, rows_far.at[1], set_sems, 1, other)]
    for copy in far + moves:
        copy.start()
    keep = pltpu.make_async_copy(sends.at[me], lands.at[0], local.at[3])
    keep.start()
    keep.wait()
    for copy in near:
        copy.wait()

    def tile_of(index):
        half, part = lax.div(index, 3), lax.rem(index, 3)
        columns = pl.ds(pl.multiple_of(part * 256, 256), 256)
        return pl.ds(pl.multiple_of(half * HALF, HALF), HALF), columns

    def gelu_both(value):
        tanh = gelu_tanh(value)
        grown = (0.5 * value * (1.0 + tanh)).astype(jnp.bfloat16)
        return grown, 0.5 * (1.0 + tanh) + 0.5 * value * (1.0 - tanh * tanh) * (
            GELU_SCALE * (1.0 + 3 * 0.044715 * (value * value))
        )

    def hidden_units(index, carry):
        quarter = lax.div(index, 6)
        lines, columns = tile_of(lax.rem(index, 6))
        grown, rate = gelu_both(plain_dot(rows[lines, :], weights[quarter, 0, :, columns]))

        @pl.when(quarter == 0)
        def _():
            act_own[lines, columns] = grown

        slope[quarter, lines, columns] = rate
        return carry

    lax.fori_loop(0, 12, hidden_units, 0)
    for copy in far:
        copy.wait_recv()
    lax.fori_loop(12, 24, hidden_units, 0)
    rows_t[...] = rows[...].T
    deal(sends, lands, (forth_send, forth_recv), True, 1, GROUP, wait_recv)
    unpack(lands, drows.at[0], 0, MAIN)
    moves.append(remote(drows.at[0], drows.at[1], set_sems, 2, across_y_peer))
    moves.append(remote(drows.at[0], drows.at[2], set_sems, 3, other))
    for copy in moves[2:]:
        copy.start()

    def hidden_back(index, carry):
        quarter = lax.div(index, 6)
        lines, columns = tile_of(lax.rem(index, 6))
        value = plain_dot(drows[0, lines, :], weights[quarter, 1, :, columns])
        dpre[quarter, lines, columns] = (value * slope[quarter, lines, columns]).astype(jnp.bfloat16)
        return carry

    lax.fori_loop(0, 24, hidden_back, 0)

    def inputs_back(index, carry):
        lines, columns = tile_of(index)
        value = over_last(dpre[0, lines, :], weights[0, 0, columns, :])
        for quarter in range(1, 4):
            value = value + over_last(dpre[quarter, lines, :], weights[quarter, 0, columns, :])
        result[lines, columns] = value
        return carry

    lax.fori_loop(0, 6, inputs_back, 0)
    pack(backs, result[:MAIN, :], result[MAIN:, :])
    deal(backs, returns, (back_send, back_recv), False, 1, GROUP, start_copy)
    keep = pltpu.make_async_copy(backs.at[0], returns.at[me], local.at[3])
    keep.start()

    def add_grads(given, down, act, first):
        drows_t[...] = drows[down].T
        if not first:
            rows_t[...] = given.T

        def step(index, carry):
            columns = pl.ds(pl.multiple_of(index * 256, 256), 256)
            inner = plain_dot(rows_t[...], (dpre.at[0] if first else dpre_set)[:, columns])
            outer = plain_dot(drows_t[...], act[:, columns])
            if first:
                kept[0, :, columns] = inner
                kept[1, :, columns] = outer
            else:
                kept[0, :, columns] = kept[0, :, columns] + inner
                kept[1, :, columns] = kept[1, :, columns] + outer
            return carry

        lax.fori_loop(0, 3, step, 0)

    def add_set(given, down):
        def step(index, carry):
            lines, columns = tile_of(index)
            grown, rate = gelu_both(plain_dot(given[lines, :], weights[0, 0, :, columns]))
            act_set[lines, columns] = grown
            value = plain_dot(drows[down, lines, :], weights[0, 1, :, columns])
            dpre_set[lines, columns] = (value * rate).astype(jnp.bfloat16)
            return carry

        lax.fori_loop(0, 6, step, 0)
        add_grads(given[...], down, act_set, False)

    add_grads(None, 0, act_own, True)
    for copy in (moves[0], moves[1], moves[3]):
        copy.wait_recv()
    add_set(rows_far.at[0], 2)
    moves[2].wait_recv()
    moves.append(remote(drows.at[1], drows.at[3], set_sems, 4, other))
    moves[4].start()
    keep.wait()
    deal(backs, returns, (back_send, back_recv), False, 1, GROUP, wait_recv)
    unpack(returns, dreturned, 0, MAIN)
    slot = iota((count, TOTAL), 1)
    placing = (slot == target_column[:, 0:1]) | (slot == target_column[:, 1:2])
    dhidden[...] = plain_dot(placing.astype(jnp.bfloat16), dreturned[...])
    add_set(rows_y, 1)
    moves[4].wait_recv()
    add_set(rows_far.at[1], 3)
    staged.give(4)
    squared[...] = jnp.zeros_like(squared)
    for which in range(2):
        square = kept[which] * kept[which]
        lines = jnp.broadcast_to(jnp.sum(square, axis=1, keepdims=True), (D, LANES)).T
        squared[which : which + 1, :] = lines[0:1]
        squared[2 + which : 3 + which, :] = jnp.sum(square, axis=0, keepdims=True)
    deal(sends, lands, (forth_send, forth_recv), True, 1, GROUP, wait_send)
    deal(backs, returns, (back_send, back_recv), False, 1, GROUP, wait_send)
    for copy in far + moves:
        copy.wait_send()


def experts_backward(*operands):
    count = operands[1].shape[0]
    low, wide = jnp.bfloat16, jnp.float32
    wire = pltpu.VMEM((GROUP, SLOTS, WIRE), low)
    shapes = [
        ((count, D), wide), ((count, LANES), low), ((PAD, D), wide),
        ((count, D), wide), ((2, D, D), wide), ((PAD, D), wide),
    ]
    sems = pltpu.SemaphoreType.DMA
    return staged_call(
        experts_back_kernel,
        operands,
        shapes,
        [pltpu.VMEM((4, 2, D, D), low)]
        + [wire] * 4
        + [pltpu.VMEM((4, TOTAL, D), wide), pltpu.VMEM((4, TOTAL, D), low)]
        + [pltpu.VMEM((TOTAL, D), low)] * 3
        + [pltpu.VMEM((2, TOTAL, D), low), pltpu.VMEM((4, TOTAL, D), low)]
        + [pltpu.VMEM((TOTAL, D), wide), pltpu.VMEM((TOTAL, D), low)]
        + [pltpu.VMEM((D, TOTAL), low)] * 2
        + [pltpu.VMEM((2, count, D), low)]
        + [sems((GROUP,))] * 4
        + [sems((3,))] * 2
        + [sems((5,))] * 2
        + [sems((4,))],
        (1, 2, 5, 6, 7),
        (4,),
        raw=(11, 12, 13),
        collective_id=8,
        megabytes=53,
        name="experts_backward",
    )


NEAR = tuple((y, core) for y in range(4) for core in range(2) if y or core)
PLANE = tuple((x, z) for x in range(4) for z in range(4) if x or z)


def near_peer(at, by):
    return moved(moved(at, "y", by[0]), "core", by[1])


def plane_peer(at, by):
    return moved(moved(at, "x", by[0]), "z", by[1])


def greet_all(at):
    barrier = pltpu.get_barrier_semaphore()
    peers = [near_peer(at, by) for by in NEAR] + [plane_peer(at, by) for by in PLANE]
    for peer in peers:
        pl.semaphore_signal(barrier, inc=1, device_id=device(peer), device_id_type=MESH)
    pl.semaphore_wait(barrier, len(peers))


def send_near(at, source, target, sems, first):
    copies = []
    for index, by in enumerate(NEAR):
        peer = near_peer(at, by)
        copies.append(remote(source(peer), target.at[at["y"], at["core"]], sems, first + index, peer))
        copies[-1].start()
    return copies


def head_kernel(
    staged, pool, head, labels, count,
    row_grad, head_grad, loss,
    near, every, pooled, pulls, got, summed, last, low, send, recv,
):
    at = place()
    sems = (send, recv)
    greet_all(at)
    copies = send_near(at, lambda peer: pool, near, sems, 0)
    near[at["y"], at["core"]] = pool[...]
    classes = head.shape[0]
    staged.need(1)
    spare = classes - classes % 16
    low[spare:, :] = jnp.zeros((low.shape[0] - spare, D), jnp.bfloat16)
    low[:classes, :] = head[...].astype(jnp.bfloat16)
    images = pooled.shape[0]
    number = (lax.axis_index("rep") * GROUP + lax.axis_index("exp")) * classes
    column = iota((images, low.shape[0]), 1)
    inside = column < classes
    column = jnp.where(inside, column + number, -2)
    hit = labels[:, 0:1] == column
    for slot in range(1, labels.shape[1]):
        hit = hit | (labels[:, slot : slot + 1] == column)
    targets = hit.astype(jnp.float32)
    valid = (jnp.max(labels[...], axis=1, keepdims=True) >= 0).astype(jnp.float32)
    for copy in copies:
        copy.wait()
    rows = near[:, 0] + near[:, 1]
    mine = every.at[:, at["x"], :, at["z"]]
    mine[...] = rows.astype(jnp.bfloat16).astype(jnp.float32).reshape(2, 2, PAD, LANES)
    copies = []
    for index, by in enumerate(PLANE):
        copies.append(remote(mine, mine, sems, 7 + index, plane_peer(at, by)))
        copies[-1].start()
    for copy in copies:
        copy.wait()
    for tile in range(D // LANES):
        lanes = slice(tile * LANES, (tile + 1) * LANES)
        pooled[:, lanes] = every[:, :, :, :, tile, :].reshape(images, LANES).astype(jnp.bfloat16)
    logits = over_last(pooled[...], low[...])
    soft = jnp.maximum(logits, 0.0) + jnp.log1p(jnp.exp(-jnp.abs(logits)))
    terms = jnp.where(inside, valid * (soft - targets * logits), 0.0)
    loss[...] = jnp.sum(jnp.sum(terms, axis=1, keepdims=True), axis=0, keepdims=True)
    sigmoid = 1.0 / (1.0 + jnp.exp(-logits))
    down = jnp.where(inside, valid * (sigmoid - targets) / count[...], 0.0)
    back = plain_dot(down.astype(jnp.bfloat16), low[...])
    pulls[...] = jnp.zeros_like(pulls)
    for tile in range(D // LANES):
        lanes = slice(tile * LANES, (tile + 1) * LANES)
        pulls[:, :, :, :, tile, :] = back[:, lanes].reshape(2, 4, 2, 4, LANES)
    copies = []
    for index, by in enumerate(PLANE):
        peer = plane_peer(at, by)
        source = pulls.at[:, peer["x"], :, peer["z"]]
        copies.append(remote(source, got.at[at["x"], at["z"]], sems, 22 + index, peer))
        copies[-1].start()
    got[at["x"], at["z"]] = pulls[:, at["x"], :, at["z"]]
    head_grad[...] = plain_dot(down.T.astype(jnp.bfloat16), pooled[...])
    for copy in copies:
        copy.wait()
    summed[...] = jnp.sum(got[...].reshape((16,) + summed.shape), axis=0)
    copies = send_near(at, lambda peer: summed.at[peer["y"]], last, sems, 37)
    last[at["y"], at["core"]] = summed[at["y"]]
    for copy in copies:
        copy.wait()
    row_grad[...] = jnp.sum(last[...].reshape((8,) + row_grad.shape), axis=0)


def head_step(pool, head, labels, count):
    images = labels.shape[0]
    classes = -(-head.shape[0] // LANES) * LANES
    wide = jnp.float32
    block = (PAD, LANES)
    sems = pltpu.SemaphoreType.DMA
    return staged_call(
        head_kernel,
        (pool, head, labels, count),
        [(block, wide), ((classes, D), wide), ((1, 1), wide)],
        [
            pltpu.VMEM((4, 2) + block, wide),
            pltpu.VMEM((2, 4, 2, 4) + block, wide),
            pltpu.VMEM((images, D), jnp.bfloat16),
            pltpu.VMEM((2, 4, 2, 4) + block, wide),
            pltpu.VMEM((4, 4, 2, 2) + block, wide),
            pltpu.VMEM((4,) + block, wide),
            pltpu.VMEM((4, 2) + block, wide),
            pltpu.VMEM((classes, D), jnp.bfloat16),
            sems((44,)),
            sems((44,)),
        ],
        (1,),
        (),
        collective_id=2,
        megabytes=16,
        name="head_step",
    )


def across_cores(value):
    return lax.ppermute(value, "rep", CORE_SWAP)


def across_y(value):
    return lax.ppermute(value, "rep", Y_SWAP)


def shards(
    patches,
    expert_ids,
    labels,
    label_count,
    square_weights,
    router_weight,
    position_table,
    head_weight,
    expert_weights,
    vector_params,
    square_rows,
    square_cols,
    router_rows,
    router_cols,
    position_rows,
    position_cols,
    head_rows,
    head_cols,
    expert_rows,
    expert_cols,
    vector_moment,
):
    bfloat = jnp.bfloat16
    num_rep = lax.axis_size("rep")
    num_exp = lax.axis_size("exp")
    rep_index = lax.axis_index("rep")
    my_image = lax.axis_index("exp")
    device_index = lax.axis_index(("rep", "exp"))
    micro, core = rep_index // 2, rep_index % 2
    num_expert = router_weight.shape[1]
    vocab_dev = head_weight.shape[1]
    ff_dev = expert_weights.shape[3]
    block = patches.shape[2]
    rows, width = 2 * block, patches.shape[3]
    num_top = expert_ids.shape[3]
    heads = width // HEAD
    scale = HEAD ** (-0.5)
    own_rows = square_weights.shape[1]

    gap = jnp.zeros((own_rows, 6), jnp.float32)
    extra = jnp.concatenate(
        [position_table.T, router_weight, vector_params.T, gap, vector_params.T], axis=1
    )
    extra = jnp.pad(extra, ((0, 0), (0, width - extra.shape[1])))
    valid = (label_count > 0).astype(jnp.float32)
    image_count = jnp.sum(valid)
    live = jnp.arange(labels.shape[2], dtype=jnp.int32) < label_count[:, :, None]
    live_labels = jnp.where(live, labels, -1).reshape(2 * num_exp, -1)

    wide_ids = jnp.pad(expert_ids.reshape(2, block, num_top), ((0, 0), (0, 0), (0, LANES - num_top)))
    *squares, extra, low, patch_rows, ids, quarter = gather_all(
        square_weights, extra, patches.reshape(2, block, width), wide_ids, expert_weights[0]
    )
    patch_rows, ids = patch_rows.reshape(rows, width), ids.reshape(rows, LANES)

    across_in = across_y(quarter[0])
    (
        embed, hidden_one, query, keys, values, mixed, after_attn, hidden_two,
        gate_probs, gates, lse, vectors, router, target, target_t, hidden_kept, *squares,
    ) = attend(patch_rows, squares, extra, low, ids)
    across_in, hidden_two = lax.optimization_barrier((across_in, hidden_two))
    received, received_y, chosen, after_moe, pool, across_out = experts_forward(
        hidden_two, target_t, target, gates, after_attn, vectors, quarter, across_in
    )
    row_grad, head_g, loss_part = head_step(
        pool, head_weight.T, live_labels, image_count.reshape(1, 1)
    )
    dmoe_in, dgate_logits, final_sums, dhidden, expert_g, expert_squared = experts_backward(
        row_grad, after_moe, chosen, gates, gate_probs, ids, received, received_y,
        target_t, target, vectors, quarter, across_in, across_out,
    )
    dafter_low, dquery_low, dkey_low, dvalue_low, dembed_low, sums = attend_back(
        dmoe_in,
        dhidden,
        dgate_logits,
        embed,
        after_attn,
        query,
        keys,
        values,
        lse,
        *squares,
        vectors,
        router,
    )
    *owned, totals = shared_gradients(
        patch_rows, hidden_one, mixed, dembed_low, dquery_low, dkey_low, dvalue_low, dafter_low,
        hidden_kept, dgate_logits, sums, final_sums, head_g, expert_squared, loss_part, square_rows, router_rows[None],
    )
    head_g = head_g[:vocab_dev].T
    expert_g = expert_g[None]
    owned = [half for part in owned for half in (part[:own_rows], part[PAD : PAD + own_rows])]
    square_g = jnp.stack(owned[:5])
    extra_g = owned[5]
    second = 3 * LANES
    few_at = EXTRA + num_expert
    vector_at = EXTRA + 96

    def positions(value):
        return jnp.concatenate(
            [value[:, start : start + block] for start in (0, second, block, second + block)], axis=1
        )

    table_g = positions(extra_g).T
    router_g = extra_g[:, few_at : few_at + num_expert]
    vector_g = extra_g[:, vector_at : vector_at + 10].T
    square_rowmean = jnp.mean(square_g * square_g, axis=2)
    router_rowmean = jnp.mean(router_g * router_g, axis=1)
    loss_total = totals[7, 0]
    norm_total = jnp.sum(totals[:7]) + totals[7, 1]
    square_colsq = totals[:5]
    square_rows_sum = totals[7, 2:7]
    square_mean_sum = jnp.mean(square_colsq, axis=1)
    router_colsq = totals[6, few_at : few_at + num_expert]
    router_rows_sum = totals[7, 7]
    router_mean_sum = jnp.sum(router_colsq) / num_expert
    table_rowsq = positions(totals[6:7])[0]
    head_rowsq = totals[5]
    expert_mine = totals[8:10][None]
    expert_colmean = (expert_squared[2:4] / width)[None]
    grad_norm = jnp.sqrt(norm_total)
    clip = jnp.minimum(1.0, CLIP_NORM / grad_norm)
    clip_sq = clip * clip
    keep = 1.0 - DECAY
    square_clip = clip * square_g
    square_rows_next = DECAY * square_rows + keep * (clip_sq * square_rowmean + EPS_SQ)
    square_cols_next = DECAY * square_cols + keep * (clip_sq * square_colsq / width + EPS_SQ)
    square_mean = (
        DECAY * square_rows_sum + keep * (clip_sq * square_mean_sum + width * EPS_SQ)
    ) / width
    square_rate = jnp.array([1.0, 1.0, 1.0, 1.0, 4.0], jnp.float32)[:, None, None] * (
        0.3 / math.sqrt(D)
    )
    square_next = factored_step(
        square_weights,
        square_clip,
        square_rows_next,
        square_cols_next,
        square_mean[:, None, None],
        square_rate,
    )
    router_clip = clip * router_g
    router_rows_next = DECAY * router_rows + keep * (clip_sq * router_rowmean + EPS_SQ)
    router_cols_next = DECAY * router_cols + keep * (clip_sq * router_colsq / width + EPS_SQ)
    router_mean = (
        DECAY * router_rows_sum + keep * (clip_sq * router_mean_sum + width * EPS_SQ)
    ) / width
    router_next = factored_step(
        router_weight,
        router_clip,
        router_rows_next,
        router_cols_next,
        router_mean,
        0.2 / math.sqrt(D),
    )
    table_clip = clip * table_g
    table_rows_next = DECAY * position_rows + keep * (clip_sq * table_rowsq / width + EPS_SQ)
    table_cols_next = DECAY * position_cols + keep * (
        clip_sq * jnp.mean(table_g * table_g, axis=0) + EPS_SQ
    )
    table_next = factored_step(
        position_table,
        table_clip,
        table_rows_next,
        table_cols_next,
        jnp.mean(table_rows_next),
        0.15,
    )
    head_clip = clip * head_g
    head_rows_next = DECAY * head_rows + keep * (
        clip_sq * head_rowsq / (vocab_dev * num_rep * num_exp) + EPS_SQ
    )
    head_cols_next = DECAY * head_cols + keep * (
        clip_sq * jnp.mean(head_g * head_g, axis=0) + EPS_SQ
    )
    head_next = factored_step(
        head_weight,
        head_clip,
        head_rows_next,
        head_cols_next,
        jnp.mean(head_rows_next),
        0.5 / math.sqrt(D),
    )
    expert_clip = clip * expert_g
    expert_rows_next = DECAY * expert_rows + keep * (
        clip_sq * expert_mine / (ff_dev * num_rep) + EPS_SQ
    )
    expert_cols_next = DECAY * expert_cols + keep * (
        clip_sq * expert_colmean + EPS_SQ
    )
    expert_rate = jnp.array([0.3 / math.sqrt(D), 4.8 / math.sqrt(FF)], jnp.float32)[
        None, :, None, None
    ]
    expert_next = factored_step(
        expert_weights,
        expert_clip,
        expert_rows_next,
        expert_cols_next,
        jnp.mean(expert_rows_next, axis=-1)[..., None, None],
        expert_rate,
    )
    vector_clip = clip * vector_g
    moment_next = DECAY * vector_moment + keep * (vector_clip * vector_clip + EPS_SQ)
    vector_next = vector_params - 0.3 * vector_clip * lax.rsqrt(moment_next)
    return (
        loss_total,
        image_count,
        grad_norm,
        square_clip,
        square_rows_next,
        square_cols_next,
        square_next,
        router_clip,
        router_rows_next,
        router_cols_next,
        router_next,
        table_clip,
        table_rows_next,
        table_cols_next,
        table_next,
        head_clip,
        head_rows_next,
        head_cols_next,
        head_next,
        expert_clip,
        expert_rows_next,
        expert_cols_next,
        expert_next,
        vector_clip,
        moment_next,
        vector_next,
    )


def solution(mesh):
    in_specs = (
        P(None, "exp", "rep", None),
        P(None, "exp", "rep", None),
        P(),
        P(),
        P(None, ("rep", "exp"), None),
        P(("rep", "exp"), None),
        P(None, ("rep", "exp")),
        P(None, ("rep", "exp")),
        P("exp", None, None, "rep"),
        P(None, ("rep", "exp")),
        P(None, ("rep", "exp")),
        P(),
        P(("rep", "exp")),
        P(),
        P(),
        P(("rep", "exp")),
        P(),
        P(("rep", "exp")),
        P("exp", None, None),
        P("exp", None, "rep"),
        P(None, ("rep", "exp")),
    )
    out_specs = (
        P(),
        P(),
        P(),
        P(None, ("rep", "exp"), None),
        P(None, ("rep", "exp")),
        P(),
        P(None, ("rep", "exp"), None),
        P(("rep", "exp"), None),
        P(("rep", "exp")),
        P(),
        P(("rep", "exp"), None),
        P(None, ("rep", "exp")),
        P(),
        P(("rep", "exp")),
        P(None, ("rep", "exp")),
        P(None, ("rep", "exp")),
        P(),
        P(("rep", "exp")),
        P(None, ("rep", "exp")),
        P("exp", None, None, "rep"),
        P("exp", None, None),
        P("exp", None, "rep"),
        P("exp", None, None, "rep"),
        P(None, ("rep", "exp")),
        P(None, ("rep", "exp")),
        P(None, ("rep", "exp")),
    )
    return jax.shard_map(shards, mesh=mesh, in_specs=in_specs, out_specs=out_specs, check_vma=False)
```

```python
import functools
import math

import jax
import jax.numpy as jnp
from jax import lax
from jax.experimental import pallas as pl
from jax.experimental.pallas import tpu as pltpu
from jax.sharding import PartitionSpec as P

D = 768
HEAD = 64
FF = 3072
PATCHES = 576
CAP = 10
VOCAB_DEV = 171
EARLY = 256
EXTRA = 640
VECTOR_AT = 608
ROUTER_AT = 64
PAD = 8
LANES = 128


DECAY = 0.8
EPS_SQ = 1e-30
CLIP_NORM = 0.25
HIGHEST = lax.Precision.HIGHEST
MESH = pl.DeviceIdType.MESH

Y_SWAP = ((0, 2), (1, 3), (2, 0), (3, 1))
CORE_SWAP = ((0, 1), (1, 0), (2, 3), (3, 2))


def plain_dot(left, right):
    return jnp.dot(left, right, preferred_element_type=jnp.float32)


def over_rows(left, right):
    return lax.dot_general(
        left, right, (((0,), (0,)), ((), ())), preferred_element_type=jnp.float32
    )


def over_last(left, right):
    return lax.dot_general(
        left, right, (((1,), (1,)), ((), ())), preferred_element_type=jnp.float32
    )


def place():
    rep = lax.axis_index("rep")
    line = lax.axis_index("exp")
    y = lax.div(rep, 2) * 2 + lax.rem(lax.div(line, 4), 2)
    return {"y": y, "core": lax.rem(rep, 2), "x": lax.div(line, 8), "z": lax.rem(line, 4)}


def device(at):
    return {
        "rep": lax.div(at["y"], 2) * 2 + at["core"],
        "exp": at["x"] * 8 + lax.rem(at["y"], 2) * 4 + at["z"],
    }


def moved(at, axis, by):
    return {**at, axis: lax.rem(at[axis] + by, 2 if axis == "core" else 4)}


def box(ref, at, free, core=False):
    whole = slice(None)
    hi = whole if "y" in free else lax.div(at["y"], 2)
    low = whole if "y" in free else lax.rem(at["y"], 2)
    x = whole if "x" in free else at["x"]
    z = whole if "z" in free else at["z"]
    if core:
        return ref.at[hi, at["core"], x, low, z]
    return ref.at[hi, x, low, z]


NEAR = tuple((y, core) for y in range(4) for core in range(2) if y or core)
PLANE = tuple((x, z) for x in range(4) for z in range(4) if x or z)


def near_peer(at, by):
    return moved(moved(at, "y", by[0]), "core", by[1])


def greet(at, near=False):
    barrier = pltpu.get_barrier_semaphore()
    peers = [moved(at, axis, by) for axis in ("x", "z") for by in (1, 2, 3)]
    peers += [near_peer(at, by) for by in NEAR if near or not (by[0] and by[1])]
    for peer in peers:
        pl.semaphore_signal(barrier, inc=1, device_id=device(peer), device_id_type=MESH)
    pl.semaphore_wait(barrier, len(peers))


def remote(src, dst, sems, index, peer):
    return pltpu.make_async_remote_copy(
        src_ref=src,
        dst_ref=dst,
        send_sem=sems[0].at[index],
        recv_sem=sems[1].at[index],
        device_id=device(peer),
        device_id_type=MESH,
    )


class Staged:
    def __init__(self, inputs, outputs):
        self.inputs, self.outputs, self.given = inputs, outputs, []

    def need(self, *indices):
        for index in indices:
            self.inputs[index].wait()

    def give(self, *indices):
        for index in indices:
            self.outputs[index].start()
            self.given.append(self.outputs[index])


def pin(value):
    return pltpu.with_memory_space_constraint(value, pltpu.HBM)


def staged_call(body, operands, shapes, scratch, far_in, far_out, **params):
    inputs, outputs = len(operands), len(shapes)
    raw, raw_out = params.pop("raw", ()), params.pop("raw_out", ())

    def kernel(*refs):
        refs = list(refs)
        stages = refs[inputs + outputs + len(scratch) :]
        stage_in, stages = stages[: len(far_in)], stages[len(far_in) :]
        stage_out, (sem_in, sem_out) = stages[: len(far_out)], stages[len(far_out) :]
        fetches, stores = {}, {}
        for number, index in enumerate(far_in):
            fetches[index] = pltpu.make_async_copy(refs[index], stage_in[number], sem_in.at[number])
            fetches[index].start()
            refs[index] = stage_in[number]
        for number, index in enumerate(far_out):
            stores[index] = pltpu.make_async_copy(stage_out[number], refs[inputs + index], sem_out.at[number])
            refs[inputs + index] = stage_out[number]
        staged = Staged(fetches, stores)
        body(staged, *refs[: inputs + outputs + len(scratch)])
        for copy in staged.given:
            copy.wait()

    anywhere, near = pl.BlockSpec(memory_space=pl.ANY), pl.BlockSpec(memory_space=pltpu.VMEM)
    return pl.pallas_call(
        kernel,
        out_shape=[
            pltpu.HBM(*shape) if index in far_out + raw_out else jax.ShapeDtypeStruct(*shape)
            for index, shape in enumerate(shapes)
        ],
        in_specs=[anywhere if index in far_in or index in raw else near for index in range(inputs)],
        out_specs=[anywhere if index in far_out + raw_out else near for index in range(outputs)],
        scratch_shapes=list(scratch)
        + [pltpu.VMEM(operands[index].shape, operands[index].dtype) for index in far_in]
        + [pltpu.VMEM(*shapes[index]) for index in far_out]
        + [pltpu.SemaphoreType.DMA((max(1, len(far_in)),)), pltpu.SemaphoreType.DMA((max(1, len(far_out)),))],
        compiler_params=pltpu.CompilerParams(
            collective_id=params["collective_id"],
            has_side_effects=True,
            vmem_limit_bytes=params["megabytes"] * 2**20,
        ),
        name=params["name"],
    )(*(pin(value) if index in far_in or index in raw else value for index, value in enumerate(operands)))


ORDERS = (("x", "y", "z"), ("y", "z", "x"), ("z", "x", "y"))


def gather_kernel(own_squares, own_extra, patches, ids, experts, *refs):
    squares, extra, spare, image, image_ids, experts_low, experts_in, across_part = refs[:5], *refs[5:12]
    outs, (x_ref, wide, narrow, send, recv, local, local_in, local_out) = refs[12:15], refs[15:]
    at = place()
    sems = (send, recv)
    value = own_extra[...]
    high = value.astype(jnp.bfloat16).astype(jnp.float32)
    lane = lax.broadcasted_iota(jnp.int32, value.shape, 1)
    rest = jnp.where(lane < PATCHES, value - high, 0.0)
    high = jnp.where(lane >= VECTOR_AT + 16, value - high, high)
    blank = jnp.zeros((2, D), jnp.float32)
    for part, rows in enumerate(
        (
            (own_squares[0], rest[0:2], own_squares[1], rest[2:4]),
            (own_squares[2], rest[4:6], own_squares[3], blank),
            (own_squares[4], blank, high, blank),
        )
    ):
        x_ref[part] = jnp.concatenate(rows).astype(jnp.bfloat16)
    own = []
    for part in range(3):
        own.append(
            pltpu.make_async_copy(
                x_ref.at[part], box(outs[part], at, (), True), local.at[part]
            )
        )
        own[part].start()
    micro = lax.div(at["y"], 2)
    kept = [
        pltpu.make_async_copy(patches.at[micro], image.at[micro], local.at[3]),
        pltpu.make_async_copy(ids.at[micro], image_ids.at[micro], local.at[4]),
    ]
    for copy in kept:
        copy.start()

    def lines(ref, step):
        return ref.at[step // 3, pl.ds(step % 3 * 256, 256)]

    def fetch(step):
        return pltpu.make_async_copy(lines(experts, step), wide.at[step % 2], local_in.at[step % 2])

    def store(step):
        return pltpu.make_async_copy(narrow.at[step % 2], lines(experts_low, step), local_out.at[step % 2])

    def store_in(step):
        lines_in = experts_in.at[pl.ds(step % 3 * 256, 256)]
        return pltpu.make_async_copy(narrow.at[step % 2], lines_in, local_out.at[2 + step % 2])

    def round_experts(step):
        if step < 5:
            fetch(step + 1).start()
        fetch(step).wait()
        if step >= 2:
            store(step - 2).wait()
            if step < 5:
                store_in(step - 2).wait()
        narrow[step % 2] = wide[step % 2].astype(jnp.bfloat16)
        store(step).start()
        if step < 3:
            store_in(step).start()

    fetch(0).start()
    greet(at)
    flights = {}

    def launch(part, stage):
        axes = ORDERS[part]
        view = box(outs[part], at, axes[:stage], True)
        source = x_ref.at[part] if stage == 0 else view
        for by in (1, 2, 3):
            copy = remote(source, view, sems, part * 13 + stage * 3 + by - 1, moved(at, axes[stage], by))
            copy.start()
            flights[part, stage, by] = copy

    def forward(part, by):
        axes = ORDERS[part]
        view = box(outs[part], moved(at, axes[2], 4 - by), axes[:2], True)
        copy = remote(view, view, sems, part * 13 + 9 + by, moved(at, "core", 1))
        copy.start()
        flights[part, 3, by] = copy

    for part in range(3):
        launch(part, 0)
    trades = [
        remote(patches.at[1 - micro], image.at[micro], sems, 39, moved(at, "y", 2)),
        remote(ids.at[1 - micro], image_ids.at[micro], sems, 40, moved(at, "y", 2)),
    ]
    for copy in trades:
        copy.start()
    round_experts(0)
    round_experts(1)
    for stage in (1, 2):
        for part in range(3):
            if stage == 1:
                own[part].wait()
            for by in (1, 2, 3):
                flights[part, stage - 1, by].wait_recv()
            launch(part, stage)
            if stage == 2:
                forward(part, 0)
        round_experts(2 * stage)
        round_experts(2 * stage + 1)
    store(4).wait()
    store(5).wait()
    for by in (1, 3, 2):
        for part in range(3):
            flights[part, 2, by].wait_recv()
            forward(part, by)
    early = remote(experts_low.at[1, pl.ds(0, EARLY)], across_part, sems, 41, moved(at, "y", 2))
    early.start()

    row = lax.broadcasted_iota(jnp.int32, (96, 256), 0)
    column = lax.broadcasted_iota(jnp.int32, (96, 256), 1)
    base = lax.div(row, 6) * 16
    inside = lax.rem(row, 6)

    def packer(offset):
        return (column == base + offset + inside).astype(jnp.bfloat16)

    first, second = packer(0), packer(8)
    low_first = jnp.where(inside < 2, packer(6), jnp.where(inside < 4, packer(12), 0)).astype(jnp.bfloat16)
    low_second = jnp.where(inside < 4, 0, packer(2)).astype(jnp.bfloat16)
    packers = [
        jnp.concatenate([first, second, low_first]),
        jnp.concatenate([first, second, low_second]),
        jnp.concatenate([first, second]),
    ]

    def pack(core):
        def step(index, carry):
            high, half = lax.div(index, 2), lax.rem(index, 2)
            place_out = pl.ds(pl.multiple_of((high * 4 + core * 2 + half) * 96, 96), 96)
            packed = []
            for part in range(3):
                block = outs[part][high, core, pl.ds(half * 2, 2)].reshape(256, D)
                packed.append(plain_dot(packers[part], block))
            for k in range(5):
                low = packed[k // 2][96 * (k % 2) : 96 * (k % 2) + 96]
                squares[k][place_out, :] = low.astype(jnp.bfloat16)
            extra[place_out, :] = packed[2][96:].astype(jnp.bfloat16)
            spare[place_out, :] = (packed[0][192:] + packed[1][192:]).astype(jnp.bfloat16)
            return carry

        lax.fori_loop(0, 4, step, 0)

    pack(at["core"])
    for key, copy in flights.items():
        if key[1] == 3:
            copy.wait_recv()
    pack(1 - at["core"])
    for copy in [*kept, *trades, early]:
        copy.wait()
    for copy in flights.values():
        copy.wait_send()


def gather_all(squares, extra, patches, ids, experts):
    shape = (2, 2, 4, 2, 4, 16, D)
    return pl.pallas_call(
        gather_kernel,
        out_shape=[jax.ShapeDtypeStruct((D, D), jnp.bfloat16)] * 7
        + [pltpu.HBM(value.shape, value.dtype) for value in (patches, ids)]
        + [pltpu.HBM(experts.shape, jnp.bfloat16), pltpu.HBM(experts.shape[1:], jnp.bfloat16)]
        + [pltpu.HBM((EARLY, D), jnp.bfloat16)],
        in_specs=[pl.BlockSpec(memory_space=pltpu.VMEM)] * 2 + [pl.BlockSpec(memory_space=pl.ANY)] * 3,
        out_specs=[pl.BlockSpec(memory_space=pltpu.VMEM)] * 7 + [pl.BlockSpec(memory_space=pl.ANY)] * 5,
        scratch_shapes=[pltpu.VMEM(shape, jnp.bfloat16)] * 3
        + [
            pltpu.VMEM((3, 16, D), jnp.bfloat16),
            pltpu.VMEM((2, 256, D), jnp.float32),
            pltpu.VMEM((2, 256, D), jnp.bfloat16),
            pltpu.SemaphoreType.DMA((42,)),
            pltpu.SemaphoreType.DMA((42,)),
            pltpu.SemaphoreType.DMA((5,)),
            pltpu.SemaphoreType.DMA((2,)),
            pltpu.SemaphoreType.DMA((4,)),
        ],
        compiler_params=pltpu.CompilerParams(
            collective_id=0, has_side_effects=True, vmem_limit_bytes=24 * 2**20
        ),
        name="gather_weights",
    )(squares, extra, pin(patches), pin(ids), pin(experts))


def gradients_kernel(
    staged, patches, hidden_one, mixed, dembed, dquery, dkey, dvalue, dafter, hidden_two, dgate, sums, final_sums,
    head_grad, loss, square_rows, router_rows, part_grads, own, rows_y, rows_last, drows_y, drows_last, *refs,
):
    outs, totals, kept, expert_cols, refs = refs[:3], refs[3], refs[4], refs[5], refs[3:]
    lefts, tables, rights, left_got, table_got, right_got, few_mine, few_got, few_t, partial, grads = refs[3:14]
    first, total_one, second, total_two, third = (refs[14 + 3 * i : 17 + 3 * i] for i in range(5))
    core_sems, sems = refs[29:31], refs[31:33]
    parts, total_sems, (act_set, dpre_set, rows_t, drows_t) = refs[33], refs[34:36], refs[36:40]
    at = place()
    other = moved(at, "core", 1)
    count = patches.shape[0]
    part_rows = D // 4
    staged.need(3, 4, 5, 6, 7)
    for index, ref in enumerate((dembed, dquery, dkey, dvalue, dafter)):
        rights[index] = ref[...]
    greet(at, near=True)
    copies = [remote(rights, right_got, core_sems, 0, other)]
    copies[0].start()
    staged.need(0, 1, 2, 8)
    for index, ref in enumerate((patches, hidden_one, mixed)):
        lefts[index] = ref[...].T.reshape(4, part_rows, count)
    padded = jnp.concatenate([dembed[...], jnp.zeros((3 * LANES - count, D), jnp.bfloat16)])
    tables[...] = padded.T.reshape(4, part_rows, 3 * LANES)
    for half in range(2):
        source = lefts.at[:, 2 * half + other["core"]]
        copies.append(remote(source, left_got.at[:, half], core_sems, 1 + half, other))
        source = tables.at[2 * half + other["core"]]
        copies.append(remote(source, table_got.at[half], core_sems, 3 + half, other))
    few_mine[:32, :] = plain_dot(dgate[...].T, hidden_two[...])[64:96]
    few_mine[32:40, :] = sums[...]
    few_mine[40:48, :] = final_sums[...]
    copies.append(remote(few_mine, few_got, core_sems, 5, other))
    for copy in copies[1:]:
        copy.start()

    pairs = ((0, 0), (1, 1), (1, 2), (1, 3), (2, 4))

    def own_product(half, carry):
        rows = 2 * half + at["core"]
        for index, (left, right) in enumerate(pairs):
            partial[index, half] = plain_dot(lefts[left, rows], rights[right])
        return carry

    lax.fori_loop(0, 2, own_product, 0)
    for copy in copies:
        copy.wait_recv()
    few = few_mine[...] + few_got[...]
    few_high = few.astype(jnp.bfloat16)
    few_low = (few - few_high.astype(jnp.float32)).astype(jnp.bfloat16)
    blank = jnp.zeros((32, D), jnp.bfloat16)
    few_rows = jnp.concatenate([blank, few_high[:32], few_low[:32], few_high[32:], few_low[32:]])
    few_t[...] = few_rows.T.reshape(4, part_rows, LANES)

    def spread(offset):
        shape = (part_rows // 6 * 2 * PAD, part_rows)
        row, column = iota(shape, 0), iota(shape, 1)
        inside = lax.rem(row, 2 * PAD) - offset
        hit = (inside >= 0) & (inside < 6) & (column == lax.div(row, 2 * PAD) * 6 + inside)
        return hit.astype(jnp.bfloat16)

    spreads = jnp.concatenate([spread(0), spread(PAD)], axis=1)

    def finish(part, half):
        rows = 2 * half + at["core"]
        pieces = []
        for index in (2 * part, 2 * part + 1):
            if index < 5:
                left, right = pairs[index]
                value = partial[index, half] + plain_dot(left_got[left, half], right_got[right])
                pieces.append(value.astype(jnp.bfloat16))
            else:
                mine, theirs = tables[rows], table_got[half]
                is_first = at["core"] == 0
                low = jnp.where(is_first, mine, theirs)
                high = jnp.where(is_first, theirs, mine)
                high = jnp.concatenate(
                    [high[:, : 2 * LANES], high[:, 2 * LANES :] + few_t[rows]], axis=1
                )
                pieces.append(jnp.concatenate([low, high], axis=1))
        value = plain_dot(spreads, jnp.concatenate(pieces)).astype(jnp.bfloat16)
        grads[part, half] = value.reshape(4, 2, 4, 2 * PAD, D)

    def names(axis):
        return ("h", "l") if axis == "y" else (axis,)

    def pick(letter, where, axis):
        if letter not in names(axis):
            return slice(None)
        if letter == "h":
            return lax.div(where["y"], 2)
        if letter == "l":
            return lax.rem(where["y"], 2)
        return where[axis]

    def part_of(source, where, axes, stage):
        if stage == 0:
            return box(source, where, axes[:2])
        if stage == 1:
            left = [letter for letter in ("h", "x", "l", "z") if letter not in names(axes[2])]
            return source.at[tuple(pick(letter, where, axes[1]) for letter in left)]
        return source.at[tuple(pick(letter, where, axes[0]) for letter in names(axes[0]))]

    sources = ([grads.at[part] for part in range(3)], total_one, total_two)
    landings = (first, second, third)
    targets = (total_one, total_two, outs)
    flights = {}

    def launch(part, stage):
        axes = ORDERS[part]
        axis = axes[2 - stage]
        flights[part, stage] = []
        for by in (1, 2, 3):
            peer = moved(at, axis, by)
            view = part_of(sources[stage][part], peer, axes, stage)
            copy = remote(view, landings[stage][part].at[by - 1], sems, part * 9 + stage * 3 + by - 1, peer)
            copy.start()
            flights[part, stage].append(copy)

    for part in (2, 0, 1):
        for half in range(2):
            finish(part, half)
        launch(part, 0)
    head_squared = jnp.sum(head_grad[...] * head_grad[...], axis=0, keepdims=True)

    staged.need(16, 17, 18, 19, 20, 21)
    for which in range(2):
        kept[which] = part_grads[which]
    quarter_set(kept, own, rows_y, drows_y, act_set, dpre_set, rows_t, drows_t)
    for stage in range(3):
        if stage == 1:
            quarter_set(kept, own, rows_last, drows_last, act_set, dpre_set, rows_t, drows_t)
            staged.give(4)
            expert_rows = []
            for which in range(2):
                square = kept[which] * kept[which]
                expert_rows.append(jnp.broadcast_to(jnp.sum(square, axis=1, keepdims=True), (D, LANES)).T[0:1])
                expert_cols[which : which + 1, :] = jnp.sum(square, axis=0, keepdims=True)
            expert_rows = jnp.concatenate(expert_rows)
            expert_norm = jnp.sum(jnp.sum(expert_rows, axis=1, keepdims=True), axis=0, keepdims=True)
        for part in (2, 0, 1):
            for copy in flights[part, stage]:
                copy.wait_recv()
            landing = landings[stage][part]
            terms = [part_of(sources[stage][part], at, ORDERS[part], stage)[...]]
            terms = [term.astype(jnp.float32) for term in terms + [landing[i] for i in range(3)]]
            target = targets[stage][part]
            target[...] = ((terms[0] + terms[1]) + (terms[2] + terms[3])).astype(target.dtype)
            if stage < 2:
                launch(part, stage + 1)

    tail = outs[2][PAD:, EXTRA:]
    lane = iota(tail.shape, 1)
    router = tail + pltpu.roll(tail, LANES - GROUP, 1)
    vectors = tail + pltpu.roll(tail, LANES - 16, 1)
    tail = jnp.where(lane < 32, tail, jnp.where(lane < 64, router, jnp.where((lane >= 96) & (lane < 112), vectors, 0.0)))
    outs[2][PAD:, EXTRA:] = tail
    squared = [outs[k // 2][PAD * (k % 2) : PAD * (k % 2) + PAD, :] for k in range(6)]
    squared = [jnp.sum(value * value, axis=0, keepdims=True) for value in squared]
    spot = iota((1, D), 1)
    last = jnp.where(spot == 1, expert_norm, 0.0) + jnp.where(spot == 0, loss[...], 0.0)
    for k in range(5):
        last = last + jnp.where(spot == 2 + k, jnp.sum(square_rows[k : k + 1, :], axis=1, keepdims=True), 0.0)
    last = last + jnp.where(spot == 7, jnp.sum(router_rows[...], axis=1, keepdims=True), 0.0)
    parts[0, 0] = jnp.concatenate(squared[:5] + [head_squared, squared[5], last])
    parts[0, 1] = jnp.concatenate([expert_rows, jnp.zeros((PAD - 2, D), jnp.float32)])
    mine = parts.at[0]
    trips = []
    for number, by in enumerate(NEAR):
        whole = by[0] in (0, 2)
        slot = parts.at[1 + at["y"] * 2 + at["core"]]
        source, target = (mine, slot) if whole else (mine.at[0], slot.at[0])
        trips.append(remote(source, target, total_sems, number, near_peer(at, by)))
        trips[-1].start()
    parts[1 + at["y"] * 2 + at["core"]] = mine[...]
    for trip in trips:
        trip.wait()
    value = parts[1, 0]
    for index in range(1, 8):
        value = value + parts[1 + index, 0]
    parts[9, 0] = value
    low = lax.rem(at["y"], 2) * 2
    totals[PAD:, :] = (parts[1 + low, 1] + parts[2 + low, 1]) + (parts[5 + low, 1] + parts[6 + low, 1])
    total = parts.at[9]
    for stage, axis in enumerate(("z", "x")):
        base = 10 + 5 * stage
        trips = []
        for by in (1, 2, 3):
            number = 7 + 3 * stage + by - 1
            slot = parts.at[base + at[axis], 0]
            trips.append(remote(total.at[0], slot, total_sems, number, moved(at, axis, by)))
            trips[-1].start()
        parts[base + at[axis], 0] = total[0]
        for trip in trips:
            trip.wait()
        value = parts[base, 0]
        for index in range(1, 4):
            value = value + parts[base + index, 0]
        parts[base + 4, 0] = value
        total = parts.at[base + 4]
    totals[:PAD, :] = total[0]
    for copy in copies:
        copy.wait_send()
    for launched in flights.values():
        for copy in launched:
            copy.wait_send()


def shared_gradients(*operands):
    count = operands[0].shape[0]
    low, wide = jnp.bfloat16, jnp.float32
    block = (2 * PAD, D)
    ones = [{"x": (2, 2, 4), "y": (4, 4), "z": (2, 4, 2)}[axes[2]] for axes in ORDERS]
    twos = [(2, 2) if axes[0] == "y" else (4,) for axes in ORDERS]
    rows = D // 4
    scratch = [
        pltpu.VMEM((3, 4, rows, count), low),
        pltpu.VMEM((4, rows, 3 * LANES), low),
        pltpu.VMEM((5, count, D), low),
        pltpu.VMEM((3, 2, rows, count), low),
        pltpu.VMEM((2, rows, 3 * LANES), low),
        pltpu.VMEM((5, count, D), low),
        pltpu.VMEM((48, D), wide),
        pltpu.VMEM((48, D), wide),
        pltpu.VMEM((4, rows, LANES), low),
        pltpu.VMEM((5, 2, rows, D), wide),
        pltpu.VMEM((3, 2, 4, 2, 4) + block, low),
    ]
    scratch += [pltpu.VMEM((3,) + one + block, low) for one in ones]
    scratch += [pltpu.VMEM(one + block, kind) for one, kind in zip(ones, (low, low, wide))]
    scratch += [pltpu.VMEM((3,) + two + block, kind) for two, kind in zip(twos, (low, low, wide))]
    scratch += [pltpu.VMEM(two + block, wide) for two in twos]
    scratch += [pltpu.VMEM((3,) + block, wide)] * 3
    scratch += [pltpu.SemaphoreType.DMA((6,))] * 2 + [pltpu.SemaphoreType.DMA((27,))] * 2
    scratch += [pltpu.VMEM((20, 2, PAD, D), wide)] + [pltpu.SemaphoreType.DMA((13,))] * 2
    scratch += [pltpu.VMEM((TOTAL, D), low)] * 2 + [pltpu.VMEM((D, TOTAL), low)] * 2
    return staged_call(
        gradients_kernel,
        operands,
        [(block, wide)] * 4 + [((2, D, D), wide), ((2, D), wide)],
        scratch,
        (3, 4, 5, 6, 7, 0, 1, 2, 8, 16, 17, 18, 19, 20, 21),
        (4,),
        collective_id=1,
        megabytes=57,
        name="shared_gradients",
    )


def meet_core(at):
    barrier = pltpu.get_barrier_semaphore()
    other = moved(at, "core", 1)
    pl.semaphore_signal(barrier, inc=1, device_id=device(other), device_id_type=MESH)
    pl.semaphore_wait(barrier, 1)
    return other


CHUNK = 48


def chunks(count, step, start=0):
    lax.fori_loop(0, count // CHUNK, lambda i, c: step(pl.ds(pl.multiple_of(i * CHUNK, CHUNK), CHUNK), c), start)


def centre(value):
    centred = value - jnp.mean(value, axis=-1, keepdims=True)
    spread = jnp.mean(centred * centred, axis=-1, keepdims=True)
    return centred * lax.rsqrt(spread + 1e-06), lax.rsqrt(spread + 1e-06)


def norm_back(value, grad, gain):
    normed, rate = centre(value)
    scaled = grad * gain
    inner = (
        scaled
        - jnp.mean(scaled, axis=-1, keepdims=True)
        - normed * jnp.mean(scaled * normed, axis=-1, keepdims=True)
    )
    return rate * inner, jnp.sum(grad * normed, axis=0, keepdims=True), jnp.sum(grad, axis=0, keepdims=True)


def attend_kernel(
    staged, x_ref, w0, w1, w2, w3, w4, extra, spare, ids,
    embed, hidden_one, query, keys, values, mixed, after, hidden_two, gate_probs, gates, lse,
    vec, router, target, target_t, hidden_kept, w1_kept, w2_kept, w3_kept, w4_kept,
    turned, local, send, recv,
):
    at = place()
    sems = (send, recv)
    saves = [
        pltpu.make_async_copy(source, target_ref, local.at[index])
        for index, (source, target_ref) in enumerate(
            ((w1, w1_kept), (w2, w2_kept), (w3, w3_kept), (w4, w4_kept), (hidden_two, hidden_kept))
        )
    ]
    for copy in saves[:4]:
        copy.start()
    other = meet_core(at)
    rows = x_ref.shape[0]
    staged.need(8)
    turned[...] = (
        extra[:, :EXTRA].astype(jnp.float32) + spare[:, :EXTRA].astype(jnp.float32)
    ).T
    vec[...] = turned[VECTOR_AT : VECTOR_AT + 16, :] + turned[VECTOR_AT + 16 : VECTOR_AT + 32, :]
    router[...] = extra[:, EXTRA - LANES : EXTRA]

    block = rows // 2
    earlier = (iota((block, block), 1) < iota((block, block), 0)).astype(jnp.bfloat16)
    lane = iota((block, LANES), 1)
    for number in range(2):
        part = slice(number * block, (number + 1) * block)
        hits = [(lane == ids[part, k : k + 1]).astype(jnp.float32) for k in range(2)]
        before = plain_dot(earlier, (hits[0] + hits[1]).astype(jnp.bfloat16))
        spots = []
        for k in range(2):
            named = ids[part, k : k + 1]
            slot = jnp.sum(hits[k] * before, axis=-1, keepdims=True).astype(jnp.int32) + number * CAP
            spots.append(
                jnp.where(slot < SLOTS, named * SLOTS + slot, MAIN + named * TAIL + slot - SLOTS)
            )
        target[part, :] = jnp.where(lane == 0, spots[0], jnp.where(lane == 1, spots[1], 0))
    target_t[...] = target[...].astype(jnp.float32).T[:PAD].astype(jnp.int32)

    staged.need(0)
    embed[...] = plain_dot(x_ref[...], w0[...])

    def first_norm(index, carry):
        part = pl.ds(pl.multiple_of(index * CHUNK, CHUNK), CHUNK)
        line = at["core"] * block + index * CHUNK + jnp.where(index * CHUNK < block, 0, block)
        value = embed[part, :] + vec[0:1, :] + turned[pl.ds(pl.multiple_of(line, CHUNK), CHUNK), :]
        embed[part, :] = value
        normed, _ = centre(value)
        hidden_one[part, :] = (normed * vec[1:2, :] + vec[2:3, :]).astype(jnp.bfloat16)
        return carry

    lax.fori_loop(0, rows // CHUNK, first_norm, 0)
    keys[0] = plain_dot(hidden_one[...], w2[...]).astype(jnp.bfloat16)
    send_keys = remote(keys.at[0], keys.at[1], sems, 0, other)
    send_keys.start()
    values[0] = (plain_dot(hidden_one[...], w3[...]) + vec[4:5, :]).astype(jnp.bfloat16)
    send_values = remote(values.at[0], values.at[1], sems, 1, other)
    send_values.start()
    query[...] = (plain_dot(hidden_one[...], w1[...]) + vec[3:4, :]).astype(jnp.bfloat16)
    send_keys.wait()
    send_values.wait()
    staged.give(0, 1, 2, 3, 4)

    def heads(index, carry):
        lanes = pl.ds(pl.multiple_of(index * LANES, LANES), LANES)
        query_two = query[:, lanes]
        key_two = keys[:, :, lanes].reshape(2 * rows, LANES)
        value_t = values[:, :, lanes].reshape(2 * rows, LANES).T
        left = lax.broadcasted_iota(jnp.int32, (rows, LANES), 1) < HEAD
        outs = []
        for half in range(2):
            own = jnp.where(left if half == 0 else ~left, query_two, jnp.zeros_like(query_two))
            scores = over_last(key_two, own) * HEAD ** (-0.5)
            most = jnp.max(scores, axis=0, keepdims=True)
            raw = jnp.exp(scores - most)
            total = jnp.sum(raw, axis=0, keepdims=True)
            lse[pl.ds(index * 2 + half, 1), :] = most + jnp.log(total)
            probs = (raw * (1.0 / total)).astype(jnp.bfloat16)
            outs.append(plain_dot(value_t[half * HEAD : (half + 1) * HEAD], probs))
        mixed[:, lanes] = jnp.concatenate(outs).T.astype(jnp.bfloat16)
        return carry

    lax.fori_loop(0, D // LANES, heads, 0)
    staged.give(5)
    after[...] = plain_dot(mixed[...], w4[...])

    def second_norm(part, carry):
        value = embed[part, :] + after[part, :] + vec[5:6, :]
        after[part, :] = value
        normed, _ = centre(value)
        low = (normed * vec[6:7, :] + vec[7:8, :]).astype(jnp.bfloat16)
        hidden_two[part, :] = low
        logits = plain_dot(low, router[...])
        lane = iota(logits.shape, 1) - ROUTER_AT
        logits = jnp.where((lane >= 0) & (lane < GROUP), logits, -jnp.inf)
        raw = jnp.exp(logits - jnp.max(logits, axis=-1, keepdims=True))
        probs = raw / jnp.sum(raw, axis=-1, keepdims=True)
        gate_probs[part, :] = probs
        first, second = (
            jnp.sum(jnp.where(lane == ids[part, k : k + 1], probs, 0.0), axis=-1, keepdims=True) for k in range(2)
        )
        gates[part, :] = jnp.where(lane == -ROUTER_AT, first, second)
        return carry

    chunks(rows, second_norm)
    staged.give(6)
    saves[4].start()
    for copy in saves:
        copy.wait()


def attend(patch_rows, squares, extra, spare, ids):
    rows = patch_rows.shape[0]
    low, wide = jnp.bfloat16, jnp.float32
    shapes = [
        ((rows, D), wide), ((rows, D), low), ((rows, D), low), ((2, rows, D), low), ((2, rows, D), low),
        ((rows, D), low), ((rows, D), wide), ((rows, D), low), ((rows, LANES), wide), ((rows, LANES), wide), ((16, rows), wide),
        ((16, D), wide), ((D, LANES), low), ((rows, LANES), jnp.int32), ((PAD, rows), jnp.int32),
        ((rows, D), low), ((D, D), low), ((D, D), low), ((D, D), low), ((D, D), low),
    ]
    sems = pltpu.SemaphoreType.DMA
    return staged_call(
        attend_kernel,
        (patch_rows, *squares, extra, spare, ids),
        shapes,
        [pltpu.VMEM((EXTRA, D), wide), sems((5,)), sems((2,)), sems((2,))],
        (0, 8),
        tuple(range(7)),
        raw_out=(15, 16, 17, 18, 19),
        collective_id=6,
        megabytes=20,
        name="attend",
    )


def attend_back_kernel(
    staged, dafter_in, dhidden, dgate, embed, after, query, keys, values, lse, w1, w2, w3, w4, vec, router,
    dafter_low, dquery, dkey, dvalue, dembed_low, sums,
    dafter, dmixed, dkey_own, dvalue_own, dkey_other, dvalue_other, dkey_got, dvalue_got, wide, send, recv,
):
    at = place()
    sems = (send, recv)
    other = meet_core(at)
    rows = dafter_in.shape[0]
    pairs = D // LANES
    zero = jnp.zeros((1, D), jnp.float32)
    wide[...] = over_last(dgate[...], router[...])
    staged.need(0, 1, 4)

    def second_norm(index, carry):
        part = pl.ds(pl.multiple_of(index * CHUNK, CHUNK), CHUNK)
        grad = wide[part, :] + dhidden[part, :]
        back, gain, shift = norm_back(after[part, :], grad, vec[6:7, :])
        total = dafter_in[part, :] + back
        dafter[part, :] = total
        dafter_low[part, :] = total.astype(jnp.bfloat16)
        return carry[0] + jnp.sum(total, axis=0, keepdims=True), carry[1] + gain, carry[2] + shift

    bias, gain, shift = lax.fori_loop(0, rows // CHUNK, second_norm, (zero, zero, zero))
    sums[5:6, :] = bias
    sums[6:7, :] = gain
    sums[7:8, :] = shift
    staged.give(0)
    staged.need(12)
    dmixed[...] = over_last(dafter_low[...], w4[...]).astype(jnp.bfloat16)
    staged.need(5, 6, 7)

    def flights(index):
        return (
            remote(dkey_other.at[index], dkey_got.at[index], sems, index, other),
            remote(dvalue_other.at[index], dvalue_got.at[index], sems, pairs + index, other),
        )

    def heads(index, carry):
        lanes = pl.ds(pl.multiple_of(index * LANES, LANES), LANES)
        query_two = query[:, lanes]
        dmixed_two = dmixed[:, lanes]
        key_two = keys[:, :, lanes].reshape(2 * rows, LANES)
        value_two = values[:, :, lanes].reshape(2 * rows, LANES)
        key_t = key_two.T
        left = lax.broadcasted_iota(jnp.int32, (rows, LANES), 1) < HEAD
        dkey_two = jnp.zeros((2 * rows, LANES), jnp.float32)
        dvalue_two = jnp.zeros((2 * rows, LANES), jnp.float32)
        outs = []
        for half in range(2):
            mask = left if half == 0 else ~left
            own = jnp.where(mask, query_two, jnp.zeros_like(query_two))
            down = jnp.where(mask, dmixed_two, jnp.zeros_like(dmixed_two))
            scores = over_last(key_two, own) * HEAD ** (-0.5)
            probs = jnp.exp(scores - lse[pl.ds(index * 2 + half, 1), :])
            dprobs = over_last(value_two, down)
            row_shift = jnp.sum(probs * dprobs, axis=0, keepdims=True)
            dscores = (probs * (dprobs - row_shift)).astype(jnp.bfloat16)
            dvalue_two = dvalue_two + plain_dot(probs.astype(jnp.bfloat16), down)
            dkey_two = dkey_two + plain_dot(dscores, own)
            outs.append(plain_dot(key_t[half * HEAD : (half + 1) * HEAD], dscores))
        dkey_two = dkey_two * HEAD ** (-0.5)
        dquery[:, lanes] = (jnp.concatenate(outs).T * HEAD ** (-0.5)).astype(jnp.bfloat16)
        dkey_own[index] = dkey_two[:rows]
        dkey_other[index] = dkey_two[rows:]
        dvalue_own[index] = dvalue_two[:rows]
        dvalue_other[index] = dvalue_two[rows:]
        for copy in flights(index):
            copy.start()
        return carry

    lax.fori_loop(0, pairs, heads, 0)

    def gather(index, carry):
        lanes = pl.ds(pl.multiple_of(index * LANES, LANES), LANES)
        for copy in flights(index):
            copy.wait()
        dkey[:, lanes] = (dkey_own[index] + dkey_got[index]).astype(jnp.bfloat16)
        dvalue[:, lanes] = (dvalue_own[index] + dvalue_got[index]).astype(jnp.bfloat16)
        return carry

    lax.fori_loop(0, pairs, gather, 0)
    staged.give(1, 2, 3)
    staged.need(3, 9, 10, 11)
    wide[...] = (
        over_last(dquery[...], w1[...]) + over_last(dkey[...], w2[...]) + over_last(dvalue[...], w3[...])
    )

    def first_norm(index, carry):
        part = pl.ds(pl.multiple_of(index * CHUNK, CHUNK), CHUNK)
        back, gain, shift = norm_back(embed[part, :], wide[part, :], vec[1:2, :])
        total = dafter[part, :] + back
        dembed_low[part, :] = total.astype(jnp.bfloat16)
        return (
            carry[0] + jnp.sum(total, axis=0, keepdims=True),
            carry[1] + gain,
            carry[2] + shift,
            carry[3] + jnp.sum(dquery[part, :].astype(jnp.float32), axis=0, keepdims=True),
            carry[4] + jnp.sum(dvalue[part, :].astype(jnp.float32), axis=0, keepdims=True),
        )

    for index, total in enumerate(lax.fori_loop(0, rows // CHUNK, first_norm, (zero,) * 5)):
        sums[index : index + 1, :] = total
    staged.give(4)


def attend_back(*operands):
    rows = operands[0].shape[0]
    low, wide = jnp.bfloat16, jnp.float32
    pairs = D // LANES
    sems = pltpu.SemaphoreType.DMA
    return staged_call(
        attend_back_kernel,
        operands,
        [((rows, D), low)] * 5 + [((8, D), wide)],
        [pltpu.VMEM((rows, D), wide), pltpu.VMEM((rows, D), low)]
        + [pltpu.VMEM((pairs, rows, LANES), wide)] * 6
        + [pltpu.VMEM((rows, D), wide), sems((2 * pairs,)), sems((2 * pairs,))],
        (0, 1, 4, 12, 5, 6, 7, 3, 9, 10, 11),
        (0, 1, 2, 3, 4),
        collective_id=7,
        megabytes=28,
        name="attend_back",
    )


SLOTS = 16
TAIL = 2 * CAP - SLOTS
WIRE = D + 2 * LANES
GROUP = 32
MAIN = GROUP * SLOTS
TOTAL = GROUP * (SLOTS + TAIL)


def iota(shape, axis):
    return lax.broadcasted_iota(jnp.int32, shape, axis)


def pack(block, main, tail):
    count = block.shape[0]
    block[:, :, :D] = main.astype(jnp.bfloat16).reshape(count, SLOTS, D)
    shape = (count * SLOTS, count * TAIL)
    row, column = iota(shape, 0), iota(shape, 1)
    spread = (lax.div(row, SLOTS) == lax.div(column, TAIL)) & (lax.rem(row, TAIL) == lax.rem(column, TAIL))
    wide = plain_dot(spread.astype(jnp.bfloat16), tail.astype(jnp.bfloat16))
    turn = lax.div(lax.rem(iota((count * SLOTS, LANES), 0), SLOTS), TAIL)
    for half, tiles in ((0, (0, 1, 2, 3)), (1, (4, 5))):
        packed = jnp.zeros((count * SLOTS, LANES), jnp.float32)
        for place_in, tile in enumerate(tiles):
            packed = jnp.where(turn == place_in, wide[:, tile * LANES : (tile + 1) * LANES], packed)
        block[:, :, D + half * LANES : D + (half + 1) * LANES] = packed.astype(jnp.bfloat16).reshape(
            count, SLOTS, LANES
        )


def unpack(block, rows, first, first_tail):
    count = block.shape[0]
    rows[first : first + count * SLOTS, :] = block[:, :, :D].reshape(count * SLOTS, D)
    shape = (count * TAIL, count * SLOTS)
    row, column = iota(shape, 0), iota(shape, 1)
    same = lax.div(column, SLOTS) == lax.div(row, TAIL)
    packed = block[:, :, D:].reshape(count * SLOTS, 2 * LANES)
    for turn in range(4):
        chosen = same & (lax.rem(column, SLOTS) == turn * TAIL + lax.rem(row, TAIL))
        part = plain_dot(chosen.astype(jnp.bfloat16), packed).astype(jnp.bfloat16)
        rows[first_tail : first_tail + count * TAIL, turn * LANES : (turn + 1) * LANES] = part[:, :LANES]
        if turn < 2:
            rows[first_tail : first_tail + count * TAIL, (4 + turn) * LANES : (5 + turn) * LANES] = part[
                :, LANES:
            ]


def meet_experts(at):
    barrier = pltpu.get_barrier_semaphore()
    me = lax.axis_index("exp")

    def greet_one(by, carry):
        peer = lax.rem(me + by, GROUP)
        pl.semaphore_signal(barrier, inc=1, device_id={"exp": peer}, device_id_type=MESH)
        return carry

    lax.fori_loop(1, GROUP, greet_one, 0)
    peers = moved(at, "core", 1), moved(at, "y", 2)
    for peer in peers:
        pl.semaphore_signal(barrier, inc=1, device_id=device(peer), device_id_type=MESH)
    return peers


def met_experts():
    pl.semaphore_wait(pltpu.get_barrier_semaphore(), GROUP + 1)


def deal(source, target, sems, forth, low, high, act):
    me = lax.axis_index("exp")

    def one(by, carry):
        peer = lax.rem(me + by, GROUP) if forth else lax.rem(me + GROUP - by, GROUP)
        copy = pltpu.make_async_remote_copy(
            src_ref=source.at[peer] if forth else source.at[by],
            dst_ref=target.at[by] if forth else target.at[me],
            send_sem=sems[0].at[by],
            recv_sem=sems[1].at[by],
            device_id={"exp": peer},
            device_id_type=MESH,
        )
        act(copy)
        return carry

    lax.fori_loop(low, high, one, 0)


def start_copy(copy):
    copy.start()


def wait_send(copy):
    copy.wait_send()


def wait_recv(copy):
    copy.wait_recv()


def load_experts(own, across, weights, sems, local, other):
    near = [pltpu.make_async_copy(own, weights.at[0], local.at[0])]
    far = [remote(own, weights.at[2], sems, 0, other)]
    for which, ref in enumerate(across):
        near.append(pltpu.make_async_copy(ref, weights.at[1, which], local.at[1 + which]))
        far.append(remote(ref, weights.at[3, which], sems, 1 + which, other))
    return near, far


GELU_SCALE = math.sqrt(2 / math.pi)


def gelu_tanh(value):
    return jnp.tanh(GELU_SCALE * (value + 0.044715 * (value * value * value)))


def halves(rows, half):
    count = MAIN // 2
    tail = (TOTAL - MAIN) // 2
    return jnp.concatenate(
        [
            rows[half * count : (half + 1) * count, :],
            rows[MAIN + half * tail : MAIN + (half + 1) * tail, :],
        ]
    )


HALF = TOTAL // 2


def experts_kernel(
    staged, hidden, target_row, target_column, gates, after, vec, own, across_in, across_part,
    rows, rows_y, chosen, total, pool, across_out,
    weights, sends, lands, backs, returns, act, result, gathered,
    forth_send, forth_recv, back_send, back_recv, weight_send, weight_recv, row_send, row_recv, local,
):
    at = place()
    me = lax.axis_index("exp")
    other, across_y_peer = meet_experts(at)
    row_copies = []
    near, far = load_experts(own, (across_in,), weights, (weight_send, weight_recv), local, other)
    late = pl.ds(EARLY, D - EARLY)
    trade = remote(own.at[1, late], weights.at[1, 1, late], (weight_send, weight_recv), 2, across_y_peer)
    pass_on = remote(weights.at[1, 1], weights.at[3, 1], (weight_send, weight_recv), 3, other)
    save = pltpu.make_async_copy(weights.at[1, 1], across_out, local.at[3])
    near.append(pltpu.make_async_copy(across_part, weights.at[1, 1, pl.ds(0, EARLY)], local.at[4]))
    for copy in near:
        copy.start()
    count = hidden.shape[0]
    slot = iota((TOTAL, count), 0)
    placing = ((slot == target_row[0:1, :]) | (slot == target_row[1:2, :])).astype(jnp.bfloat16)
    placed = plain_dot(placing, hidden[...])
    pack(sends, placed[:MAIN], placed[MAIN:])
    met_experts()
    deal(sends, lands, (forth_send, forth_recv), True, 1, GROUP, start_copy)
    for copy in [*far, trade]:
        copy.start()
    keep = pltpu.make_async_copy(sends.at[me], lands.at[0], local.at[2])
    keep.start()
    keep.wait()
    deal(sends, lands, (forth_send, forth_recv), True, 1, GROUP // 2, wait_recv)
    for copy in near:
        copy.wait()
    for half in range(2):
        if half == 1:
            deal(sends, lands, (forth_send, forth_recv), True, GROUP // 2, GROUP, wait_recv)
        sources = pl.ds(half * (GROUP // 2), GROUP // 2)
        first, first_tail = half * (MAIN // 2), MAIN + half * (TOTAL - MAIN) // 2
        unpack(lands.at[sources], rows, first, first_tail)
        for piece, (start, size) in enumerate(((first, MAIN // 2), (first_tail, (TOTAL - MAIN) // 2))):
            view = pl.ds(start, size)
            copy = remote(rows.at[view], rows_y.at[view], (row_send, row_recv), half * 2 + piece, across_y_peer)
            copy.start()
            row_copies.append(copy)
        if half == 0:
            for copy in far:
                copy.wait_recv()
        given = halves(rows, half)

        def hidden_units(index, carry):
            quarter, part = lax.div(index, 3), lax.rem(index, 3)
            columns = pl.ds(pl.multiple_of(part * 256, 256), 256)
            value = plain_dot(given, weights[quarter, 0, :, columns])
            act[quarter, :, columns] = (0.5 * value * (1.0 + gelu_tanh(value))).astype(jnp.bfloat16)
            return carry

        lax.fori_loop(0, 12, hidden_units, 0)
        if half == 0:
            trade.wait_recv()
            pass_on.start()
            save.start()
            pass_on.wait_recv()

        def outputs(index, carry):
            columns = pl.ds(pl.multiple_of(index * 256, 256), 256)
            value = over_last(act[0], weights[0, 1, columns, :])
            for quarter in range(1, 4):
                value = value + over_last(act[quarter], weights[quarter, 1, columns, :])
            result[:, columns] = value
            return carry

        lax.fori_loop(0, 3, outputs, 0)
        pack(backs.at[sources], result[: MAIN // 2, :], result[MAIN // 2 :, :])
        deal(backs, returns, (back_send, back_recv), False, max(1, half * (GROUP // 2)), (half + 1) * (GROUP // 2), start_copy)
    keep = pltpu.make_async_copy(backs.at[0], returns.at[me], local.at[2])
    keep.start()
    keep.wait()
    deal(backs, returns, (back_send, back_recv), False, 1, GROUP, wait_recv)
    unpack(returns, gathered, 0, MAIN)
    slot = iota((count, TOTAL), 1)
    for k in range(2):
        placing = (slot == target_column[:, k : k + 1]).astype(jnp.bfloat16)
        chosen[k] = plain_dot(placing, gathered[...]).astype(jnp.bfloat16)
    staged.give(0, 2)
    staged.need(4)

    def final_norm(index, carry):
        part = pl.ds(pl.multiple_of(index * CHUNK, CHUNK), CHUNK)
        value = after[part, :] + (
            gates[part, 0:1] * chosen[0, part, :].astype(jnp.float32)
            + gates[part, 1:2] * chosen[1, part, :].astype(jnp.float32)
        )
        total[part, :] = value
        normed, _ = centre(value)
        return carry + jnp.sum(normed * vec[8:9, :] + vec[9:10, :], axis=0, keepdims=True)

    summed = lax.fori_loop(0, count // CHUNK, final_norm, jnp.zeros((1, D), jnp.float32)) / PATCHES
    staged.give(3)
    pool[...] = jnp.zeros_like(pool)
    for tile in range(D // LANES):
        pool[tile : tile + 1, :] = summed[:, tile * LANES : (tile + 1) * LANES]
    deal(sends, lands, (forth_send, forth_recv), True, 1, GROUP, wait_send)
    deal(backs, returns, (back_send, back_recv), False, 1, GROUP, wait_send)
    for copy in [*far, trade, pass_on]:
        copy.wait_send()
    save.wait()
    for copy in row_copies:
        copy.wait()
    staged.give(1)


def experts_forward(*operands):
    count = operands[0].shape[0]
    low, wide = jnp.bfloat16, jnp.float32
    wire = pltpu.VMEM((GROUP, SLOTS, WIRE), low)
    sems = pltpu.SemaphoreType.DMA
    return staged_call(
        experts_kernel,
        operands,
        [((TOTAL, D), low), ((TOTAL, D), low), ((2, count, D), low), ((count, D), wide), ((PAD, LANES), wide), ((D, D), low)],
        [pltpu.VMEM((4, 2, D, D), low)]
        + [wire] * 4
        + [pltpu.VMEM((4, HALF, D), low), pltpu.VMEM((HALF, D), wide), pltpu.VMEM((TOTAL, D), low)]
        + [sems((GROUP,))] * 4
        + [sems((4,))] * 4
        + [sems((5,))],
        (4,),
        (0, 1, 2, 3),
        raw=(6, 7, 8),
        raw_out=(5,),
        collective_id=5,
        megabytes=25,
        name="experts_forward",
    )


def tile_of(index):
    half, part = lax.div(index, 3), lax.rem(index, 3)
    columns = pl.ds(pl.multiple_of(part * 256, 256), 256)
    return pl.ds(pl.multiple_of(half * HALF, HALF), HALF), columns


def gelu_both(value):
    tanh = gelu_tanh(value)
    grown = (0.5 * value * (1.0 + tanh)).astype(jnp.bfloat16)
    return grown, 0.5 * (1.0 + tanh) + 0.5 * value * (1.0 - tanh * tanh) * (
        GELU_SCALE * (1.0 + 3 * 0.044715 * (value * value))
    )


def quarter_grads(kept, rows_t, drows_t, dpre, act, first):
    def step(index, carry):
        columns = pl.ds(pl.multiple_of(index * 256, 256), 256)
        for which, (left, right) in enumerate(((rows_t, dpre), (drows_t, act))):
            value = plain_dot(left[...], right[:, columns])
            kept[which, :, columns] = value if first else kept[which, :, columns] + value
        return carry

    lax.fori_loop(0, 3, step, 0)


def quarter_set(kept, weights, rows, drows, act, dpre, rows_t, drows_t):
    def step(index, carry):
        lines, columns = tile_of(index)
        grown, rate = gelu_both(plain_dot(rows[lines, :], weights[0, :, columns]))
        act[lines, columns] = grown
        value = plain_dot(drows[lines, :], weights[1, :, columns])
        dpre[lines, columns] = (value * rate).astype(jnp.bfloat16)
        return carry

    lax.fori_loop(0, 6, step, 0)
    rows_t[...] = rows[...].T
    drows_t[...] = drows[...].T
    quarter_grads(kept, rows_t, drows_t, dpre, act, False)


def experts_back_kernel(
    staged, row_grad, total, chosen, gates, gate_probs, ids, rows, rows_y, target_row, target_column, vec, own, across_in, across_out,
    dtotal, dgate, sums, dhidden, kept, rows_last, drows_y, drows_last,
    weights, sends, lands, backs, returns, slope, dpre, act_own, act_set, dpre_set, rows_far, drows, drows_far, result, dreturned,
    rows_t, drows_t, outward,
    forth_send, forth_recv, back_send, back_recv, weight_send, weight_recv, set_send, set_recv, local,
):
    at = place()
    me = lax.axis_index("exp")
    other, across_y_peer = meet_experts(at)
    near, far = load_experts(own, (across_in, across_out), weights, (weight_send, weight_recv), local, other)
    for copy in near:
        copy.start()
    count = total.shape[0]
    grad = jnp.concatenate([row_grad[tile : tile + 1, :] for tile in range(D // LANES)], axis=1) / PATCHES
    zero = jnp.zeros((1, D), jnp.float32)
    staged.need(1, 2, 5)

    def final_norm(index, carry):
        part = pl.ds(pl.multiple_of(index * CHUNK, CHUNK), CHUNK)
        back, gain, shift = norm_back(total[part, :], jnp.broadcast_to(grad, (CHUNK, D)), vec[8:9, :])
        dtotal[part, :] = back
        dgates = [
            jnp.sum(back * chosen[k, part, :].astype(jnp.float32), axis=-1, keepdims=True) for k in range(2)
        ]
        for k in range(2):
            outward[k, part, :] = (gates[part, k : k + 1] * back).astype(jnp.bfloat16)
        lane = iota((CHUNK, LANES), 1) - ROUTER_AT
        probs = gate_probs[part, :]
        dprobs = jnp.where(lane == ids[part, 0:1], dgates[0], 0.0) + jnp.where(
            lane == ids[part, 1:2], dgates[1], 0.0
        )
        inner = dprobs - jnp.sum(probs * dprobs, axis=-1, keepdims=True)
        dgate[part, :] = (probs * inner).astype(jnp.bfloat16)
        return carry[0] + gain, carry[1] + shift

    gain, shift = lax.fori_loop(0, count // CHUNK, final_norm, (zero, zero))
    sums[...] = jnp.concatenate([gain, shift, jnp.zeros((PAD - 2, D), jnp.float32)])
    staged.give(0)
    slot = iota((TOTAL, count), 0)
    placed = [
        plain_dot((slot == target_row[k : k + 1, :]).astype(jnp.bfloat16), outward[k]) for k in range(2)
    ]
    placed = placed[0] + placed[1]
    pack(sends, placed[:MAIN], placed[MAIN:])
    met_experts()
    deal(sends, lands, (forth_send, forth_recv), True, 1, GROUP, start_copy)
    staged.need(6, 7)
    set_sems = (set_send, set_recv)
    moves = [remote(rows, rows_far, set_sems, 0, other), remote(rows_y, rows_last, set_sems, 1, other)]
    for copy in far + moves:
        copy.start()
    keep = pltpu.make_async_copy(sends.at[me], lands.at[0], local.at[3])
    keep.start()
    keep.wait()
    for copy in near:
        copy.wait()

    def hidden_units(index, carry):
        quarter = lax.div(index, 6)
        lines, columns = tile_of(lax.rem(index, 6))
        grown, rate = gelu_both(plain_dot(rows[lines, :], weights[quarter, 0, :, columns]))

        @pl.when(quarter == 0)
        def _():
            act_own[lines, columns] = grown

        slope[quarter, lines, columns] = rate
        return carry

    lax.fori_loop(0, 12, hidden_units, 0)
    for copy in far:
        copy.wait_recv()
    lax.fori_loop(12, 24, hidden_units, 0)
    deal(sends, lands, (forth_send, forth_recv), True, 1, GROUP, wait_recv)
    unpack(lands, drows, 0, MAIN)
    moves.append(remote(drows, drows_y, set_sems, 2, across_y_peer))
    moves.append(remote(drows, drows_far, set_sems, 3, other))
    for copy in moves[2:]:
        copy.start()

    def hidden_back(index, carry):
        quarter = lax.div(index, 6)
        lines, columns = tile_of(lax.rem(index, 6))
        value = plain_dot(drows[lines, :], weights[quarter, 1, :, columns])
        dpre[quarter, lines, columns] = (value * slope[quarter, lines, columns]).astype(jnp.bfloat16)
        return carry

    lax.fori_loop(0, 24, hidden_back, 0)

    def inputs_back(index, carry):
        lines, columns = tile_of(index)
        value = over_last(dpre[0, lines, :], weights[0, 0, columns, :])
        for quarter in range(1, 4):
            value = value + over_last(dpre[quarter, lines, :], weights[quarter, 0, columns, :])
        result[lines, columns] = value
        return carry

    lax.fori_loop(0, 6, inputs_back, 0)
    pack(backs, result[:MAIN, :], result[MAIN:, :])
    deal(backs, returns, (back_send, back_recv), False, 1, GROUP, start_copy)
    keep = pltpu.make_async_copy(backs.at[0], returns.at[me], local.at[3])
    keep.start()

    rows_t[...] = rows[...].T
    drows_t[...] = drows[...].T
    quarter_grads(kept, rows_t, drows_t, dpre.at[0], act_own, True)
    for copy in (moves[0], moves[3]):
        copy.wait_recv()
    quarter_set(kept, weights.at[0], rows_far, drows_far, act_set, dpre_set, rows_t, drows_t)
    staged.give(4)
    moves[2].wait_recv()
    moves.append(remote(drows_y, drows_last, set_sems, 4, other))
    moves[4].start()
    keep.wait()
    deal(backs, returns, (back_send, back_recv), False, 1, GROUP, wait_recv)
    unpack(returns, dreturned, 0, MAIN)
    slot = iota((count, TOTAL), 1)
    placing = (slot == target_column[:, 0:1]) | (slot == target_column[:, 1:2])
    dhidden[...] = plain_dot(placing.astype(jnp.bfloat16), dreturned[...])
    staged.give(3)
    moves[1].wait_recv()
    moves[4].wait_recv()
    staged.give(5, 6, 7)
    deal(sends, lands, (forth_send, forth_recv), True, 1, GROUP, wait_send)
    deal(backs, returns, (back_send, back_recv), False, 1, GROUP, wait_send)
    for copy in far + moves:
        copy.wait_send()


def experts_backward(*operands):
    count = operands[1].shape[0]
    low, wide = jnp.bfloat16, jnp.float32
    wire = pltpu.VMEM((GROUP, SLOTS, WIRE), low)
    shapes = [
        ((count, D), wide), ((count, LANES), low), ((PAD, D), wide),
        ((count, D), wide), ((2, D, D), wide), ((TOTAL, D), low), ((TOTAL, D), low), ((TOTAL, D), low),
    ]
    sems = pltpu.SemaphoreType.DMA
    return staged_call(
        experts_back_kernel,
        operands,
        shapes,
        [pltpu.VMEM((4, 2, D, D), low)]
        + [wire] * 4
        + [pltpu.VMEM((4, TOTAL, D), wide), pltpu.VMEM((4, TOTAL, D), low)]
        + [pltpu.VMEM((TOTAL, D), low)] * 6
        + [pltpu.VMEM((TOTAL, D), wide), pltpu.VMEM((TOTAL, D), low)]
        + [pltpu.VMEM((D, TOTAL), low)] * 2
        + [pltpu.VMEM((2, count, D), low)]
        + [sems((GROUP,))] * 4
        + [sems((3,))] * 2
        + [sems((5,))] * 2
        + [sems((4,))],
        (1, 2, 5, 6, 7),
        (0, 3, 4, 5, 6, 7),
        raw=(11, 12, 13),
        collective_id=8,
        megabytes=57,
        name="experts_backward",
    )


def plane_peer(at, by):
    return moved(moved(at, "x", by[0]), "z", by[1])


def greet_all(at):
    barrier = pltpu.get_barrier_semaphore()
    peers = [near_peer(at, by) for by in NEAR] + [plane_peer(at, by) for by in PLANE]
    for peer in peers:
        pl.semaphore_signal(barrier, inc=1, device_id=device(peer), device_id_type=MESH)
    pl.semaphore_wait(barrier, len(peers))


def send_near(at, source, target, sems, first):
    copies = []
    for index, by in enumerate(NEAR):
        peer = near_peer(at, by)
        copies.append(remote(source(peer), target.at[at["y"], at["core"]], sems, first + index, peer))
        copies[-1].start()
    return copies


def head_kernel(
    staged, pool, head, labels, count,
    row_grad, head_grad, loss,
    near, every, pooled, pulls, got, summed, last, low, send, recv,
):
    at = place()
    sems = (send, recv)
    greet_all(at)
    copies = send_near(at, lambda peer: pool, near, sems, 0)
    near[at["y"], at["core"]] = pool[...]
    classes = head.shape[0]
    staged.need(1)
    spare = classes - classes % 16
    low[spare:, :] = jnp.zeros((low.shape[0] - spare, D), jnp.bfloat16)
    low[:classes, :] = head[...].astype(jnp.bfloat16)
    images = pooled.shape[0]
    number = (lax.axis_index("rep") * GROUP + lax.axis_index("exp")) * classes
    column = iota((images, low.shape[0]), 1)
    inside = column < classes
    column = jnp.where(inside, column + number, -2)
    hit = labels[:, 0:1] == column
    for slot in range(1, labels.shape[1]):
        hit = hit | (labels[:, slot : slot + 1] == column)
    targets = hit.astype(jnp.float32)
    valid = (jnp.max(labels[...], axis=1, keepdims=True) >= 0).astype(jnp.float32)
    for copy in copies:
        copy.wait()
    rows = near[:, 0] + near[:, 1]
    mine = every.at[:, at["x"], :, at["z"]]
    mine[...] = rows.astype(jnp.bfloat16).astype(jnp.float32).reshape(2, 2, PAD, LANES)
    copies = []
    for index, by in enumerate(PLANE):
        copies.append(remote(mine, mine, sems, 7 + index, plane_peer(at, by)))
        copies[-1].start()
    for copy in copies:
        copy.wait()
    for tile in range(D // LANES):
        lanes = slice(tile * LANES, (tile + 1) * LANES)
        pooled[:, lanes] = every[:, :, :, :, tile, :].reshape(images, LANES).astype(jnp.bfloat16)
    logits = over_last(pooled[...], low[...])
    soft = jnp.maximum(logits, 0.0) + jnp.log1p(jnp.exp(-jnp.abs(logits)))
    terms = jnp.where(inside, valid * (soft - targets * logits), 0.0)
    loss[...] = jnp.sum(jnp.sum(terms, axis=1, keepdims=True), axis=0, keepdims=True)
    sigmoid = 1.0 / (1.0 + jnp.exp(-logits))
    down = jnp.where(inside, valid * (sigmoid - targets) / count[...], 0.0)
    back = plain_dot(down.astype(jnp.bfloat16), low[...])
    pulls[...] = jnp.zeros_like(pulls)
    for tile in range(D // LANES):
        lanes = slice(tile * LANES, (tile + 1) * LANES)
        pulls[:, :, :, :, tile, :] = back[:, lanes].reshape(2, 4, 2, 4, LANES)
    copies = []
    for index, by in enumerate(PLANE):
        peer = plane_peer(at, by)
        source = pulls.at[:, peer["x"], :, peer["z"]]
        copies.append(remote(source, got.at[at["x"], at["z"]], sems, 22 + index, peer))
        copies[-1].start()
    got[at["x"], at["z"]] = pulls[:, at["x"], :, at["z"]]
    head_grad[...] = plain_dot(down.T.astype(jnp.bfloat16), pooled[...])
    for copy in copies:
        copy.wait()
    summed[...] = jnp.sum(got[...].reshape((16,) + summed.shape), axis=0)
    copies = send_near(at, lambda peer: summed.at[peer["y"]], last, sems, 37)
    last[at["y"], at["core"]] = summed[at["y"]]
    for copy in copies:
        copy.wait()
    row_grad[...] = jnp.sum(last[...].reshape((8,) + row_grad.shape), axis=0)


def head_step(pool, head, labels, count):
    images = labels.shape[0]
    classes = -(-head.shape[0] // LANES) * LANES
    wide = jnp.float32
    block = (PAD, LANES)
    sems = pltpu.SemaphoreType.DMA
    return staged_call(
        head_kernel,
        (pool, head, labels, count),
        [(block, wide), ((classes, D), wide), ((1, 1), wide)],
        [
            pltpu.VMEM((4, 2) + block, wide),
            pltpu.VMEM((2, 4, 2, 4) + block, wide),
            pltpu.VMEM((images, D), jnp.bfloat16),
            pltpu.VMEM((2, 4, 2, 4) + block, wide),
            pltpu.VMEM((4, 4, 2, 2) + block, wide),
            pltpu.VMEM((4,) + block, wide),
            pltpu.VMEM((4, 2) + block, wide),
            pltpu.VMEM((classes, D), jnp.bfloat16),
            sems((44,)),
            sems((44,)),
        ],
        (1,),
        (),
        collective_id=2,
        megabytes=16,
        name="head_step",
    )


def follow(old, square):
    return DECAY * old + (1.0 - DECAY) * (square + EPS_SQ)


def update_kernel(
    part_one, part_two, part_three, totals, head_grad, table_grad, table_squared, expert_cols_squared, expert_grad,
    squares, router, table, head, vectors, experts,
    square_rows, square_cols, router_rows, router_cols, table_rows, table_cols, head_rows, head_cols,
    expert_rows, expert_cols, moment,
    loss, norm, square_clip, square_rows_next, square_cols_next, square_next,
    router_clip, router_rows_next, router_cols_next, router_next,
    table_clip, table_rows_next, table_cols_next, table_next,
    head_clip, head_rows_next, head_cols_next, head_next,
    expert_clip, expert_rows_next, expert_cols_next, expert_next,
    vector_clip, moment_next, vector_next,
    turned, scale_ref, column_ref, line_ref,
):
    step = pl.program_id(0)

    def stand(line):
        count = line.shape[1]
        column_ref[...] = jnp.zeros_like(column_ref)
        column_ref[0:1, :count] = line
        return column_ref[...].T[:count, 0:1]

    def lie(column):
        count = column.shape[0]
        line_ref[...] = jnp.zeros_like(line_ref)
        line_ref[:count, :] = jnp.broadcast_to(column, (count, LANES))
        return line_ref[...].T[0:1, :count]

    expert_rates = (0.3 / math.sqrt(D), 4.8 / math.sqrt(FF))

    def total(value):
        return jnp.sum(jnp.sum(value, axis=1, keepdims=True), axis=0, keepdims=True)

    @pl.when(step == 0)
    def _():
        size = jnp.sqrt(total(totals[:7, :]) + totals[7:8, 1:2])
        clip = jnp.minimum(1.0, CLIP_NORM / size)
        clip_sq = clip * clip
        loss[...] = totals[7:8, 0:1]
        norm[...] = size
        scale_ref[...] = jnp.broadcast_to(clip, scale_ref.shape)
        rows = squares.shape[1]
        parts = (part_one, part_two, part_three)
        for k in range(5):
            grad = parts[k // 2][PAD * (k % 2) : PAD * (k % 2) + rows, :]
            near = follow(stand(square_rows[k : k + 1, :]), clip_sq * jnp.mean(grad * grad, axis=1, keepdims=True))
            far = follow(square_cols[k : k + 1, :], clip_sq * totals[k : k + 1, :] / D)
            middle = jnp.mean(totals[k : k + 1, :], axis=1, keepdims=True)
            middle = follow(totals[7:8, 2 + k : 3 + k] / D, clip_sq * middle / D)
            square_rows_next[k : k + 1, :] = lie(near)
            square_cols_next[k : k + 1, :] = far
            square_clip[k] = clip * grad
            rate = (4.0 if k == 4 else 1.0) * (0.3 / math.sqrt(D))
            square_next[k] = squares[k] - rate * (clip * grad) * lax.rsqrt(near * far / middle)
        tail = part_three[PAD : PAD + rows, EXTRA:]
        grad = tail[:, 32:64]
        near = follow(stand(router_rows[...][None]), clip_sq * jnp.mean(grad * grad, axis=1, keepdims=True))
        squared = totals[6:7, EXTRA + 32 : EXTRA + 64]
        far = follow(router_cols[...][None], clip_sq * squared / D)
        middle = jnp.sum(squared, axis=1, keepdims=True) / GROUP
        middle = follow(totals[7:8, 7:8] / D, clip_sq * middle / D)
        router_rows_next[...] = lie(near)[0]
        router_cols_next[...] = far[0]
        router_clip[...] = clip * grad
        router_next[...] = router[...] - (0.2 / math.sqrt(D)) * (clip * grad) * lax.rsqrt(near * far / middle)
        grad = table_grad[...]
        near = follow(table_rows[...][None], clip_sq * table_squared[...] / D)
        far = follow(stand(table_cols[...][None]), clip_sq * jnp.mean(grad * grad, axis=1, keepdims=True))
        middle = jnp.mean(near, axis=1, keepdims=True)
        table_rows_next[...] = near[0]
        table_cols_next[...] = lie(far)[0]
        table_clip[...] = clip * grad
        table_next[...] = table[...] - 0.15 * (clip * grad) * lax.rsqrt(near * far / middle)
        classes = head.shape[0]
        grad = head_grad[:classes, :]
        near = follow(head_rows[...][None], clip_sq * totals[5:6, :] / (classes * 4 * GROUP))
        far = follow(stand(head_cols[...][None]), clip_sq * jnp.mean(grad * grad, axis=1, keepdims=True))
        middle = jnp.mean(near, axis=1, keepdims=True)
        head_rows_next[...] = near[0]
        head_cols_next[...] = lie(far)[0]
        head_clip[...] = clip * grad
        head_next[...] = head[...] - (0.5 / math.sqrt(D)) * (clip * grad) * lax.rsqrt(near * far / middle)
        grad = clip * tail[:, 96:106]
        state = follow(moment[...], grad * grad)
        vector_clip[...] = grad
        moment_next[...] = state
        vector_next[...] = vectors[...] - 0.3 * grad * lax.rsqrt(state)
        near = follow(expert_rows[...], clip_sq * totals[PAD : PAD + 2, :] / FF)
        far = follow(expert_cols[...], clip_sq * expert_cols_squared[...] / D)
        middle = jnp.mean(near, axis=1, keepdims=True)
        expert_rows_next[...] = near
        expert_cols_next[...] = far
        for which in range(2):
            ratio = near[which : which + 1, :] / middle[which : which + 1, :]
            turned[which] = jnp.broadcast_to(ratio, (LANES, D)).T

    lines = expert_grad.shape[1]
    steps = D // lines
    which = lax.div(step, steps)
    column = turned[which, pl.ds(pl.multiple_of(lax.rem(step, steps) * lines, lines), lines), 0:1]
    row = expert_cols_next[pl.ds(which, 1), :]
    clipped = scale_ref[0:1, 0:1] * expert_grad[0]
    rate = jnp.where(which == 0, expert_rates[0], expert_rates[1])
    expert_clip[0] = clipped
    expert_next[0] = experts[0] - rate * clipped * lax.rsqrt(column * row)


def update_all(*operands):
    lines = 256
    wide = jnp.float32
    squares, router, table, head, vectors = (operands[index].shape for index in range(9, 14))
    rows = squares[1]
    expert = operands[14].shape
    shapes = [
        (1, 1), (1, 1), squares, (5, rows), (5, D), squares, router, (rows,), (GROUP,), router,
        table, (PATCHES,), (rows,), table, head, (D,), (head[0],), head,
        expert, (2, D), (2, D), expert, vectors, vectors, vectors,
    ]

    def spec(shape, streamed):
        if streamed:
            return pl.BlockSpec((1, lines, D), lambda step: (step // (D // lines), step % (D // lines), 0))
        return pl.BlockSpec(shape, lambda step: (0,) * len(shape))

    return pl.pallas_call(
        update_kernel,
        grid=(2 * D // lines,),
        out_shape=[jax.ShapeDtypeStruct(shape, wide) for shape in shapes],
        in_specs=[spec(value.shape, index in (8, 14)) for index, value in enumerate(operands)],
        out_specs=[spec(shape, index in (18, 21)) for index, shape in enumerate(shapes)],
        scratch_shapes=[pltpu.VMEM((2, D, LANES), wide), pltpu.VMEM((PAD, LANES), wide)]
        + [pltpu.VMEM((LANES, 2 * LANES), wide), pltpu.VMEM((2 * LANES, LANES), wide)],
        compiler_params=pltpu.CompilerParams(vmem_limit_bytes=32 * 2**20),
        name="update_all",
    )(*(pin(value) for value in operands))


def across_cores(value):
    return lax.ppermute(value, "rep", CORE_SWAP)


def across_y(value):
    return lax.ppermute(value, "rep", Y_SWAP)


def shards(
    patches,
    expert_ids,
    labels,
    label_count,
    square_weights,
    router_weight,
    position_table,
    head_weight,
    expert_weights,
    vector_params,
    square_rows,
    square_cols,
    router_rows,
    router_cols,
    position_rows,
    position_cols,
    head_rows,
    head_cols,
    expert_rows,
    expert_cols,
    vector_moment,
):
    bfloat = jnp.bfloat16
    num_rep = lax.axis_size("rep")
    num_exp = lax.axis_size("exp")
    rep_index = lax.axis_index("rep")
    my_image = lax.axis_index("exp")
    device_index = lax.axis_index(("rep", "exp"))
    micro, core = rep_index // 2, rep_index % 2
    num_expert = router_weight.shape[1]
    vocab_dev = head_weight.shape[1]
    ff_dev = expert_weights.shape[3]
    block = patches.shape[2]
    rows, width = 2 * block, patches.shape[3]
    num_top = expert_ids.shape[3]
    heads = width // HEAD
    scale = HEAD ** (-0.5)
    own_rows = square_weights.shape[1]

    gap = jnp.zeros((own_rows, 6), jnp.float32)
    extra = jnp.concatenate(
        [position_table.T, router_weight, vector_params.T, gap, vector_params.T], axis=1
    )
    extra = jnp.pad(extra, ((0, 0), (0, width - extra.shape[1])))
    valid = (label_count > 0).astype(jnp.float32)
    image_count = jnp.sum(valid)
    live = jnp.arange(labels.shape[2], dtype=jnp.int32) < label_count[:, :, None]
    live_labels = jnp.where(live, labels, -1).reshape(2 * num_exp, -1)

    counted = image_count.reshape(1, 1)
    extra, live_labels, counted = lax.optimization_barrier((extra, live_labels, counted))

    wide_ids = jnp.pad(expert_ids.reshape(2, block, num_top), ((0, 0), (0, 0), (0, LANES - num_top)))
    *squares, extra, low, patch_rows, ids, quarter, quarter_in, across_part = gather_all(
        square_weights, extra, patches.reshape(2, block, width), wide_ids, expert_weights[0]
    )
    patch_rows, ids = patch_rows.reshape(rows, width), ids.reshape(rows, LANES)

    across_in = across_y(quarter_in)
    (
        embed, hidden_one, query, keys, values, mixed, after_attn, hidden_two,
        gate_probs, gates, lse, vectors, router, target, target_t, hidden_kept, *squares,
    ) = attend(patch_rows, squares, extra, low, ids)
    across_in, hidden_two = lax.optimization_barrier((across_in, hidden_two))
    received, received_y, chosen, after_moe, pool, across_out = experts_forward(
        hidden_two, target_t, target, gates, after_attn, vectors, quarter, across_in, across_part
    )
    row_grad, head_g, loss_part = head_step(
        pool, head_weight.T, live_labels, counted
    )
    dmoe_in, dgate_logits, final_sums, dhidden, part_g, received_last, down_y, down_last = experts_backward(
        row_grad, after_moe, chosen, gates, gate_probs, ids, received, received_y,
        target_t, target, vectors, quarter, across_in, across_out,
    )
    dafter_low, dquery_low, dkey_low, dvalue_low, dembed_low, sums = attend_back(
        dmoe_in,
        dhidden,
        dgate_logits,
        embed,
        after_attn,
        query,
        keys,
        values,
        lse,
        *squares,
        vectors,
        router,
    )
    *owned, totals, expert_g, expert_colsq = shared_gradients(
        patch_rows, hidden_one, mixed, dembed_low, dquery_low, dkey_low, dvalue_low, dafter_low,
        hidden_kept, dgate_logits, sums, final_sums, head_g, loss_part, square_rows, router_rows[None],
        part_g, quarter, received_y, received_last, down_y, down_last,
    )
    second = 3 * LANES

    def positions(value):
        return jnp.concatenate(
            [value[:, start : start + block] for start in (0, second, block, second + block)], axis=1
        )

    (
        loss_total, grad_norm, square_clip, square_rows_next, square_cols_next, square_next,
        router_clip, router_rows_next, router_cols_next, router_next,
        table_clip, table_rows_next, table_cols_next, table_next,
        head_clip, head_rows_next, head_cols_next, head_next,
        expert_clip, expert_rows_next, expert_cols_next, expert_next,
        vector_clip, moment_next, vector_next,
    ) = update_all(
        *owned, totals, head_g, positions(owned[2][PAD : PAD + own_rows]), positions(totals[6:7]),
        expert_colsq, expert_g,
        square_weights, router_weight, position_table.T, head_weight.T, vector_params.T, expert_weights[0],
        square_rows, square_cols, router_rows, router_cols, position_rows,
        position_cols, head_rows, head_cols, expert_rows[0], expert_cols[0],
        vector_moment.T,
    )
    return (
        loss_total[0, 0],
        image_count,
        grad_norm[0, 0],
        square_clip,
        square_rows_next,
        square_cols_next,
        square_next,
        router_clip,
        router_rows_next,
        router_cols_next,
        router_next,
        table_clip.T,
        table_rows_next,
        table_cols_next,
        table_next.T,
        head_clip.T,
        head_rows_next,
        head_cols_next,
        head_next.T,
        expert_clip[None],
        expert_rows_next[None],
        expert_cols_next[None],
        expert_next[None],
        vector_clip.T,
        moment_next.T,
        vector_next.T,
    )


def solution(mesh):
    in_specs = (
        P(None, "exp", "rep", None),
        P(None, "exp", "rep", None),
        P(),
        P(),
        P(None, ("rep", "exp"), None),
        P(("rep", "exp"), None),
        P(None, ("rep", "exp")),
        P(None, ("rep", "exp")),
        P("exp", None, None, "rep"),
        P(None, ("rep", "exp")),
        P(None, ("rep", "exp")),
        P(),
        P(("rep", "exp")),
        P(),
        P(),
        P(("rep", "exp")),
        P(),
        P(("rep", "exp")),
        P("exp", None, None),
        P("exp", None, "rep"),
        P(None, ("rep", "exp")),
    )
    out_specs = (
        P(),
        P(),
        P(),
        P(None, ("rep", "exp"), None),
        P(None, ("rep", "exp")),
        P(),
        P(None, ("rep", "exp"), None),
        P(("rep", "exp"), None),
        P(("rep", "exp")),
        P(),
        P(("rep", "exp"), None),
        P(None, ("rep", "exp")),
        P(),
        P(("rep", "exp")),
        P(None, ("rep", "exp")),
        P(None, ("rep", "exp")),
        P(),
        P(("rep", "exp")),
        P(None, ("rep", "exp")),
        P("exp", None, None, "rep"),
        P("exp", None, None),
        P("exp", None, "rep"),
        P("exp", None, None, "rep"),
        P(None, ("rep", "exp")),
        P(None, ("rep", "exp")),
        P(None, ("rep", "exp")),
    )
    return jax.shard_map(shards, mesh=mesh, in_specs=in_specs, out_specs=out_specs, check_vma=False)
```

```python
import functools
import math

import jax
import jax.numpy as jnp
from jax import lax
from jax.experimental import pallas as pl
from jax.experimental.pallas import tpu as pltpu
from jax.sharding import PartitionSpec as P

D = 768
HEAD = 64
FF = 3072
PATCHES = 576
CAP = 10
VOCAB_DEV = 171
EARLY = 256
EXTRA = 640
VECTOR_AT = 608
ROUTER_AT = 64
PAD = 8
LANES = 128


DECAY = 0.8
EPS_SQ = 1e-30
CLIP_NORM = 0.25
HIGHEST = lax.Precision.HIGHEST
MESH = pl.DeviceIdType.MESH

Y_SWAP = ((0, 2), (1, 3), (2, 0), (3, 1))
CORE_SWAP = ((0, 1), (1, 0), (2, 3), (3, 2))


def plain_dot(left, right):
    return jnp.dot(left, right, preferred_element_type=jnp.float32)


def over_rows(left, right):
    return lax.dot_general(
        left, right, (((0,), (0,)), ((), ())), preferred_element_type=jnp.float32
    )


def over_last(left, right):
    return lax.dot_general(
        left, right, (((1,), (1,)), ((), ())), preferred_element_type=jnp.float32
    )


def place():
    rep = lax.axis_index("rep")
    line = lax.axis_index("exp")
    y = lax.div(rep, 2) * 2 + lax.rem(lax.div(line, 4), 2)
    return {"y": y, "core": lax.rem(rep, 2), "x": lax.div(line, 8), "z": lax.rem(line, 4)}


def device(at):
    return {
        "rep": lax.div(at["y"], 2) * 2 + at["core"],
        "exp": at["x"] * 8 + lax.rem(at["y"], 2) * 4 + at["z"],
    }


def moved(at, axis, by):
    return {**at, axis: lax.rem(at[axis] + by, 2 if axis == "core" else 4)}


def box(ref, at, free, core=False):
    whole = slice(None)
    hi = whole if "y" in free else lax.div(at["y"], 2)
    low = whole if "y" in free else lax.rem(at["y"], 2)
    x = whole if "x" in free else at["x"]
    z = whole if "z" in free else at["z"]
    if core:
        return ref.at[hi, at["core"], x, low, z]
    return ref.at[hi, x, low, z]


NEAR = tuple((y, core) for y in range(4) for core in range(2) if y or core)
PLANE = tuple((x, z) for x in range(4) for z in range(4) if x or z)


def near_peer(at, by):
    return moved(moved(at, "y", by[0]), "core", by[1])


def greet(at, near=False):
    barrier = pltpu.get_barrier_semaphore()
    peers = [moved(at, axis, by) for axis in ("x", "z") for by in (1, 2, 3)]
    peers += [near_peer(at, by) for by in NEAR if near or not (by[0] and by[1])]
    for peer in peers:
        pl.semaphore_signal(barrier, inc=1, device_id=device(peer), device_id_type=MESH)
    pl.semaphore_wait(barrier, len(peers))


def remote(src, dst, sems, index, peer):
    return pltpu.make_async_remote_copy(
        src_ref=src,
        dst_ref=dst,
        send_sem=sems[0].at[index],
        recv_sem=sems[1].at[index],
        device_id=device(peer),
        device_id_type=MESH,
    )


class Staged:
    def __init__(self, inputs, outputs):
        self.inputs, self.outputs, self.given = inputs, outputs, []

    def need(self, *indices):
        for index in indices:
            self.inputs[index].wait()

    def give(self, *indices):
        for index in indices:
            self.outputs[index].start()
            self.given.append(self.outputs[index])


def pin(value):
    return pltpu.with_memory_space_constraint(value, pltpu.HBM)


def staged_call(body, operands, shapes, scratch, far_in, far_out, **params):
    inputs, outputs = len(operands), len(shapes)
    raw, raw_out = params.pop("raw", ()), params.pop("raw_out", ())

    def kernel(*refs):
        refs = list(refs)
        stages = refs[inputs + outputs + len(scratch) :]
        stage_in, stages = stages[: len(far_in)], stages[len(far_in) :]
        stage_out, (sem_in, sem_out) = stages[: len(far_out)], stages[len(far_out) :]
        fetches, stores = {}, {}
        for number, index in enumerate(far_in):
            fetches[index] = pltpu.make_async_copy(refs[index], stage_in[number], sem_in.at[number])
            fetches[index].start()
            refs[index] = stage_in[number]
        for number, index in enumerate(far_out):
            stores[index] = pltpu.make_async_copy(stage_out[number], refs[inputs + index], sem_out.at[number])
            refs[inputs + index] = stage_out[number]
        staged = Staged(fetches, stores)
        body(staged, *refs[: inputs + outputs + len(scratch)])
        for copy in staged.given:
            copy.wait()

    anywhere, near = pl.BlockSpec(memory_space=pl.ANY), pl.BlockSpec(memory_space=pltpu.VMEM)
    return pl.pallas_call(
        kernel,
        out_shape=[
            pltpu.HBM(*shape) if index in far_out + raw_out else jax.ShapeDtypeStruct(*shape)
            for index, shape in enumerate(shapes)
        ],
        in_specs=[anywhere if index in far_in or index in raw else near for index in range(inputs)],
        out_specs=[anywhere if index in far_out + raw_out else near for index in range(outputs)],
        scratch_shapes=list(scratch)
        + [pltpu.VMEM(operands[index].shape, operands[index].dtype) for index in far_in]
        + [pltpu.VMEM(*shapes[index]) for index in far_out]
        + [pltpu.SemaphoreType.DMA((max(1, len(far_in)),)), pltpu.SemaphoreType.DMA((max(1, len(far_out)),))],
        compiler_params=pltpu.CompilerParams(
            collective_id=params["collective_id"],
            has_side_effects=True,
            vmem_limit_bytes=params["megabytes"] * 2**20,
        ),
        name=params["name"],
    )(*(pin(value) if index in far_in or index in raw else value for index, value in enumerate(operands)))


ORDERS = (("x", "y", "z"), ("y", "z", "x"), ("z", "x", "y"))


def gather_kernel(own_squares, own_extra, patches, ids, experts, *refs):
    squares, extra, spare, image, image_ids, experts_low, experts_in, across_part = refs[:5], *refs[5:12]
    outs, (x_ref, wide, narrow, send, recv, local, local_in, local_out) = refs[12:15], refs[15:]
    at = place()
    sems = (send, recv)
    value = own_extra[...]
    high = value.astype(jnp.bfloat16).astype(jnp.float32)
    lane = lax.broadcasted_iota(jnp.int32, value.shape, 1)
    rest = jnp.where(lane < PATCHES, value - high, 0.0)
    high = jnp.where(lane >= VECTOR_AT + 16, value - high, high)
    blank = jnp.zeros((2, D), jnp.float32)
    for part, rows in enumerate(
        (
            (own_squares[0], rest[0:2], own_squares[1], rest[2:4]),
            (own_squares[2], rest[4:6], own_squares[3], blank),
            (own_squares[4], blank, high, blank),
        )
    ):
        x_ref[part] = jnp.concatenate(rows).astype(jnp.bfloat16)
    own = []
    for part in range(3):
        own.append(
            pltpu.make_async_copy(
                x_ref.at[part], box(outs[part], at, (), True), local.at[part]
            )
        )
        own[part].start()
    micro = lax.div(at["y"], 2)
    kept = [
        pltpu.make_async_copy(patches.at[micro], image.at[micro], local.at[3]),
        pltpu.make_async_copy(ids.at[micro], image_ids.at[micro], local.at[4]),
    ]
    for copy in kept:
        copy.start()

    def lines(ref, step):
        return ref.at[step // 3, pl.ds(step % 3 * 256, 256)]

    def fetch(step):
        return pltpu.make_async_copy(lines(experts, step), wide.at[step % 2], local_in.at[step % 2])

    def store(step):
        return pltpu.make_async_copy(narrow.at[step % 2], lines(experts_low, step), local_out.at[step % 2])

    def store_in(step):
        lines_in = experts_in.at[pl.ds(step % 3 * 256, 256)]
        return pltpu.make_async_copy(narrow.at[step % 2], lines_in, local_out.at[2 + step % 2])

    def round_experts(step):
        if step < 5:
            fetch(step + 1).start()
        fetch(step).wait()
        if step >= 2:
            store(step - 2).wait()
            if step < 5:
                store_in(step - 2).wait()
        narrow[step % 2] = wide[step % 2].astype(jnp.bfloat16)
        store(step).start()
        if step < 3:
            store_in(step).start()

    fetch(0).start()
    greet(at)
    flights = {}

    def launch(part, stage):
        axes = ORDERS[part]
        view = box(outs[part], at, axes[:stage], True)
        source = x_ref.at[part] if stage == 0 else view
        for by in (1, 2, 3):
            copy = remote(source, view, sems, part * 13 + stage * 3 + by - 1, moved(at, axes[stage], by))
            copy.start()
            flights[part, stage, by] = copy

    def forward(part, by):
        axes = ORDERS[part]
        view = box(outs[part], moved(at, axes[2], 4 - by), axes[:2], True)
        copy = remote(view, view, sems, part * 13 + 9 + by, moved(at, "core", 1))
        copy.start()
        flights[part, 3, by] = copy

    for part in range(3):
        launch(part, 0)
    trades = [
        remote(patches.at[1 - micro], image.at[micro], sems, 39, moved(at, "y", 2)),
        remote(ids.at[1 - micro], image_ids.at[micro], sems, 40, moved(at, "y", 2)),
    ]
    for copy in trades:
        copy.start()
    round_experts(0)
    round_experts(1)
    for stage in (1, 2):
        for part in range(3):
            if stage == 1:
                own[part].wait()
            for by in (1, 2, 3):
                flights[part, stage - 1, by].wait_recv()
            launch(part, stage)
            if stage == 2:
                forward(part, 0)
        round_experts(2 * stage)
        round_experts(2 * stage + 1)
    store(4).wait()
    store(5).wait()
    for by in (1, 3, 2):
        for part in range(3):
            flights[part, 2, by].wait_recv()
            forward(part, by)
    early = remote(experts_low.at[1, pl.ds(0, EARLY)], across_part, sems, 41, moved(at, "y", 2))
    early.start()

    row = lax.broadcasted_iota(jnp.int32, (96, 256), 0)
    column = lax.broadcasted_iota(jnp.int32, (96, 256), 1)
    base = lax.div(row, 6) * 16
    inside = lax.rem(row, 6)

    def packer(offset):
        return (column == base + offset + inside).astype(jnp.bfloat16)

    first, second = packer(0), packer(8)
    low_first = jnp.where(inside < 2, packer(6), jnp.where(inside < 4, packer(12), 0)).astype(jnp.bfloat16)
    low_second = jnp.where(inside < 4, 0, packer(2)).astype(jnp.bfloat16)
    packers = [
        jnp.concatenate([first, second, low_first]),
        jnp.concatenate([first, second, low_second]),
        jnp.concatenate([first, second]),
    ]

    def pack(core):
        def step(index, carry):
            high, half = lax.div(index, 2), lax.rem(index, 2)
            place_out = pl.ds(pl.multiple_of((high * 4 + core * 2 + half) * 96, 96), 96)
            packed = []
            for part in range(3):
                block = outs[part][high, core, pl.ds(half * 2, 2)].reshape(256, D)
                packed.append(plain_dot(packers[part], block))
            for k in range(5):
                low = packed[k // 2][96 * (k % 2) : 96 * (k % 2) + 96]
                squares[k][place_out, :] = low.astype(jnp.bfloat16)
            extra[place_out, :] = packed[2][96:].astype(jnp.bfloat16)
            spare[place_out, :] = (packed[0][192:] + packed[1][192:]).astype(jnp.bfloat16)
            return carry

        lax.fori_loop(0, 4, step, 0)

    pack(at["core"])
    for key, copy in flights.items():
        if key[1] == 3:
            copy.wait_recv()
    pack(1 - at["core"])
    for copy in [*kept, *trades, early]:
        copy.wait()
    for copy in flights.values():
        copy.wait_send()


def gather_all(squares, extra, patches, ids, experts):
    shape = (2, 2, 4, 2, 4, 16, D)
    return pl.pallas_call(
        gather_kernel,
        out_shape=[jax.ShapeDtypeStruct((D, D), jnp.bfloat16)] * 7
        + [pltpu.HBM(value.shape, value.dtype) for value in (patches, ids)]
        + [pltpu.HBM(experts.shape, jnp.bfloat16), pltpu.HBM(experts.shape[1:], jnp.bfloat16)]
        + [pltpu.HBM((EARLY, D), jnp.bfloat16)],
        in_specs=[pl.BlockSpec(memory_space=pltpu.VMEM)] * 2 + [pl.BlockSpec(memory_space=pl.ANY)] * 3,
        out_specs=[pl.BlockSpec(memory_space=pltpu.VMEM)] * 7 + [pl.BlockSpec(memory_space=pl.ANY)] * 5,
        scratch_shapes=[pltpu.VMEM(shape, jnp.bfloat16)] * 3
        + [
            pltpu.VMEM((3, 16, D), jnp.bfloat16),
            pltpu.VMEM((2, 256, D), jnp.float32),
            pltpu.VMEM((2, 256, D), jnp.bfloat16),
            pltpu.SemaphoreType.DMA((42,)),
            pltpu.SemaphoreType.DMA((42,)),
            pltpu.SemaphoreType.DMA((5,)),
            pltpu.SemaphoreType.DMA((2,)),
            pltpu.SemaphoreType.DMA((4,)),
        ],
        compiler_params=pltpu.CompilerParams(
            collective_id=0, has_side_effects=True, vmem_limit_bytes=24 * 2**20
        ),
        name="gather_weights",
    )(squares, extra, pin(patches), pin(ids), pin(experts))


def gradients_kernel(
    staged, patches, hidden_one, mixed, dembed, dquery, dkey, dvalue, dafter, hidden_two, dgate, sums, final_sums,
    head_grad, loss, square_rows, router_rows, part_grads, own, rows_y, rows_last, drows_y, drows_last, *refs,
):
    outs, totals, kept, expert_cols, refs = refs[:3], refs[3], refs[4], refs[5], refs[3:]
    lefts, tables, rights, left_got, table_got, right_got, few_mine, few_got, few_t, partial, grads = refs[3:14]
    first, total_one, second, total_two, third = (refs[14 + 3 * i : 17 + 3 * i] for i in range(5))
    core_sems, sems = refs[29:31], refs[31:33]
    parts, total_sems, (act_set, dpre_set, rows_t, drows_t) = refs[33], refs[34:36], refs[36:40]
    at = place()
    other = moved(at, "core", 1)
    count = patches.shape[0]
    part_rows = D // 4
    staged.need(3, 4, 5, 6, 7)
    for index, ref in enumerate((dembed, dquery, dkey, dvalue, dafter)):
        rights[index] = ref[...]
    greet(at, near=True)
    copies = [remote(rights, right_got, core_sems, 0, other)]
    copies[0].start()
    staged.need(0, 1, 2, 8)
    for index, ref in enumerate((patches, hidden_one, mixed)):
        lefts[index] = ref[...].T.reshape(4, part_rows, count)
    padded = jnp.concatenate([dembed[...], jnp.zeros((3 * LANES - count, D), jnp.bfloat16)])
    tables[...] = padded.T.reshape(4, part_rows, 3 * LANES)
    for half in range(2):
        source = lefts.at[:, 2 * half + other["core"]]
        copies.append(remote(source, left_got.at[:, half], core_sems, 1 + half, other))
        source = tables.at[2 * half + other["core"]]
        copies.append(remote(source, table_got.at[half], core_sems, 3 + half, other))
    few_mine[:32, :] = plain_dot(dgate[...].T, hidden_two[...])[64:96]
    few_mine[32:40, :] = sums[...]
    few_mine[40:48, :] = final_sums[...]
    copies.append(remote(few_mine, few_got, core_sems, 5, other))
    for copy in copies[1:]:
        copy.start()

    pairs = ((0, 0), (1, 1), (1, 2), (1, 3), (2, 4))

    def own_product(half, carry):
        rows = 2 * half + at["core"]
        for index, (left, right) in enumerate(pairs):
            partial[index, half] = plain_dot(lefts[left, rows], rights[right])
        return carry

    lax.fori_loop(0, 2, own_product, 0)
    for copy in copies:
        copy.wait_recv()
    few = few_mine[...] + few_got[...]
    few_high = few.astype(jnp.bfloat16)
    few_low = (few - few_high.astype(jnp.float32)).astype(jnp.bfloat16)
    blank = jnp.zeros((32, D), jnp.bfloat16)
    few_rows = jnp.concatenate([blank, few_high[:32], few_low[:32], few_high[32:], few_low[32:]])
    few_t[...] = few_rows.T.reshape(4, part_rows, LANES)

    def spread(offset):
        shape = (part_rows // 6 * 2 * PAD, part_rows)
        row, column = iota(shape, 0), iota(shape, 1)
        inside = lax.rem(row, 2 * PAD) - offset
        hit = (inside >= 0) & (inside < 6) & (column == lax.div(row, 2 * PAD) * 6 + inside)
        return hit.astype(jnp.bfloat16)

    spreads = jnp.concatenate([spread(0), spread(PAD)], axis=1)

    def finish(part, half):
        rows = 2 * half + at["core"]
        pieces = []
        for index in (2 * part, 2 * part + 1):
            if index < 5:
                left, right = pairs[index]
                value = partial[index, half] + plain_dot(left_got[left, half], right_got[right])
                pieces.append(value.astype(jnp.bfloat16))
            else:
                mine, theirs = tables[rows], table_got[half]
                is_first = at["core"] == 0
                low = jnp.where(is_first, mine, theirs)
                high = jnp.where(is_first, theirs, mine)
                high = jnp.concatenate(
                    [high[:, : 2 * LANES], high[:, 2 * LANES :] + few_t[rows]], axis=1
                )
                pieces.append(jnp.concatenate([low, high], axis=1))
        value = plain_dot(spreads, jnp.concatenate(pieces)).astype(jnp.bfloat16)
        grads[part, half] = value.reshape(4, 2, 4, 2 * PAD, D)

    def names(axis):
        return ("h", "l") if axis == "y" else (axis,)

    def pick(letter, where, axis):
        if letter not in names(axis):
            return slice(None)
        if letter == "h":
            return lax.div(where["y"], 2)
        if letter == "l":
            return lax.rem(where["y"], 2)
        return where[axis]

    def part_of(source, where, axes, stage):
        if stage == 0:
            return box(source, where, axes[:2])
        if stage == 1:
            left = [letter for letter in ("h", "x", "l", "z") if letter not in names(axes[2])]
            return source.at[tuple(pick(letter, where, axes[1]) for letter in left)]
        return source.at[tuple(pick(letter, where, axes[0]) for letter in names(axes[0]))]

    sources = ([grads.at[part] for part in range(3)], total_one, total_two)
    landings = (first, second, third)
    targets = (total_one, total_two, outs)
    flights = {}

    def launch(part, stage):
        axes = ORDERS[part]
        axis = axes[2 - stage]
        flights[part, stage] = []
        for by in (1, 2, 3):
            peer = moved(at, axis, by)
            view = part_of(sources[stage][part], peer, axes, stage)
            copy = remote(view, landings[stage][part].at[by - 1], sems, part * 9 + stage * 3 + by - 1, peer)
            copy.start()
            flights[part, stage].append(copy)

    for part in (2, 0, 1):
        for half in range(2):
            finish(part, half)
        launch(part, 0)
    head_squared = jnp.sum(head_grad[...] * head_grad[...], axis=0, keepdims=True)

    staged.need(16, 17, 18, 19, 20, 21)
    for which in range(2):
        kept[which] = part_grads[which]
    quarter_set(kept, own, rows_y, drows_y, act_set, dpre_set, rows_t, drows_t)
    for stage in range(3):
        if stage == 1:
            quarter_set(kept, own, rows_last, drows_last, act_set, dpre_set, rows_t, drows_t)
            staged.give(4)
            expert_rows = []
            for which in range(2):
                square = kept[which] * kept[which]
                expert_rows.append(jnp.broadcast_to(jnp.sum(square, axis=1, keepdims=True), (D, LANES)).T[0:1])
                expert_cols[which : which + 1, :] = jnp.sum(square, axis=0, keepdims=True)
            expert_rows = jnp.concatenate(expert_rows)
            expert_norm = jnp.sum(jnp.sum(expert_rows, axis=1, keepdims=True), axis=0, keepdims=True)
        for part in (2, 0, 1):
            for copy in flights[part, stage]:
                copy.wait_recv()
            landing = landings[stage][part]
            terms = [part_of(sources[stage][part], at, ORDERS[part], stage)[...]]
            terms = [term.astype(jnp.float32) for term in terms + [landing[i] for i in range(3)]]
            target = targets[stage][part]
            target[...] = ((terms[0] + terms[1]) + (terms[2] + terms[3])).astype(target.dtype)
            if stage < 2:
                launch(part, stage + 1)

    tail = outs[2][PAD:, EXTRA:]
    lane = iota(tail.shape, 1)
    router = tail + pltpu.roll(tail, LANES - GROUP, 1)
    vectors = tail + pltpu.roll(tail, LANES - 16, 1)
    tail = jnp.where(lane < 32, tail, jnp.where(lane < 64, router, jnp.where((lane >= 96) & (lane < 112), vectors, 0.0)))
    outs[2][PAD:, EXTRA:] = tail
    squared = [outs[k // 2][PAD * (k % 2) : PAD * (k % 2) + PAD, :] for k in range(6)]
    squared = [jnp.sum(value * value, axis=0, keepdims=True) for value in squared]
    spot = iota((1, D), 1)
    last = jnp.where(spot == 1, expert_norm, 0.0) + jnp.where(spot == 0, loss[...], 0.0)
    for k in range(5):
        last = last + jnp.where(spot == 2 + k, jnp.sum(square_rows[k : k + 1, :], axis=1, keepdims=True), 0.0)
    last = last + jnp.where(spot == 7, jnp.sum(router_rows[...], axis=1, keepdims=True), 0.0)
    parts[0, 0] = jnp.concatenate(squared[:5] + [head_squared, squared[5], last])
    parts[0, 1] = jnp.concatenate([expert_rows, jnp.zeros((PAD - 2, D), jnp.float32)])
    mine = parts.at[0]
    trips = []
    for number, by in enumerate(NEAR):
        whole = by[0] in (0, 2)
        slot = parts.at[1 + at["y"] * 2 + at["core"]]
        source, target = (mine, slot) if whole else (mine.at[0], slot.at[0])
        trips.append(remote(source, target, total_sems, number, near_peer(at, by)))
        trips[-1].start()
    parts[1 + at["y"] * 2 + at["core"]] = mine[...]
    for trip in trips:
        trip.wait()
    value = parts[1, 0]
    for index in range(1, 8):
        value = value + parts[1 + index, 0]
    parts[9, 0] = value
    low = lax.rem(at["y"], 2) * 2
    totals[PAD:, :] = (parts[1 + low, 1] + parts[2 + low, 1]) + (parts[5 + low, 1] + parts[6 + low, 1])
    total = parts.at[9]
    for stage, axis in enumerate(("z", "x")):
        base = 10 + 5 * stage
        trips = []
        for by in (1, 2, 3):
            number = 7 + 3 * stage + by - 1
            slot = parts.at[base + at[axis], 0]
            trips.append(remote(total.at[0], slot, total_sems, number, moved(at, axis, by)))
            trips[-1].start()
        parts[base + at[axis], 0] = total[0]
        for trip in trips:
            trip.wait()
        value = parts[base, 0]
        for index in range(1, 4):
            value = value + parts[base + index, 0]
        parts[base + 4, 0] = value
        total = parts.at[base + 4]
    totals[:PAD, :] = total[0]
    for copy in copies:
        copy.wait_send()
    for launched in flights.values():
        for copy in launched:
            copy.wait_send()


def shared_gradients(*operands):
    count = operands[0].shape[0]
    low, wide = jnp.bfloat16, jnp.float32
    block = (2 * PAD, D)
    ones = [{"x": (2, 2, 4), "y": (4, 4), "z": (2, 4, 2)}[axes[2]] for axes in ORDERS]
    twos = [(2, 2) if axes[0] == "y" else (4,) for axes in ORDERS]
    rows = D // 4
    scratch = [
        pltpu.VMEM((3, 4, rows, count), low),
        pltpu.VMEM((4, rows, 3 * LANES), low),
        pltpu.VMEM((5, count, D), low),
        pltpu.VMEM((3, 2, rows, count), low),
        pltpu.VMEM((2, rows, 3 * LANES), low),
        pltpu.VMEM((5, count, D), low),
        pltpu.VMEM((48, D), wide),
        pltpu.VMEM((48, D), wide),
        pltpu.VMEM((4, rows, LANES), low),
        pltpu.VMEM((5, 2, rows, D), wide),
        pltpu.VMEM((3, 2, 4, 2, 4) + block, low),
    ]
    scratch += [pltpu.VMEM((3,) + one + block, low) for one in ones]
    scratch += [pltpu.VMEM(one + block, kind) for one, kind in zip(ones, (low, low, wide))]
    scratch += [pltpu.VMEM((3,) + two + block, kind) for two, kind in zip(twos, (low, low, wide))]
    scratch += [pltpu.VMEM(two + block, wide) for two in twos]
    scratch += [pltpu.VMEM((3,) + block, wide)] * 3
    scratch += [pltpu.SemaphoreType.DMA((6,))] * 2 + [pltpu.SemaphoreType.DMA((27,))] * 2
    scratch += [pltpu.VMEM((20, 2, PAD, D), wide)] + [pltpu.SemaphoreType.DMA((13,))] * 2
    scratch += [pltpu.VMEM((TOTAL, D), low)] * 2 + [pltpu.VMEM((D, TOTAL), low)] * 2
    return staged_call(
        gradients_kernel,
        operands,
        [(block, wide)] * 4 + [((2, D, D), wide), ((2, D), wide)],
        scratch,
        (3, 4, 5, 6, 7, 0, 1, 2, 8, 16, 17, 18, 19, 20, 21),
        (4,),
        collective_id=1,
        megabytes=57,
        name="shared_gradients",
    )


def meet_core(at):
    barrier = pltpu.get_barrier_semaphore()
    other = moved(at, "core", 1)
    pl.semaphore_signal(barrier, inc=1, device_id=device(other), device_id_type=MESH)
    pl.semaphore_wait(barrier, 1)
    return other


CHUNK = 48


def chunks(count, step, start=0):
    lax.fori_loop(0, count // CHUNK, lambda i, c: step(pl.ds(pl.multiple_of(i * CHUNK, CHUNK), CHUNK), c), start)


def centre(value):
    centred = value - jnp.mean(value, axis=-1, keepdims=True)
    spread = jnp.mean(centred * centred, axis=-1, keepdims=True)
    return centred * lax.rsqrt(spread + 1e-06), lax.rsqrt(spread + 1e-06)


def norm_back(value, grad, gain):
    normed, rate = centre(value)
    scaled = grad * gain
    inner = (
        scaled
        - jnp.mean(scaled, axis=-1, keepdims=True)
        - normed * jnp.mean(scaled * normed, axis=-1, keepdims=True)
    )
    return rate * inner, jnp.sum(grad * normed, axis=0, keepdims=True), jnp.sum(grad, axis=0, keepdims=True)


def attend_kernel(
    staged, x_ref, w0, w1, w2, w3, w4, extra, spare, ids,
    embed, hidden_one, query, keys, values, mixed, after, hidden_two, gate_probs, gates, lse,
    vec, router, target, target_t, hidden_kept, w1_kept, w2_kept, w3_kept, w4_kept,
    turned, local, send, recv,
):
    at = place()
    sems = (send, recv)
    saves = [
        pltpu.make_async_copy(source, target_ref, local.at[index])
        for index, (source, target_ref) in enumerate(
            ((w1, w1_kept), (w2, w2_kept), (w3, w3_kept), (w4, w4_kept), (hidden_two, hidden_kept))
        )
    ]
    for copy in saves[:4]:
        copy.start()
    other = meet_core(at)
    rows = x_ref.shape[0]
    staged.need(8)
    turned[...] = (
        extra[:, :EXTRA].astype(jnp.float32) + spare[:, :EXTRA].astype(jnp.float32)
    ).T
    vec[...] = turned[VECTOR_AT : VECTOR_AT + 16, :] + turned[VECTOR_AT + 16 : VECTOR_AT + 32, :]
    router[...] = extra[:, EXTRA - LANES : EXTRA]

    block = rows // 2
    earlier = (iota((block, block), 1) < iota((block, block), 0)).astype(jnp.bfloat16)
    lane = iota((block, LANES), 1)
    for number in range(2):
        part = slice(number * block, (number + 1) * block)
        hits = [(lane == ids[part, k : k + 1]).astype(jnp.float32) for k in range(2)]
        before = plain_dot(earlier, (hits[0] + hits[1]).astype(jnp.bfloat16))
        spots = []
        for k in range(2):
            named = ids[part, k : k + 1]
            slot = jnp.sum(hits[k] * before, axis=-1, keepdims=True).astype(jnp.int32) + number * CAP
            spots.append(
                jnp.where(slot < SLOTS, named * SLOTS + slot, MAIN + named * TAIL + slot - SLOTS)
            )
        target[part, :] = jnp.where(lane == 0, spots[0], jnp.where(lane == 1, spots[1], 0))
    target_t[...] = target[...].astype(jnp.float32).T[:PAD].astype(jnp.int32)

    staged.need(0)
    embed[...] = plain_dot(x_ref[...], w0[...])

    def first_norm(index, carry):
        part = pl.ds(pl.multiple_of(index * CHUNK, CHUNK), CHUNK)
        line = at["core"] * block + index * CHUNK + jnp.where(index * CHUNK < block, 0, block)
        value = embed[part, :] + vec[0:1, :] + turned[pl.ds(pl.multiple_of(line, CHUNK), CHUNK), :]
        embed[part, :] = value
        normed, _ = centre(value)
        hidden_one[part, :] = (normed * vec[1:2, :] + vec[2:3, :]).astype(jnp.bfloat16)
        return carry

    lax.fori_loop(0, rows // CHUNK, first_norm, 0)
    keys[0] = plain_dot(hidden_one[...], w2[...]).astype(jnp.bfloat16)
    send_keys = remote(keys.at[0], keys.at[1], sems, 0, other)
    send_keys.start()
    values[0] = (plain_dot(hidden_one[...], w3[...]) + vec[4:5, :]).astype(jnp.bfloat16)
    send_values = remote(values.at[0], values.at[1], sems, 1, other)
    send_values.start()
    query[...] = (plain_dot(hidden_one[...], w1[...]) + vec[3:4, :]).astype(jnp.bfloat16)
    send_keys.wait()
    send_values.wait()
    staged.give(0, 1, 2, 3, 4)

    def heads(index, carry):
        lanes = pl.ds(pl.multiple_of(index * LANES, LANES), LANES)
        query_two = query[:, lanes]
        key_two = keys[:, :, lanes].reshape(2 * rows, LANES)
        value_t = values[:, :, lanes].reshape(2 * rows, LANES).T
        left = lax.broadcasted_iota(jnp.int32, (rows, LANES), 1) < HEAD
        outs = []
        for half in range(2):
            own = jnp.where(left if half == 0 else ~left, query_two, jnp.zeros_like(query_two))
            scores = over_last(key_two, own) * HEAD ** (-0.5)
            most = jnp.max(scores, axis=0, keepdims=True)
            raw = jnp.exp(scores - most)
            total = jnp.sum(raw, axis=0, keepdims=True)
            lse[pl.ds(index * 2 + half, 1), :] = most + jnp.log(total)
            probs = (raw * (1.0 / total)).astype(jnp.bfloat16)
            outs.append(plain_dot(value_t[half * HEAD : (half + 1) * HEAD], probs))
        mixed[:, lanes] = jnp.concatenate(outs).T.astype(jnp.bfloat16)
        return carry

    lax.fori_loop(0, D // LANES, heads, 0)
    staged.give(5)
    after[...] = plain_dot(mixed[...], w4[...])

    def second_norm(part, carry):
        value = embed[part, :] + after[part, :] + vec[5:6, :]
        after[part, :] = value
        normed, _ = centre(value)
        low = (normed * vec[6:7, :] + vec[7:8, :]).astype(jnp.bfloat16)
        hidden_two[part, :] = low
        logits = plain_dot(low, router[...])
        lane = iota(logits.shape, 1) - ROUTER_AT
        logits = jnp.where((lane >= 0) & (lane < GROUP), logits, -jnp.inf)
        raw = jnp.exp(logits - jnp.max(logits, axis=-1, keepdims=True))
        probs = raw / jnp.sum(raw, axis=-1, keepdims=True)
        gate_probs[part, :] = probs
        first, second = (
            jnp.sum(jnp.where(lane == ids[part, k : k + 1], probs, 0.0), axis=-1, keepdims=True) for k in range(2)
        )
        gates[part, :] = jnp.where(lane == -ROUTER_AT, first, second)
        return carry

    chunks(rows, second_norm)
    staged.give(6)
    saves[4].start()
    for copy in saves:
        copy.wait()


def attend(patch_rows, squares, extra, spare, ids):
    rows = patch_rows.shape[0]
    low, wide = jnp.bfloat16, jnp.float32
    shapes = [
        ((rows, D), wide), ((rows, D), low), ((rows, D), low), ((2, rows, D), low), ((2, rows, D), low),
        ((rows, D), low), ((rows, D), wide), ((rows, D), low), ((rows, LANES), wide), ((rows, LANES), wide), ((16, rows), wide),
        ((16, D), wide), ((D, LANES), low), ((rows, LANES), jnp.int32), ((PAD, rows), jnp.int32),
        ((rows, D), low), ((D, D), low), ((D, D), low), ((D, D), low), ((D, D), low),
    ]
    sems = pltpu.SemaphoreType.DMA
    return staged_call(
        attend_kernel,
        (patch_rows, *squares, extra, spare, ids),
        shapes,
        [pltpu.VMEM((EXTRA, D), wide), sems((5,)), sems((2,)), sems((2,))],
        (0, 8),
        tuple(range(7)),
        raw_out=(15, 16, 17, 18, 19),
        collective_id=6,
        megabytes=20,
        name="attend",
    )


def attend_back_kernel(
    staged, dafter_in, dhidden, dgate, embed, after, query, keys, values, lse, w1, w2, w3, w4, vec, router,
    dafter_low, dquery, dkey, dvalue, dembed_low, sums,
    dafter, dmixed, dkey_own, dvalue_own, dkey_other, dvalue_other, dkey_got, dvalue_got, wide, send, recv,
):
    at = place()
    sems = (send, recv)
    other = meet_core(at)
    rows = dafter_in.shape[0]
    pairs = D // LANES
    zero = jnp.zeros((1, D), jnp.float32)
    wide[...] = over_last(dgate[...], router[...])
    staged.need(0, 1, 4)

    def second_norm(index, carry):
        part = pl.ds(pl.multiple_of(index * CHUNK, CHUNK), CHUNK)
        grad = wide[part, :] + dhidden[part, :]
        back, gain, shift = norm_back(after[part, :], grad, vec[6:7, :])
        total = dafter_in[part, :] + back
        dafter[part, :] = total
        dafter_low[part, :] = total.astype(jnp.bfloat16)
        return carry[0] + jnp.sum(total, axis=0, keepdims=True), carry[1] + gain, carry[2] + shift

    bias, gain, shift = lax.fori_loop(0, rows // CHUNK, second_norm, (zero, zero, zero))
    sums[5:6, :] = bias
    sums[6:7, :] = gain
    sums[7:8, :] = shift
    staged.give(0)
    staged.need(12)
    dmixed[...] = over_last(dafter_low[...], w4[...]).astype(jnp.bfloat16)
    staged.need(5, 6, 7)

    def flights(index):
        return (
            remote(dkey_other.at[index], dkey_got.at[index], sems, index, other),
            remote(dvalue_other.at[index], dvalue_got.at[index], sems, pairs + index, other),
        )

    def heads(index, carry):
        lanes = pl.ds(pl.multiple_of(index * LANES, LANES), LANES)
        query_two = query[:, lanes]
        dmixed_two = dmixed[:, lanes]
        key_two = keys[:, :, lanes].reshape(2 * rows, LANES)
        value_two = values[:, :, lanes].reshape(2 * rows, LANES)
        key_t = key_two.T
        left = lax.broadcasted_iota(jnp.int32, (rows, LANES), 1) < HEAD
        dkey_two = jnp.zeros((2 * rows, LANES), jnp.float32)
        dvalue_two = jnp.zeros((2 * rows, LANES), jnp.float32)
        outs = []
        for half in range(2):
            mask = left if half == 0 else ~left
            own = jnp.where(mask, query_two, jnp.zeros_like(query_two))
            down = jnp.where(mask, dmixed_two, jnp.zeros_like(dmixed_two))
            scores = over_last(key_two, own) * HEAD ** (-0.5)
            probs = jnp.exp(scores - lse[pl.ds(index * 2 + half, 1), :])
            dprobs = over_last(value_two, down)
            row_shift = jnp.sum(probs * dprobs, axis=0, keepdims=True)
            dscores = (probs * (dprobs - row_shift)).astype(jnp.bfloat16)
            dvalue_two = dvalue_two + plain_dot(probs.astype(jnp.bfloat16), down)
            dkey_two = dkey_two + plain_dot(dscores, own)
            outs.append(plain_dot(key_t[half * HEAD : (half + 1) * HEAD], dscores))
        dkey_two = dkey_two * HEAD ** (-0.5)
        dquery[:, lanes] = (jnp.concatenate(outs).T * HEAD ** (-0.5)).astype(jnp.bfloat16)
        dkey_own[index] = dkey_two[:rows]
        dkey_other[index] = dkey_two[rows:]
        dvalue_own[index] = dvalue_two[:rows]
        dvalue_other[index] = dvalue_two[rows:]
        for copy in flights(index):
            copy.start()
        return carry

    lax.fori_loop(0, pairs, heads, 0)

    def gather(index, carry):
        lanes = pl.ds(pl.multiple_of(index * LANES, LANES), LANES)
        for copy in flights(index):
            copy.wait()
        dkey[:, lanes] = (dkey_own[index] + dkey_got[index]).astype(jnp.bfloat16)
        dvalue[:, lanes] = (dvalue_own[index] + dvalue_got[index]).astype(jnp.bfloat16)
        return carry

    lax.fori_loop(0, pairs, gather, 0)
    staged.give(1, 2, 3)
    staged.need(3, 9, 10, 11)
    wide[...] = (
        over_last(dquery[...], w1[...]) + over_last(dkey[...], w2[...]) + over_last(dvalue[...], w3[...])
    )

    def first_norm(index, carry):
        part = pl.ds(pl.multiple_of(index * CHUNK, CHUNK), CHUNK)
        back, gain, shift = norm_back(embed[part, :], wide[part, :], vec[1:2, :])
        total = dafter[part, :] + back
        dembed_low[part, :] = total.astype(jnp.bfloat16)
        return (
            carry[0] + jnp.sum(total, axis=0, keepdims=True),
            carry[1] + gain,
            carry[2] + shift,
            carry[3] + jnp.sum(dquery[part, :].astype(jnp.float32), axis=0, keepdims=True),
            carry[4] + jnp.sum(dvalue[part, :].astype(jnp.float32), axis=0, keepdims=True),
        )

    for index, total in enumerate(lax.fori_loop(0, rows // CHUNK, first_norm, (zero,) * 5)):
        sums[index : index + 1, :] = total
    staged.give(4)


def attend_back(*operands):
    rows = operands[0].shape[0]
    low, wide = jnp.bfloat16, jnp.float32
    pairs = D // LANES
    sems = pltpu.SemaphoreType.DMA
    return staged_call(
        attend_back_kernel,
        operands,
        [((rows, D), low)] * 5 + [((8, D), wide)],
        [pltpu.VMEM((rows, D), wide), pltpu.VMEM((rows, D), low)]
        + [pltpu.VMEM((pairs, rows, LANES), wide)] * 6
        + [pltpu.VMEM((rows, D), wide), sems((2 * pairs,)), sems((2 * pairs,))],
        (0, 1, 4, 12, 5, 6, 7, 3, 9, 10, 11),
        (0, 1, 2, 3, 4),
        collective_id=7,
        megabytes=28,
        name="attend_back",
    )


SLOTS = 16
TAIL = 2 * CAP - SLOTS
WIRE = D + 2 * LANES
GROUP = 32
MAIN = GROUP * SLOTS
TOTAL = GROUP * (SLOTS + TAIL)


def iota(shape, axis):
    return lax.broadcasted_iota(jnp.int32, shape, axis)


def pack(block, main, tail):
    count = block.shape[0]
    block[:, :, :D] = main.astype(jnp.bfloat16).reshape(count, SLOTS, D)
    shape = (count * SLOTS, count * TAIL)
    row, column = iota(shape, 0), iota(shape, 1)
    spread = (lax.div(row, SLOTS) == lax.div(column, TAIL)) & (lax.rem(row, TAIL) == lax.rem(column, TAIL))
    wide = plain_dot(spread.astype(jnp.bfloat16), tail.astype(jnp.bfloat16))
    turn = lax.div(lax.rem(iota((count * SLOTS, LANES), 0), SLOTS), TAIL)
    for half, tiles in ((0, (0, 1, 2, 3)), (1, (4, 5))):
        packed = jnp.zeros((count * SLOTS, LANES), jnp.float32)
        for place_in, tile in enumerate(tiles):
            packed = jnp.where(turn == place_in, wide[:, tile * LANES : (tile + 1) * LANES], packed)
        block[:, :, D + half * LANES : D + (half + 1) * LANES] = packed.astype(jnp.bfloat16).reshape(
            count, SLOTS, LANES
        )


def unpack(block, rows, first, first_tail):
    count = block.shape[0]
    rows[first : first + count * SLOTS, :] = block[:, :, :D].reshape(count * SLOTS, D)
    shape = (count * TAIL, count * SLOTS)
    row, column = iota(shape, 0), iota(shape, 1)
    same = lax.div(column, SLOTS) == lax.div(row, TAIL)
    packed = block[:, :, D:].reshape(count * SLOTS, 2 * LANES)
    for turn in range(4):
        chosen = same & (lax.rem(column, SLOTS) == turn * TAIL + lax.rem(row, TAIL))
        part = plain_dot(chosen.astype(jnp.bfloat16), packed).astype(jnp.bfloat16)
        rows[first_tail : first_tail + count * TAIL, turn * LANES : (turn + 1) * LANES] = part[:, :LANES]
        if turn < 2:
            rows[first_tail : first_tail + count * TAIL, (4 + turn) * LANES : (5 + turn) * LANES] = part[
                :, LANES:
            ]


def meet_experts(at):
    barrier = pltpu.get_barrier_semaphore()
    me = lax.axis_index("exp")

    def greet_one(by, carry):
        peer = lax.rem(me + by, GROUP)
        pl.semaphore_signal(barrier, inc=1, device_id={"exp": peer}, device_id_type=MESH)
        return carry

    lax.fori_loop(1, GROUP, greet_one, 0)
    peers = moved(at, "core", 1), moved(at, "y", 2)
    for peer in peers:
        pl.semaphore_signal(barrier, inc=1, device_id=device(peer), device_id_type=MESH)
    return peers


def met_experts():
    pl.semaphore_wait(pltpu.get_barrier_semaphore(), GROUP + 1)


def deal(source, target, sems, forth, low, high, act):
    me = lax.axis_index("exp")

    def one(by, carry):
        peer = lax.rem(me + by, GROUP) if forth else lax.rem(me + GROUP - by, GROUP)
        copy = pltpu.make_async_remote_copy(
            src_ref=source.at[peer] if forth else source.at[by],
            dst_ref=target.at[by] if forth else target.at[me],
            send_sem=sems[0].at[by],
            recv_sem=sems[1].at[by],
            device_id={"exp": peer},
            device_id_type=MESH,
        )
        act(copy)
        return carry

    lax.fori_loop(low, high, one, 0)


def start_copy(copy):
    copy.start()


def wait_send(copy):
    copy.wait_send()


def wait_recv(copy):
    copy.wait_recv()


def load_experts(own, across, weights, sems, local, other):
    near = [pltpu.make_async_copy(own, weights.at[0], local.at[0])]
    far = [remote(own, weights.at[2], sems, 0, other)]
    for which, ref in enumerate(across):
        near.append(pltpu.make_async_copy(ref, weights.at[1, which], local.at[1 + which]))
        far.append(remote(ref, weights.at[3, which], sems, 1 + which, other))
    return near, far


GELU_SCALE = math.sqrt(2 / math.pi)


def gelu_tanh(value):
    return jnp.tanh(GELU_SCALE * (value + 0.044715 * (value * value * value)))


def halves(rows, half):
    count = MAIN // 2
    tail = (TOTAL - MAIN) // 2
    return jnp.concatenate(
        [
            rows[half * count : (half + 1) * count, :],
            rows[MAIN + half * tail : MAIN + (half + 1) * tail, :],
        ]
    )


HALF = TOTAL // 2


def experts_kernel(
    staged, hidden, target_row, target_column, gates, after, vec, own, across_in, across_part,
    rows, rows_y, chosen, total, pool, across_out,
    weights, sends, lands, backs, returns, act, result, gathered,
    forth_send, forth_recv, back_send, back_recv, weight_send, weight_recv, row_send, row_recv, local,
):
    at = place()
    me = lax.axis_index("exp")
    other, across_y_peer = meet_experts(at)
    row_copies = []
    near, far = load_experts(own, (across_in,), weights, (weight_send, weight_recv), local, other)
    late = pl.ds(EARLY, D - EARLY)
    trade = remote(own.at[1, late], weights.at[1, 1, late], (weight_send, weight_recv), 2, across_y_peer)
    pass_on = remote(weights.at[1, 1], weights.at[3, 1], (weight_send, weight_recv), 3, other)
    save = pltpu.make_async_copy(weights.at[1, 1], across_out, local.at[3])
    near.append(pltpu.make_async_copy(across_part, weights.at[1, 1, pl.ds(0, EARLY)], local.at[4]))
    for copy in near:
        copy.start()
    count = hidden.shape[0]
    slot = iota((TOTAL, count), 0)
    placing = ((slot == target_row[0:1, :]) | (slot == target_row[1:2, :])).astype(jnp.bfloat16)
    placed = plain_dot(placing, hidden[...])
    pack(sends, placed[:MAIN], placed[MAIN:])
    met_experts()
    deal(sends, lands, (forth_send, forth_recv), True, 1, GROUP, start_copy)
    for copy in [*far, trade]:
        copy.start()
    keep = pltpu.make_async_copy(sends.at[me], lands.at[0], local.at[2])
    keep.start()
    keep.wait()
    deal(sends, lands, (forth_send, forth_recv), True, 1, GROUP // 2, wait_recv)
    for copy in near:
        copy.wait()
    for half in range(2):
        if half == 1:
            deal(sends, lands, (forth_send, forth_recv), True, GROUP // 2, GROUP, wait_recv)
        sources = pl.ds(half * (GROUP // 2), GROUP // 2)
        first, first_tail = half * (MAIN // 2), MAIN + half * (TOTAL - MAIN) // 2
        unpack(lands.at[sources], rows, first, first_tail)
        for piece, (start, size) in enumerate(((first, MAIN // 2), (first_tail, (TOTAL - MAIN) // 2))):
            view = pl.ds(start, size)
            copy = remote(rows.at[view], rows_y.at[view], (row_send, row_recv), half * 2 + piece, across_y_peer)
            copy.start()
            row_copies.append(copy)
        if half == 0:
            for copy in far:
                copy.wait_recv()
        given = halves(rows, half)
        lines = pl.ds(half * HALF, HALF)

        def hidden_units(index, carry):
            quarter, part = lax.div(index, 3), lax.rem(index, 3)
            columns = pl.ds(pl.multiple_of(part * 256, 256), 256)
            value = plain_dot(given, weights[quarter, 0, :, columns])
            act[quarter, lines, columns] = (0.5 * value * (1.0 + gelu_tanh(value))).astype(jnp.bfloat16)
            return carry

        lax.fori_loop(0, 12, hidden_units, 0)
    trade.wait_recv()
    pass_on.start()
    save.start()
    pass_on.wait_recv()
    for half in range(2):
        sources = pl.ds(half * (GROUP // 2), GROUP // 2)
        lines = pl.ds(half * HALF, HALF)

        def outputs(index, carry):
            columns = pl.ds(pl.multiple_of(index * 256, 256), 256)
            value = over_last(act[0, lines, :], weights[0, 1, columns, :])
            for quarter in range(1, 4):
                value = value + over_last(act[quarter, lines, :], weights[quarter, 1, columns, :])
            result[:, columns] = value
            return carry

        lax.fori_loop(0, 3, outputs, 0)
        pack(backs.at[sources], result[: MAIN // 2, :], result[MAIN // 2 :, :])
        low, high = max(1, half * (GROUP // 2)), (half + 1) * (GROUP // 2)
        deal(backs, returns, (back_send, back_recv), False, low, high, start_copy)
    keep = pltpu.make_async_copy(backs.at[0], returns.at[me], local.at[2])
    keep.start()
    keep.wait()
    deal(backs, returns, (back_send, back_recv), False, 1, GROUP, wait_recv)
    unpack(returns, gathered, 0, MAIN)
    slot = iota((count, TOTAL), 1)
    for k in range(2):
        placing = (slot == target_column[:, k : k + 1]).astype(jnp.bfloat16)
        chosen[k] = plain_dot(placing, gathered[...]).astype(jnp.bfloat16)
    staged.give(0, 2)
    staged.need(4)

    def final_norm(index, carry):
        part = pl.ds(pl.multiple_of(index * CHUNK, CHUNK), CHUNK)
        value = after[part, :] + (
            gates[part, 0:1] * chosen[0, part, :].astype(jnp.float32)
            + gates[part, 1:2] * chosen[1, part, :].astype(jnp.float32)
        )
        total[part, :] = value
        normed, _ = centre(value)
        return carry + jnp.sum(normed * vec[8:9, :] + vec[9:10, :], axis=0, keepdims=True)

    summed = lax.fori_loop(0, count // CHUNK, final_norm, jnp.zeros((1, D), jnp.float32)) / PATCHES
    staged.give(3)
    pool[...] = jnp.zeros_like(pool)
    for tile in range(D // LANES):
        pool[tile : tile + 1, :] = summed[:, tile * LANES : (tile + 1) * LANES]
    deal(sends, lands, (forth_send, forth_recv), True, 1, GROUP, wait_send)
    deal(backs, returns, (back_send, back_recv), False, 1, GROUP, wait_send)
    for copy in [*far, trade, pass_on]:
        copy.wait_send()
    save.wait()
    for copy in row_copies:
        copy.wait()
    staged.give(1)


def experts_forward(*operands):
    count = operands[0].shape[0]
    low, wide = jnp.bfloat16, jnp.float32
    wire = pltpu.VMEM((GROUP, SLOTS, WIRE), low)
    sems = pltpu.SemaphoreType.DMA
    return staged_call(
        experts_kernel,
        operands,
        [((TOTAL, D), low), ((TOTAL, D), low), ((2, count, D), low), ((count, D), wide), ((PAD, LANES), wide), ((D, D), low)],
        [pltpu.VMEM((4, 2, D, D), low)]
        + [wire] * 4
        + [pltpu.VMEM((4, TOTAL, D), low), pltpu.VMEM((HALF, D), wide), pltpu.VMEM((TOTAL, D), low)]
        + [sems((GROUP,))] * 4
        + [sems((4,))] * 4
        + [sems((5,))],
        (4,),
        (0, 1, 2, 3),
        raw=(6, 7, 8),
        raw_out=(5,),
        collective_id=5,
        megabytes=28,
        name="experts_forward",
    )


def tile_of(index):
    half, part = lax.div(index, 3), lax.rem(index, 3)
    columns = pl.ds(pl.multiple_of(part * 256, 256), 256)
    return pl.ds(pl.multiple_of(half * HALF, HALF), HALF), columns


def gelu_both(value):
    tanh = gelu_tanh(value)
    grown = (0.5 * value * (1.0 + tanh)).astype(jnp.bfloat16)
    return grown, 0.5 * (1.0 + tanh) + 0.5 * value * (1.0 - tanh * tanh) * (
        GELU_SCALE * (1.0 + 3 * 0.044715 * (value * value))
    )


def quarter_grads(kept, rows_t, drows_t, dpre, act, first):
    def step(index, carry):
        columns = pl.ds(pl.multiple_of(index * 256, 256), 256)
        for which, (left, right) in enumerate(((rows_t, dpre), (drows_t, act))):
            value = plain_dot(left[...], right[:, columns])
            kept[which, :, columns] = value if first else kept[which, :, columns] + value
        return carry

    lax.fori_loop(0, 3, step, 0)


def quarter_set(kept, weights, rows, drows, act, dpre, rows_t, drows_t):
    def step(index, carry):
        lines, columns = tile_of(index)
        grown, rate = gelu_both(plain_dot(rows[lines, :], weights[0, :, columns]))
        act[lines, columns] = grown
        value = plain_dot(drows[lines, :], weights[1, :, columns])
        dpre[lines, columns] = (value * rate).astype(jnp.bfloat16)
        return carry

    lax.fori_loop(0, 6, step, 0)
    rows_t[...] = rows[...].T
    drows_t[...] = drows[...].T
    quarter_grads(kept, rows_t, drows_t, dpre, act, False)


def experts_back_kernel(
    staged, row_grad, total, chosen, gates, gate_probs, ids, rows, rows_y, target_row, target_column, vec, own, across_in, across_out,
    dtotal, dgate, sums, dhidden, kept, rows_last, drows_y, drows_last,
    weights, sends, lands, backs, returns, slope, dpre, act_own, act_set, dpre_set, rows_far, drows, drows_far, result, dreturned,
    rows_t, drows_t, outward,
    forth_send, forth_recv, back_send, back_recv, weight_send, weight_recv, set_send, set_recv, local,
):
    at = place()
    me = lax.axis_index("exp")
    other, across_y_peer = meet_experts(at)
    near, far = load_experts(own, (across_in, across_out), weights, (weight_send, weight_recv), local, other)
    for copy in near:
        copy.start()
    count = total.shape[0]
    grad = jnp.concatenate([row_grad[tile : tile + 1, :] for tile in range(D // LANES)], axis=1) / PATCHES
    zero = jnp.zeros((1, D), jnp.float32)
    staged.need(1, 2, 5)

    def final_norm(index, carry):
        part = pl.ds(pl.multiple_of(index * CHUNK, CHUNK), CHUNK)
        back, gain, shift = norm_back(total[part, :], jnp.broadcast_to(grad, (CHUNK, D)), vec[8:9, :])
        dtotal[part, :] = back
        dgates = [
            jnp.sum(back * chosen[k, part, :].astype(jnp.float32), axis=-1, keepdims=True) for k in range(2)
        ]
        for k in range(2):
            outward[k, part, :] = (gates[part, k : k + 1] * back).astype(jnp.bfloat16)
        lane = iota((CHUNK, LANES), 1) - ROUTER_AT
        probs = gate_probs[part, :]
        dprobs = jnp.where(lane == ids[part, 0:1], dgates[0], 0.0) + jnp.where(
            lane == ids[part, 1:2], dgates[1], 0.0
        )
        inner = dprobs - jnp.sum(probs * dprobs, axis=-1, keepdims=True)
        dgate[part, :] = (probs * inner).astype(jnp.bfloat16)
        return carry[0] + gain, carry[1] + shift

    gain, shift = lax.fori_loop(0, count // CHUNK, final_norm, (zero, zero))
    sums[...] = jnp.concatenate([gain, shift, jnp.zeros((PAD - 2, D), jnp.float32)])
    staged.give(0)
    slot = iota((TOTAL, count), 0)
    placed = [
        plain_dot((slot == target_row[k : k + 1, :]).astype(jnp.bfloat16), outward[k]) for k in range(2)
    ]
    placed = placed[0] + placed[1]
    pack(sends, placed[:MAIN], placed[MAIN:])
    met_experts()
    deal(sends, lands, (forth_send, forth_recv), True, 1, GROUP, start_copy)
    staged.need(6, 7)
    set_sems = (set_send, set_recv)
    moves = [remote(rows, rows_far, set_sems, 0, other), remote(rows_y, rows_last, set_sems, 1, other)]
    for copy in far + moves:
        copy.start()
    keep = pltpu.make_async_copy(sends.at[me], lands.at[0], local.at[3])
    keep.start()
    keep.wait()
    for copy in near:
        copy.wait()

    def hidden_units(index, carry):
        quarter = lax.div(index, 6)
        lines, columns = tile_of(lax.rem(index, 6))
        grown, rate = gelu_both(plain_dot(rows[lines, :], weights[quarter, 0, :, columns]))

        @pl.when(quarter == 0)
        def _():
            act_own[lines, columns] = grown

        slope[quarter, lines, columns] = rate
        return carry

    lax.fori_loop(0, 12, hidden_units, 0)
    for copy in far:
        copy.wait_recv()
    lax.fori_loop(12, 24, hidden_units, 0)
    deal(sends, lands, (forth_send, forth_recv), True, 1, GROUP, wait_recv)
    unpack(lands, drows, 0, MAIN)
    moves.append(remote(drows, drows_y, set_sems, 2, across_y_peer))
    moves.append(remote(drows, drows_far, set_sems, 3, other))
    for copy in moves[2:]:
        copy.start()

    def hidden_back(index, carry):
        quarter = lax.div(index, 6)
        lines, columns = tile_of(lax.rem(index, 6))
        value = plain_dot(drows[lines, :], weights[quarter, 1, :, columns])
        dpre[quarter, lines, columns] = (value * slope[quarter, lines, columns]).astype(jnp.bfloat16)
        return carry

    lax.fori_loop(0, 24, hidden_back, 0)

    def inputs_back(index, carry):
        lines, columns = tile_of(index)
        value = over_last(dpre[0, lines, :], weights[0, 0, columns, :])
        for quarter in range(1, 4):
            value = value + over_last(dpre[quarter, lines, :], weights[quarter, 0, columns, :])
        result[lines, columns] = value
        return carry

    lax.fori_loop(0, 6, inputs_back, 0)
    pack(backs, result[:MAIN, :], result[MAIN:, :])
    deal(backs, returns, (back_send, back_recv), False, 1, GROUP, start_copy)
    keep = pltpu.make_async_copy(backs.at[0], returns.at[me], local.at[3])
    keep.start()

    rows_t[...] = rows[...].T
    drows_t[...] = drows[...].T
    quarter_grads(kept, rows_t, drows_t, dpre.at[0], act_own, True)
    for copy in (moves[0], moves[3]):
        copy.wait_recv()
    quarter_set(kept, weights.at[0], rows_far, drows_far, act_set, dpre_set, rows_t, drows_t)
    staged.give(4)
    moves[2].wait_recv()
    moves.append(remote(drows_y, drows_last, set_sems, 4, other))
    moves[4].start()
    keep.wait()
    deal(backs, returns, (back_send, back_recv), False, 1, GROUP, wait_recv)
    unpack(returns, dreturned, 0, MAIN)
    slot = iota((count, TOTAL), 1)
    placing = (slot == target_column[:, 0:1]) | (slot == target_column[:, 1:2])
    dhidden[...] = plain_dot(placing.astype(jnp.bfloat16), dreturned[...])
    staged.give(3)
    moves[1].wait_recv()
    moves[4].wait_recv()
    staged.give(5, 6, 7)
    deal(sends, lands, (forth_send, forth_recv), True, 1, GROUP, wait_send)
    deal(backs, returns, (back_send, back_recv), False, 1, GROUP, wait_send)
    for copy in far + moves:
        copy.wait_send()


def experts_backward(*operands):
    count = operands[1].shape[0]
    low, wide = jnp.bfloat16, jnp.float32
    wire = pltpu.VMEM((GROUP, SLOTS, WIRE), low)
    shapes = [
        ((count, D), wide), ((count, LANES), low), ((PAD, D), wide),
        ((count, D), wide), ((2, D, D), wide), ((TOTAL, D), low), ((TOTAL, D), low), ((TOTAL, D), low),
    ]
    sems = pltpu.SemaphoreType.DMA
    return staged_call(
        experts_back_kernel,
        operands,
        shapes,
        [pltpu.VMEM((4, 2, D, D), low)]
        + [wire] * 4
        + [pltpu.VMEM((4, TOTAL, D), wide), pltpu.VMEM((4, TOTAL, D), low)]
        + [pltpu.VMEM((TOTAL, D), low)] * 6
        + [pltpu.VMEM((TOTAL, D), wide), pltpu.VMEM((TOTAL, D), low)]
        + [pltpu.VMEM((D, TOTAL), low)] * 2
        + [pltpu.VMEM((2, count, D), low)]
        + [sems((GROUP,))] * 4
        + [sems((3,))] * 2
        + [sems((5,))] * 2
        + [sems((4,))],
        (1, 2, 5, 6, 7),
        (0, 3, 4, 5, 6, 7),
        raw=(11, 12, 13),
        collective_id=8,
        megabytes=57,
        name="experts_backward",
    )


def plane_peer(at, by):
    return moved(moved(at, "x", by[0]), "z", by[1])


def greet_all(at):
    barrier = pltpu.get_barrier_semaphore()
    peers = [near_peer(at, by) for by in NEAR] + [plane_peer(at, by) for by in PLANE]
    for peer in peers:
        pl.semaphore_signal(barrier, inc=1, device_id=device(peer), device_id_type=MESH)
    pl.semaphore_wait(barrier, len(peers))


def send_near(at, source, target, sems, first):
    copies = []
    for index, by in enumerate(NEAR):
        peer = near_peer(at, by)
        copies.append(remote(source(peer), target.at[at["y"], at["core"]], sems, first + index, peer))
        copies[-1].start()
    return copies


def head_kernel(
    staged, pool, head, labels, count,
    row_grad, head_grad, loss,
    near, every, pooled, pulls, got, summed, last, low, send, recv,
):
    at = place()
    sems = (send, recv)
    greet_all(at)
    copies = send_near(at, lambda peer: pool, near, sems, 0)
    near[at["y"], at["core"]] = pool[...]
    classes = head.shape[0]
    staged.need(1)
    spare = classes - classes % 16
    low[spare:, :] = jnp.zeros((low.shape[0] - spare, D), jnp.bfloat16)
    low[:classes, :] = head[...].astype(jnp.bfloat16)
    images = pooled.shape[0]
    number = (lax.axis_index("rep") * GROUP + lax.axis_index("exp")) * classes
    column = iota((images, low.shape[0]), 1)
    inside = column < classes
    column = jnp.where(inside, column + number, -2)
    hit = labels[:, 0:1] == column
    for slot in range(1, labels.shape[1]):
        hit = hit | (labels[:, slot : slot + 1] == column)
    targets = hit.astype(jnp.float32)
    valid = (jnp.max(labels[...], axis=1, keepdims=True) >= 0).astype(jnp.float32)
    for copy in copies:
        copy.wait()
    rows = near[:, 0] + near[:, 1]
    mine = every.at[:, at["x"], :, at["z"]]
    mine[...] = rows.astype(jnp.bfloat16).astype(jnp.float32).reshape(2, 2, PAD, LANES)
    copies = []
    for index, by in enumerate(PLANE):
        copies.append(remote(mine, mine, sems, 7 + index, plane_peer(at, by)))
        copies[-1].start()
    for copy in copies:
        copy.wait()
    for tile in range(D // LANES):
        lanes = slice(tile * LANES, (tile + 1) * LANES)
        pooled[:, lanes] = every[:, :, :, :, tile, :].reshape(images, LANES).astype(jnp.bfloat16)
    logits = over_last(pooled[...], low[...])
    soft = jnp.maximum(logits, 0.0) + jnp.log1p(jnp.exp(-jnp.abs(logits)))
    terms = jnp.where(inside, valid * (soft - targets * logits), 0.0)
    loss[...] = jnp.sum(jnp.sum(terms, axis=1, keepdims=True), axis=0, keepdims=True)
    sigmoid = 1.0 / (1.0 + jnp.exp(-logits))
    down = jnp.where(inside, valid * (sigmoid - targets) / count[...], 0.0)
    back = plain_dot(down.astype(jnp.bfloat16), low[...])
    pulls[...] = jnp.zeros_like(pulls)
    for tile in range(D // LANES):
        lanes = slice(tile * LANES, (tile + 1) * LANES)
        pulls[:, :, :, :, tile, :] = back[:, lanes].reshape(2, 4, 2, 4, LANES)
    copies = []
    for index, by in enumerate(PLANE):
        peer = plane_peer(at, by)
        source = pulls.at[:, peer["x"], :, peer["z"]]
        copies.append(remote(source, got.at[at["x"], at["z"]], sems, 22 + index, peer))
        copies[-1].start()
    got[at["x"], at["z"]] = pulls[:, at["x"], :, at["z"]]
    head_grad[...] = plain_dot(down.T.astype(jnp.bfloat16), pooled[...])
    for copy in copies:
        copy.wait()
    summed[...] = jnp.sum(got[...].reshape((16,) + summed.shape), axis=0)
    copies = send_near(at, lambda peer: summed.at[peer["y"]], last, sems, 37)
    last[at["y"], at["core"]] = summed[at["y"]]
    for copy in copies:
        copy.wait()
    row_grad[...] = jnp.sum(last[...].reshape((8,) + row_grad.shape), axis=0)


def head_step(pool, head, labels, count):
    images = labels.shape[0]
    classes = -(-head.shape[0] // LANES) * LANES
    wide = jnp.float32
    block = (PAD, LANES)
    sems = pltpu.SemaphoreType.DMA
    return staged_call(
        head_kernel,
        (pool, head, labels, count),
        [(block, wide), ((classes, D), wide), ((1, 1), wide)],
        [
            pltpu.VMEM((4, 2) + block, wide),
            pltpu.VMEM((2, 4, 2, 4) + block, wide),
            pltpu.VMEM((images, D), jnp.bfloat16),
            pltpu.VMEM((2, 4, 2, 4) + block, wide),
            pltpu.VMEM((4, 4, 2, 2) + block, wide),
            pltpu.VMEM((4,) + block, wide),
            pltpu.VMEM((4, 2) + block, wide),
            pltpu.VMEM((classes, D), jnp.bfloat16),
            sems((44,)),
            sems((44,)),
        ],
        (1,),
        (),
        collective_id=2,
        megabytes=16,
        name="head_step",
    )


def follow(old, square):
    return DECAY * old + (1.0 - DECAY) * (square + EPS_SQ)


def update_kernel(
    part_one, part_two, part_three, totals, head_grad, table_grad, table_squared, expert_cols_squared, expert_grad,
    squares, router, table, head, vectors, experts,
    square_rows, square_cols, router_rows, router_cols, table_rows, table_cols, head_rows, head_cols,
    expert_rows, expert_cols, moment,
    loss, norm, square_clip, square_rows_next, square_cols_next, square_next,
    router_clip, router_rows_next, router_cols_next, router_next,
    table_clip, table_rows_next, table_cols_next, table_next,
    head_clip, head_rows_next, head_cols_next, head_next,
    expert_clip, expert_rows_next, expert_cols_next, expert_next,
    vector_clip, moment_next, vector_next,
    turned, scale_ref, column_ref, line_ref,
):
    step = pl.program_id(0)

    def stand(line):
        count = line.shape[1]
        column_ref[...] = jnp.zeros_like(column_ref)
        column_ref[0:1, :count] = line
        return column_ref[...].T[:count, 0:1]

    def lie(column):
        count = column.shape[0]
        line_ref[...] = jnp.zeros_like(line_ref)
        line_ref[:count, :] = jnp.broadcast_to(column, (count, LANES))
        return line_ref[...].T[0:1, :count]

    expert_rates = (0.3 / math.sqrt(D), 4.8 / math.sqrt(FF))

    def total(value):
        return jnp.sum(jnp.sum(value, axis=1, keepdims=True), axis=0, keepdims=True)

    @pl.when(step == 0)
    def _():
        size = jnp.sqrt(total(totals[:7, :]) + totals[7:8, 1:2])
        clip = jnp.minimum(1.0, CLIP_NORM / size)
        clip_sq = clip * clip
        loss[...] = totals[7:8, 0:1]
        norm[...] = size
        scale_ref[...] = jnp.broadcast_to(clip, scale_ref.shape)
        rows = squares.shape[1]
        parts = (part_one, part_two, part_three)
        for k in range(5):
            grad = parts[k // 2][PAD * (k % 2) : PAD * (k % 2) + rows, :]
            near = follow(stand(square_rows[k : k + 1, :]), clip_sq * jnp.mean(grad * grad, axis=1, keepdims=True))
            far = follow(square_cols[k : k + 1, :], clip_sq * totals[k : k + 1, :] / D)
            middle = jnp.mean(totals[k : k + 1, :], axis=1, keepdims=True)
            middle = follow(totals[7:8, 2 + k : 3 + k] / D, clip_sq * middle / D)
            square_rows_next[k : k + 1, :] = lie(near)
            square_cols_next[k : k + 1, :] = far
            square_clip[k] = clip * grad
            rate = (4.0 if k == 4 else 1.0) * (0.3 / math.sqrt(D))
            square_next[k] = squares[k] - rate * (clip * grad) * lax.rsqrt(near * far / middle)
        tail = part_three[PAD : PAD + rows, EXTRA:]
        grad = tail[:, 32:64]
        near = follow(stand(router_rows[...][None]), clip_sq * jnp.mean(grad * grad, axis=1, keepdims=True))
        squared = totals[6:7, EXTRA + 32 : EXTRA + 64]
        far = follow(router_cols[...][None], clip_sq * squared / D)
        middle = jnp.sum(squared, axis=1, keepdims=True) / GROUP
        middle = follow(totals[7:8, 7:8] / D, clip_sq * middle / D)
        router_rows_next[...] = lie(near)[0]
        router_cols_next[...] = far[0]
        router_clip[...] = clip * grad
        router_next[...] = router[...] - (0.2 / math.sqrt(D)) * (clip * grad) * lax.rsqrt(near * far / middle)
        grad = table_grad[...]
        near = follow(table_rows[...][None], clip_sq * table_squared[...] / D)
        far = follow(stand(table_cols[...][None]), clip_sq * jnp.mean(grad * grad, axis=1, keepdims=True))
        middle = jnp.mean(near, axis=1, keepdims=True)
        table_rows_next[...] = near[0]
        table_cols_next[...] = lie(far)[0]
        table_clip[...] = clip * grad
        table_next[...] = table[...] - 0.15 * (clip * grad) * lax.rsqrt(near * far / middle)
        classes = head.shape[0]
        grad = head_grad[:classes, :]
        near = follow(head_rows[...][None], clip_sq * totals[5:6, :] / (classes * 4 * GROUP))
        far = follow(stand(head_cols[...][None]), clip_sq * jnp.mean(grad * grad, axis=1, keepdims=True))
        middle = jnp.mean(near, axis=1, keepdims=True)
        head_rows_next[...] = near[0]
        head_cols_next[...] = lie(far)[0]
        head_clip[...] = clip * grad
        head_next[...] = head[...] - (0.5 / math.sqrt(D)) * (clip * grad) * lax.rsqrt(near * far / middle)
        grad = clip * tail[:, 96:106]
        state = follow(moment[...], grad * grad)
        vector_clip[...] = grad
        moment_next[...] = state
        vector_next[...] = vectors[...] - 0.3 * grad * lax.rsqrt(state)
        near = follow(expert_rows[...], clip_sq * totals[PAD : PAD + 2, :] / FF)
        far = follow(expert_cols[...], clip_sq * expert_cols_squared[...] / D)
        middle = jnp.mean(near, axis=1, keepdims=True)
        expert_rows_next[...] = near
        expert_cols_next[...] = far
        for which in range(2):
            ratio = near[which : which + 1, :] / middle[which : which + 1, :]
            turned[which] = jnp.broadcast_to(ratio, (LANES, D)).T

    lines = expert_grad.shape[1]
    steps = D // lines
    which = lax.div(step, steps)
    column = turned[which, pl.ds(pl.multiple_of(lax.rem(step, steps) * lines, lines), lines), 0:1]
    row = expert_cols_next[pl.ds(which, 1), :]
    clipped = scale_ref[0:1, 0:1] * expert_grad[0]
    rate = jnp.where(which == 0, expert_rates[0], expert_rates[1])
    expert_clip[0] = clipped
    expert_next[0] = experts[0] - rate * clipped * lax.rsqrt(column * row)


def update_all(*operands):
    lines = 384
    wide = jnp.float32
    squares, router, table, head, vectors = (operands[index].shape for index in range(9, 14))
    rows = squares[1]
    expert = operands[14].shape
    shapes = [
        (1, 1), (1, 1), squares, (5, rows), (5, D), squares, router, (rows,), (GROUP,), router,
        table, (PATCHES,), (rows,), table, head, (D,), (head[0],), head,
        expert, (2, D), (2, D), expert, vectors, vectors, vectors,
    ]

    def spec(shape, streamed):
        if streamed:
            return pl.BlockSpec((1, lines, D), lambda step: (step // (D // lines), step % (D // lines), 0))
        return pl.BlockSpec(shape, lambda step: (0,) * len(shape))

    return pl.pallas_call(
        update_kernel,
        grid=(2 * D // lines,),
        out_shape=[jax.ShapeDtypeStruct(shape, wide) for shape in shapes],
        in_specs=[spec(value.shape, index in (8, 14)) for index, value in enumerate(operands)],
        out_specs=[spec(shape, index in (18, 21)) for index, shape in enumerate(shapes)],
        scratch_shapes=[pltpu.VMEM((2, D, LANES), wide), pltpu.VMEM((PAD, LANES), wide)]
        + [pltpu.VMEM((LANES, 2 * LANES), wide), pltpu.VMEM((2 * LANES, LANES), wide)],
        compiler_params=pltpu.CompilerParams(vmem_limit_bytes=32 * 2**20),
        name="update_all",
    )(*(pin(value) for value in operands))


def across_cores(value):
    return lax.ppermute(value, "rep", CORE_SWAP)


def across_y(value):
    return lax.ppermute(value, "rep", Y_SWAP)


def shards(
    patches,
    expert_ids,
    labels,
    label_count,
    square_weights,
    router_weight,
    position_table,
    head_weight,
    expert_weights,
    vector_params,
    square_rows,
    square_cols,
    router_rows,
    router_cols,
    position_rows,
    position_cols,
    head_rows,
    head_cols,
    expert_rows,
    expert_cols,
    vector_moment,
):
    bfloat = jnp.bfloat16
    num_rep = lax.axis_size("rep")
    num_exp = lax.axis_size("exp")
    rep_index = lax.axis_index("rep")
    my_image = lax.axis_index("exp")
    device_index = lax.axis_index(("rep", "exp"))
    micro, core = rep_index // 2, rep_index % 2
    num_expert = router_weight.shape[1]
    vocab_dev = head_weight.shape[1]
    ff_dev = expert_weights.shape[3]
    block = patches.shape[2]
    rows, width = 2 * block, patches.shape[3]
    num_top = expert_ids.shape[3]
    heads = width // HEAD
    scale = HEAD ** (-0.5)
    own_rows = square_weights.shape[1]

    gap = jnp.zeros((own_rows, 6), jnp.float32)
    extra = jnp.concatenate(
        [position_table.T, router_weight, vector_params.T, gap, vector_params.T], axis=1
    )
    extra = jnp.pad(extra, ((0, 0), (0, width - extra.shape[1])))
    valid = (label_count > 0).astype(jnp.float32)
    image_count = jnp.sum(valid)
    live = jnp.arange(labels.shape[2], dtype=jnp.int32) < label_count[:, :, None]
    live_labels = jnp.where(live, labels, -1).reshape(2 * num_exp, -1)

    counted = image_count.reshape(1, 1)
    extra, live_labels, counted = lax.optimization_barrier((extra, live_labels, counted))

    wide_ids = jnp.pad(expert_ids.reshape(2, block, num_top), ((0, 0), (0, 0), (0, LANES - num_top)))
    *squares, extra, low, patch_rows, ids, quarter, quarter_in, across_part = gather_all(
        square_weights, extra, patches.reshape(2, block, width), wide_ids, expert_weights[0]
    )
    patch_rows, ids = patch_rows.reshape(rows, width), ids.reshape(rows, LANES)

    across_in = across_y(quarter_in)
    (
        embed, hidden_one, query, keys, values, mixed, after_attn, hidden_two,
        gate_probs, gates, lse, vectors, router, target, target_t, hidden_kept, *squares,
    ) = attend(patch_rows, squares, extra, low, ids)
    across_in, hidden_two = lax.optimization_barrier((across_in, hidden_two))
    received, received_y, chosen, after_moe, pool, across_out = experts_forward(
        hidden_two, target_t, target, gates, after_attn, vectors, quarter, across_in, across_part
    )
    row_grad, head_g, loss_part = head_step(
        pool, head_weight.T, live_labels, counted
    )
    dmoe_in, dgate_logits, final_sums, dhidden, part_g, received_last, down_y, down_last = experts_backward(
        row_grad, after_moe, chosen, gates, gate_probs, ids, received, received_y,
        target_t, target, vectors, quarter, across_in, across_out,
    )
    dafter_low, dquery_low, dkey_low, dvalue_low, dembed_low, sums = attend_back(
        dmoe_in,
        dhidden,
        dgate_logits,
        embed,
        after_attn,
        query,
        keys,
        values,
        lse,
        *squares,
        vectors,
        router,
    )
    *owned, totals, expert_g, expert_colsq = shared_gradients(
        patch_rows, hidden_one, mixed, dembed_low, dquery_low, dkey_low, dvalue_low, dafter_low,
        hidden_kept, dgate_logits, sums, final_sums, head_g, loss_part, square_rows, router_rows[None],
        part_g, quarter, received_y, received_last, down_y, down_last,
    )
    second = 3 * LANES

    def positions(value):
        return jnp.concatenate(
            [value[:, start : start + block] for start in (0, second, block, second + block)], axis=1
        )

    (
        loss_total, grad_norm, square_clip, square_rows_next, square_cols_next, square_next,
        router_clip, router_rows_next, router_cols_next, router_next,
        table_clip, table_rows_next, table_cols_next, table_next,
        head_clip, head_rows_next, head_cols_next, head_next,
        expert_clip, expert_rows_next, expert_cols_next, expert_next,
        vector_clip, moment_next, vector_next,
    ) = update_all(
        *owned, totals, head_g, positions(owned[2][PAD : PAD + own_rows]), positions(totals[6:7]),
        expert_colsq, expert_g,
        square_weights, router_weight, position_table.T, head_weight.T, vector_params.T, expert_weights[0],
        square_rows, square_cols, router_rows, router_cols, position_rows,
        position_cols, head_rows, head_cols, expert_rows[0], expert_cols[0],
        vector_moment.T,
    )
    return (
        loss_total[0, 0],
        image_count,
        grad_norm[0, 0],
        square_clip,
        square_rows_next,
        square_cols_next,
        square_next,
        router_clip,
        router_rows_next,
        router_cols_next,
        router_next,
        table_clip.T,
        table_rows_next,
        table_cols_next,
        table_next.T,
        head_clip.T,
        head_rows_next,
        head_cols_next,
        head_next.T,
        expert_clip[None],
        expert_rows_next[None],
        expert_cols_next[None],
        expert_next[None],
        vector_clip.T,
        moment_next.T,
        vector_next.T,
    )


def solution(mesh):
    in_specs = (
        P(None, "exp", "rep", None),
        P(None, "exp", "rep", None),
        P(),
        P(),
        P(None, ("rep", "exp"), None),
        P(("rep", "exp"), None),
        P(None, ("rep", "exp")),
        P(None, ("rep", "exp")),
        P("exp", None, None, "rep"),
        P(None, ("rep", "exp")),
        P(None, ("rep", "exp")),
        P(),
        P(("rep", "exp")),
        P(),
        P(),
        P(("rep", "exp")),
        P(),
        P(("rep", "exp")),
        P("exp", None, None),
        P("exp", None, "rep"),
        P(None, ("rep", "exp")),
    )
    out_specs = (
        P(),
        P(),
        P(),
        P(None, ("rep", "exp"), None),
        P(None, ("rep", "exp")),
        P(),
        P(None, ("rep", "exp"), None),
        P(("rep", "exp"), None),
        P(("rep", "exp")),
        P(),
        P(("rep", "exp"), None),
        P(None, ("rep", "exp")),
        P(),
        P(("rep", "exp")),
        P(None, ("rep", "exp")),
        P(None, ("rep", "exp")),
        P(),
        P(("rep", "exp")),
        P(None, ("rep", "exp")),
        P("exp", None, None, "rep"),
        P("exp", None, None),
        P("exp", None, "rep"),
        P("exp", None, None, "rep"),
        P(None, ("rep", "exp")),
        P(None, ("rep", "exp")),
        P(None, ("rep", "exp")),
    )
    return jax.shard_map(shards, mesh=mesh, in_specs=in_specs, out_specs=out_specs, check_vma=False)
```
